32 devices in a mesh: dp: 8 (over z, core), tensor: 4 (over y, x).
Axes of the slice: x: 2, y: 2, z: 4, core: 2. Of those that a mesh axis runs over, the one named last changes fastest.
Arguments:
- tokens: bfloat16 [8192, 2048], P('dp'), may hold values from -6 to 6
- lengths: int32 [8], P('dp'), may hold values from 256 to 1024, as said below
- in_gain: float32 [2048], replicated, may hold values from 0.5 to 1.5
- w_query: bfloat16 [2048, 2048], P(None, 'tensor'), may hold values from -0.125 to 0.125
- w_key: bfloat16 [2048, 1024], P(None, 'tensor'), may hold values from -0.125 to 0.125
- w_value: bfloat16 [2048, 1024], P(None, 'tensor'), may hold values from -0.125 to 0.125
- query_gain: float32 [128], replicated, may hold values from 1 to 2
- key_gain: float32 [128], replicated, may hold values from 1 to 2
- w_out: bfloat16 [2048, 2048], P('tensor'), may hold values from -0.75 to 0.75
- post_gain: float32 [2048], replicated, may hold values from 0.5 to 1.5
- w_gate: bfloat16 [2048, 6144], P(None, 'tensor'), may hold values from -0.125 to 0.125
- w_up: bfloat16 [2048, 6144], P(None, 'tensor'), may hold values from -0.125 to 0.125
- w_down: bfloat16 [6144, 2048], P('tensor'), may hold values from -0.109375 to 0.109375
- out_grad: bfloat16 [8192, 2048], P('dp'), may hold values from -6 to 6
Outputs:
- output: bfloat16 [8192, 2048], P('dp')
- in_grad: bfloat16 [8192, 2048], P('dp')
- grad_in_gain: float32 [2048], replicated
- grad_query: float32 [2048, 2048], P('dp', 'tensor')
- grad_key: float32 [2048, 1024], P('dp', 'tensor')
- grad_value: float32 [2048, 1024], P('dp', 'tensor')
- grad_query_gain: float32 [128], replicated
- grad_key_gain: float32 [128], replicated
- grad_out: float32 [2048, 2048], P('tensor', 'dp')
- grad_post_gain: float32 [2048], replicated
- grad_gate: float32 [2048, 6144], P('dp', 'tensor')
- grad_up: float32 [2048, 6144], P('dp', 'tensor')
- grad_down: float32 [6144, 2048], P('tensor', 'dp')
The draws below stay inside these ranges and needn't reach their ends.
Inputs may be any that keep to these rules, and one draw needn't show every extreme that they name: `lengths`: valid tokens of each slot of 1024; in every draw some slot is full and some holds exactly 256.
All inputs are finite; a program needn't handle non-finite values.
Results may differ from the reference program's by a relative error of at most 0.024.
Values may be sent and summed in bfloat16 or wider, within the bound.
A program may use at most 256 MiB of HBM per device.

```python
import math
import jax
import jax.numpy as jnp
from jax import lax

D = 2048
H = 16
KV = 8
HD = 128
FF = 6144
SLOT = 1024
MIN_LEN = 256
SEQS = 8
TOKENS = 8192


def draw_lengths(key, part):
    key = jax.random.fold_in(key, 7)
    first_key, second_key, third_key = jax.random.split(key, 3)
    values = jax.random.randint(first_key, (SEQS,), MIN_LEN, SLOT + 1)
    full_spot = jax.random.randint(second_key, (), 0, SEQS)
    short_spot = (full_spot + 1 + jax.random.randint(third_key, (), 0, SEQS - 1)) % SEQS
    slots = jnp.arange(SEQS)
    values = jnp.where(slots == full_spot, SLOT, values)
    values = jnp.where(slots == short_spot, MIN_LEN, values)
    return values.astype(jnp.int32)


def spiked(drawn, stream_key, source, target, blocks, factor):
    def block_of(dim):
        return (jnp.arange(drawn.shape[dim]) // (drawn.shape[dim] // blocks)).reshape((-1,) + (1,) * (drawn.ndim - 1 - dim))

    first = jax.random.permutation(stream_key, blocks)[block_of(target)]
    other_side = (block_of(target) + blocks // 2) % blocks
    return jnp.where((block_of(source) == first) | (block_of(source) == other_side), factor * drawn, drawn)


def level_of(own_key, extent, shards, smallest, high):
    level, own = 1.0, jax.random.fold_in(own_key, 6)
    for dim, shards_of in shards:
        heights = jnp.exp(jax.random.uniform(jax.random.fold_in(own, dim), (shards_of,), jnp.float32, smallest / len(shards), high / len(shards)))
        level = level * jnp.repeat(heights, extent[dim] // shards_of).reshape([-1 if axis == dim else 1 for axis in range(len(extent))])
    return level


def scatter_about(rng, shape, spread, limit, cuts=(), kind=jnp.bfloat16):
    result = jax.random.normal(rng, shape, jnp.float32) * spread
    if len(cuts) > 0:
        result = level_of(rng, shape, cuts, -0.22, 0.18) * result
    return jnp.clip(result, min=-limit, max=limit).astype(kind)


def noise_with(stream_key, shape, deviation, bound, cuts, heavy, kind=jnp.bfloat16):
    drawn = deviation * jax.random.normal(stream_key, shape, jnp.float32)
    if cuts:
        drawn = drawn * level_of(stream_key, shape, cuts, -0.22, 0.18)
    return jnp.clip(spiked(drawn, jax.random.fold_in(stream_key, 3), *heavy), -bound, bound).astype(kind)


def setup_inputs(seed: int = 0) -> dict:
    splits = jax.random.split(jax.random.key(seed), 15)
    return {
        "tokens": noise_with(splits[0], (TOKENS, D), 1.0, 6.0, ((0, 8),), (0, 1, 8, 2.0)),
        "lengths": draw_lengths(jax.random.fold_in(splits[14], 71), 0),
        "in_gain": jnp.clip(1.0 + 0.1 * jax.random.normal(splits[2], (D,), jnp.float32), 0.5, 1.5),
        "w_query": scatter_about(splits[3], (D, H * HD), D ** -0.5, 0.125, ((1, 4),)),
        "w_key": scatter_about(splits[4], (D, KV * HD), D ** -0.5, 0.125, ((1, 4),)),
        "w_value": scatter_about(splits[5], (D, KV * HD), D ** -0.5, 0.125, ((1, 4),)),
        "query_gain": jnp.clip(jnp.exp(jax.random.uniform(splits[6], (HD,), jnp.float32, math.log(1.0), math.log(2.0))), 1.0, 2.0),
        "key_gain": jnp.clip(jnp.exp(jax.random.uniform(splits[7], (HD,), jnp.float32, math.log(1.0), math.log(2.0))), 1.0, 2.0),
        "w_out": scatter_about(splits[8], (H * HD, D), (H * HD // 32) ** -0.5, 0.75, ((0, 4),)),
        "post_gain": jnp.clip(1.0 + 0.1 * jax.random.normal(splits[9], (D,), jnp.float32), 0.5, 1.5),
        "w_gate": scatter_about(splits[10], (D, FF), D ** -0.5, 0.125, ((1, 4),)),
        "w_up": scatter_about(splits[11], (D, FF), D ** -0.5, 0.125, ((1, 4),)),
        "w_down": scatter_about(splits[12], (FF, D), (FF // 2) ** -0.5, 0.109375, ((0, 4),)),
        "out_grad": scatter_about(splits[13], (TOKENS, D), 1.0, 6.0, ((0, 8),)),
    }


NORM_EPS = 1e-06
ROPE_BASE = 1000000.0
MASK_FILL = -1e+30

@jax.custom_vjp
def low(v):
    return lax.optimization_barrier(v.astype(jnp.bfloat16)).astype(jnp.float32)

@jax.custom_vjp
def low_back(v):
    return v

def low_keep(v):
    return (low(v), None)

def low_pass(kept, grad):
    return (grad,)

def back_keep(v):
    return (v, None)

def back_low(kept, grad):
    return (low(grad),)
low.defvjp(low_keep, low_pass)
low_back.defvjp(back_keep, back_low)

def low_both(matrix):
    return low_back(low(matrix))

def norm_rows(matrix, scale_gain):
    return matrix * lax.rsqrt(lax.optimization_barrier(jnp.mean(matrix * matrix, axis=-1, keepdims=True)) + NORM_EPS) * scale_gain

def rotary(head_width, row_count):
    half_width = head_width // 2
    inv_freq = ROPE_BASE ** (-2.0 * jnp.arange(half_width, dtype=jnp.float32) / head_width)
    angles = jnp.arange(row_count, dtype=jnp.float32)[:, None] * inv_freq[None, :]
    return (jnp.cos(angles), jnp.sin(angles))

def rotate(matrix, cosine, sine_table):
    half_width = matrix.shape[-1] // 2
    first_half = matrix[..., :half_width]
    second_half = matrix[..., half_width:]
    cos_part = cosine[:, None, :]
    sin_part = sine_table[:, None, :]
    return jnp.concatenate([first_half * cos_part - second_half * sin_part, second_half * cos_part + first_half * sin_part], axis=-1)

def mat_dot(left, right):
    return jnp.dot(left, right, precision=lax.Precision.HIGHEST)

def one_sequence(seq_x, length, params):
    in_gain, w_query, w_key, w_value, query_gain, key_gain, w_out, post_gain, w_gate, w_up, w_down = params
    cosine, sine_table = rotary(HD, SLOT)
    normed = low(norm_rows(seq_x, in_gain))
    q_raw = low_back(mat_dot(normed, w_query)).reshape(SLOT, H, HD)
    k_raw = low_back(mat_dot(normed, w_key)).reshape(SLOT, KV, HD)
    values = low_both(mat_dot(normed, w_value)).reshape(SLOT, KV, HD)
    query = low(rotate(norm_rows(q_raw, query_gain), cosine, sine_table))
    keys = low(rotate(norm_rows(k_raw, key_gain), cosine, sine_table))
    key_rep = jnp.repeat(keys, H // KV, axis=1)
    value_rep = jnp.repeat(values, H // KV, axis=1)
    position = jnp.arange(SLOT, dtype=jnp.int32)
    allowed = (position[None, :] <= position[:, None]) & (position[None, :] < length)
    scores = low_back(jnp.einsum('qhd,khd->hqk', query, key_rep, precision=lax.Precision.HIGHEST) * HD ** (-0.5))
    probs = low(jax.nn.softmax(jnp.where(allowed[None], scores, MASK_FILL), axis=-1))
    heads = low_both(jnp.einsum('hqk,khd->qhd', probs, value_rep, precision=lax.Precision.HIGHEST).reshape(SLOT, H * HD))
    resid = seq_x + low_back(mat_dot(heads, w_out))
    hidden_in = low(norm_rows(resid, post_gain))
    gate_pre = low_back(mat_dot(hidden_in, w_gate))
    up_pre = low_back(mat_dot(hidden_in, w_up))
    act_low = low(jax.nn.silu(gate_pre) * up_pre)
    mixed = low_back(mat_dot(act_low, w_down))
    keep_rows = (position < length).astype(seq_x.dtype)[:, None]
    return keep_rows * (resid + mixed)

def layer(tokens_f, in_gain, w_query, w_key, w_value, query_gain, key_gain, w_out, post_gain, w_gate, w_up, w_down, lengths):
    params = (in_gain, w_query, w_key, w_value, query_gain, key_gain, w_out, post_gain, w_gate, w_up, w_down)
    seq_fn = jax.checkpoint(one_sequence)

    def seq_step(state_carry, seq_item):
        return (state_carry, seq_fn(seq_item[0], seq_item[1], params))
    _, pieces = lax.scan(seq_step, 0, (tokens_f.reshape(SEQS, SLOT, D), lengths))
    return pieces.reshape(SEQS * SLOT, D)

def reference(tokens, lengths, in_gain, w_query, w_key, w_value, query_gain, key_gain, w_out, post_gain, w_gate, w_up, w_down, out_grad):
    floats = [arr.astype(jnp.float32) for arr in (tokens, in_gain, w_query, w_key, w_value, query_gain, key_gain, w_out, post_gain, w_gate, w_up, w_down)]

    def forward(tokens_f, in_gain_f, wq_f, wk_f, wv_f, qg_f, kg_f, wo_f, pg_f, wg_f, wu_f, wd_f):
        return layer(tokens_f, in_gain_f, wq_f, wk_f, wv_f, qg_f, kg_f, wo_f, pg_f, wg_f, wu_f, wd_f, lengths)
    value, back = jax.vjp(forward, *floats)
    grads = back(out_grad.astype(jnp.float32))
    return (value.astype(jnp.bfloat16), grads[0].astype(jnp.bfloat16), grads[1], grads[2], grads[3], grads[4], grads[5], grads[6], grads[7], grads[8], grads[9], grads[10], grads[11])
```

```python
import functools

import jax
import jax.numpy as jnp
from jax import lax
from jax.experimental import pallas as pl
from jax.experimental.pallas import tpu as pltpu
from jax.sharding import PartitionSpec as P

NORM_EPS = 1e-06
ROPE_BASE = 1000000.0
MASK_FILL = -1e30
LOW = jnp.bfloat16
F32 = jnp.float32
MESH = pl.DeviceIdType.MESH
VMEM_BYTES = 60 * 1024 * 1024
SUBS = 2


def unit_rows(matrix):
    return matrix * lax.rsqrt(jnp.mean(matrix * matrix, axis=-1, keepdims=True) + NORM_EPS)


def norm_rows(matrix, scale_gain):
    return unit_rows(matrix) * scale_gain


def rotary(head_width, row_count):
    half_width = head_width // 2
    inv_freq = ROPE_BASE ** (-2.0 * jnp.arange(half_width, dtype=F32) / head_width)
    angles = jnp.arange(row_count, dtype=F32)[:, None] * inv_freq[None, :]
    return (jnp.cos(angles), jnp.sin(angles))


def rotate(matrix, cosine, sine_table):
    half_width = matrix.shape[-1] // 2
    first_half = matrix[..., :half_width]
    second_half = matrix[..., half_width:]
    cos_part = cosine[:, None, :]
    sin_part = sine_table[:, None, :]
    return jnp.concatenate(
        [
            first_half * cos_part - second_half * sin_part,
            second_half * cos_part + first_half * sin_part,
        ],
        axis=-1,
    )


def dot_nn(left, right):
    return jnp.dot(left, right, preferred_element_type=F32)


def dot_tn(left, right):
    return lax.dot_general(left, right, (((0,), (0,)), ((), ())), preferred_element_type=F32)


def dot_nt(left, right):
    return lax.dot_general(left, right, (((1,), (1,)), ((), ())), preferred_element_type=F32)


def masked_scores(query_blk, key_blk, length, offset, score_scale):
    scores = (
        jnp.einsum("qcgd,kcd->cgqk", query_blk, key_blk, preferred_element_type=F32) * score_scale
    )
    q_pos = offset + jnp.arange(query_blk.shape[0], dtype=jnp.int32)
    k_pos = jnp.arange(key_blk.shape[0], dtype=jnp.int32)
    allowed = (k_pos[None, :] <= q_pos[:, None]) & (k_pos[None, :] < length)
    return jnp.where(allowed, scores, MASK_FILL)


class Swap:
    def __init__(self, count, rows, width):
        self.count, self.width = count, width
        self.bits = count.bit_length() - 1
        self.block = rows // count
        self.sub = self.block // SUBS
        self.half = width // 2
        self.orders = [list(range(self.bits)), list(range(self.bits))[::-1]]
        self.slots = []
        for order in self.orders:
            slot = {}
            for step in range(self.bits):
                for r in range(count):
                    if not any(r >> b & 1 for b in order[: step + 1]):
                        slot[step, r] = len(slot)
            self.slots.append(slot)

    def scratch(self):
        n = self.count
        return [
            pltpu.VMEM((2, n - 1, self.block, self.half), LOW),
            pltpu.SemaphoreType.DMA((2, n, SUBS)),
            pltpu.SemaphoreType.DMA((2, n, SUBS)),
            pltpu.SemaphoreType.DMA((2, n * self.bits, SUBS)),
            pltpu.SemaphoreType.DMA((2, n, SUBS)),
        ]

    def bind(self, part, recv, scatter_send, scatter_recv, gather_send, gather_recv, dest):
        self.part, self.recv, self.dest = part, recv, dest
        self.sems = scatter_send, scatter_recv, gather_send, gather_recv
        self.me = lax.axis_index("tensor")

    def near(self, bit):
        own = (self.me // 2**bit) % 2
        return self.me + (1 - 2 * own) * 2**bit

    def rows(self, r, sub=None):
        owner = self.me
        for bit in range(self.bits):
            if r >> bit & 1:
                own = (self.me // 2**bit) % 2
                owner = owner + (1 - 2 * own) * 2**bit
        start = owner * self.block
        if sub is None:
            return pl.ds(pl.multiple_of(start, self.block), self.block)
        return pl.ds(pl.multiple_of(start + sub * self.sub, self.sub), self.sub)

    def columns(self, half):
        return pl.ds(half * self.half, self.half)

    def greet(self):
        barrier = pltpu.get_barrier_semaphore()
        for bit in range(self.bits):
            pl.semaphore_signal(
                barrier, inc=1, device_id={"tensor": self.near(bit)}, device_id_type=MESH
            )
        pl.semaphore_wait(barrier, self.bits)

    def first(self, half, r):
        return next(k for k, bit in enumerate(self.orders[half]) if r >> bit & 1)

    def scatter_copy(self, half, r, sub):
        step = self.first(half, r)
        bit = self.orders[half][step]
        slot = self.slots[half][step, r ^ (1 << bit)]
        return pltpu.make_async_remote_copy(
            src_ref=self.part.at[self.rows(r, sub), self.columns(half)],
            dst_ref=self.recv.at[half, slot, pl.ds(sub * self.sub, self.sub)],
            send_sem=self.sems[0].at[half, r, sub],
            recv_sem=self.sems[1].at[half, slot, sub],
            device_id={"tensor": self.near(bit)},
            device_id_type=MESH,
        )

    def scatter_wait(self, half, step, r, sub):
        slot = self.slots[half][step, r]
        ref = self.recv.at[half, slot, pl.ds(sub * self.sub, self.sub)]
        pltpu.make_async_copy(ref, ref, self.sems[1].at[half, slot, sub]).wait()
        return ref

    def scatter_start(self, r):
        for sub in range(SUBS):
            for half in range(2):
                if self.first(half, r) == 0:
                    self.scatter_copy(half, r, sub).start()

    def scatter_forward(self, half, r):
        step = self.first(half, r)
        for sub in range(SUBS):
            where = self.rows(r, sub), self.columns(half)
            total = self.part[where].astype(F32)
            for j in range(step):
                total = total + self.scatter_wait(half, j, r, sub)[...].astype(F32)
            self.part[where] = total.astype(LOW)
            self.scatter_copy(half, r, sub).start()

    def forwards(self):
        todo = [
            (self.first(half, r), half, r)
            for half in range(2)
            for r in range(1, self.count)
            if self.first(half, r) > 0
        ]
        return [(half, r) for _, half, r in sorted(todo)]

    def scatter_result(self, sub):
        total = []
        for half in range(2):
            value = self.part[self.rows(0, sub), self.columns(half)].astype(F32)
            for j in range(self.bits):
                value = value + self.scatter_wait(half, j, 0, sub)[...].astype(F32)
            total.append(value)
        return jnp.concatenate(total, axis=1)

    def scatter_end(self):
        for half in range(2):
            for r in range(1, self.count):
                for sub in range(SUBS):
                    self.scatter_copy(half, r, sub).wait_send()

    def last(self, half, r):
        order = self.orders[half][::-1]
        return max([-1] + [j for j, bit in enumerate(order) if r >> bit & 1])

    def gather_copy(self, half, r, step, sub, source=None):
        bit = self.orders[half][::-1][step]
        where = self.rows(r, sub), self.columns(half)
        return pltpu.make_async_remote_copy(
            src_ref=self.dest.at[where],
            dst_ref=self.dest.at[where],
            send_sem=self.sems[2].at[half, r * self.bits + step, sub],
            recv_sem=self.sems[3].at[half, r ^ (1 << bit), sub],
            device_id={"tensor": self.near(bit)},
            device_id_type=MESH,
        )

    def gather_start(self, sub):
        for step in range(self.bits):
            for half in range(2):
                self.gather_copy(half, 0, step, sub).start()

    def gather_wait(self, half, r, sub):
        ref = self.dest.at[self.rows(r, sub), self.columns(half)]
        pltpu.make_async_copy(ref, ref, self.sems[3].at[half, r, sub]).wait()

    def gather_steps(self):
        todo = [
            (self.last(half, r), sub, bin(r).count("1"), half, r)
            for half in range(2)
            for r in range(1, self.count)
            for sub in range(SUBS)
        ]
        return [(half, r, sub) for _, sub, _, half, r in sorted(todo)]

    def gather_pass(self, half, r, sub):
        self.gather_wait(half, r, sub)
        for step in range(self.last(half, r) + 1, self.bits):
            self.gather_copy(half, r, step, sub).start()

    def gather_end(self):
        for half in range(2):
            for r in range(self.count):
                for step in range(self.last(half, r) + 1, self.bits):
                    for sub in range(SUBS):
                        self.gather_copy(half, r, step, sub).wait_send()

    def order(self):
        return sorted(range(self.count), key=lambda r: (-bin(r).count("1"), r))


def tiled(total, size, body):
    count = total // size

    def step(i, carry):
        body(pl.ds(pl.multiple_of(i * size, size), size))
        return carry

    lax.fori_loop(0, count, step, 0)


def any_spec():
    return pl.BlockSpec(memory_space=pl.ANY)


def vmem_spec():
    return pl.BlockSpec(memory_space=pltpu.VMEM)


def kernel_params(identity):
    return pltpu.CompilerParams(
        collective_id=identity, has_side_effects=True, vmem_limit_bytes=VMEM_BYTES
    )


def out_kernel(
    swap, heads_ref, w_ref, x_ref, gain_ref, resid_ref, hidden_ref, part, dest, local_sem, *comm
):
    swap.bind(part, *comm, dest)
    swap.greet()
    for r in swap.order():
        rows = swap.rows(r)

        def columns(cols):
            part[rows, cols] = dot_nn(heads_ref[rows, :], w_ref[:, cols]).astype(LOW)

        tiled(swap.width, 512, columns)
        if r:
            swap.scatter_start(r)
    for half, r in swap.forwards():
        swap.scatter_forward(half, r)
    for sub in range(SUBS):
        local = pl.ds(sub * swap.sub, swap.sub)
        resid = x_ref[local, :].astype(F32) + swap.scatter_result(sub)
        resid_ref[local, :] = resid
        dest[swap.rows(0, sub), :] = (unit_rows(resid) * gain_ref[...]).astype(LOW)
        swap.gather_start(sub)
    for half, r, sub in swap.gather_steps():
        swap.gather_pass(half, r, sub)
    swap.scatter_end()
    swap.gather_end()
    copy = pltpu.make_async_copy(dest, hidden_ref, local_sem)
    copy.start()
    copy.wait()


def out_sum(count, heads, w_out, x_rows, gain):
    rows, width = heads.shape[0], w_out.shape[1]
    swap = Swap(count, rows, width)
    return pl.pallas_call(
        functools.partial(out_kernel, swap),
        out_shape=(
            jax.ShapeDtypeStruct((swap.block, width), F32),
            jax.ShapeDtypeStruct((rows, width), LOW),
        ),
        in_specs=[vmem_spec()] * 4,
        out_specs=(vmem_spec(), any_spec()),
        scratch_shapes=[
            pltpu.VMEM((rows, width), LOW),
            pltpu.VMEM((rows, width), LOW),
            pltpu.SemaphoreType.DMA,
            *swap.scratch(),
        ],
        compiler_params=kernel_params(0),
        name="out_sum",
    )(heads, w_out, x_rows, gain[None, :])


def feed_kernel(
    swap,
    shards,
    hidden_hbm,
    grad_hbm,
    wg_hbm,
    wu_hbm,
    wd_hbm,
    resid_ref,
    gain_ref,
    act_out,
    gg_out,
    gu_out,
    gd_out,
    d_resid_ref,
    low_out,
    gain_part_ref,
    hidden,
    grad,
    wg,
    wu,
    wd,
    act,
    dg,
    du,
    part,
    dest,
    stage,
    in_sems,
    stage_sems,
    out_sems,
    *comm,
):
    swap.bind(part, *comm, dest)
    loads = [
        pltpu.make_async_copy(src, dst, in_sems.at[i])
        for i, (src, dst) in enumerate(
            [(hidden_hbm, hidden), (wg_hbm, wg), (wu_hbm, wu), (grad_hbm, grad), (wd_hbm, wd)]
        )
    ]
    for load in loads:
        load.start()
    swap.greet()
    for load in loads:
        load.wait()
    units = wg.shape[1]
    unit_tile = 512 if units % 512 == 0 else 256
    forwards = swap.forwards()
    order = swap.order()
    for place, r in enumerate(order):
        rows = swap.rows(r)

        def unit_step(cols):
            gate = dot_nn(hidden[rows, :], wg[:, cols])
            up = dot_nn(hidden[rows, :], wu[:, cols])
            d_act = dot_nt(grad[rows, :], wd[cols, :])
            sig = jax.nn.sigmoid(gate)
            silu = gate * sig
            act[rows, cols] = (silu * up).astype(LOW)
            dg[rows, cols] = (d_act * up * sig * (1.0 + gate * (1.0 - sig))).astype(LOW)
            du[rows, cols] = (d_act * silu).astype(LOW)

        tiled(units, unit_tile, unit_step)

        def back_step(cols):
            part[rows, cols] = (
                dot_nt(dg[rows, :], wg[cols, :]) + dot_nt(du[rows, :], wu[cols, :])
            ).astype(LOW)

        tiled(swap.width, 512, back_step)
        if r:
            swap.scatter_start(r)
        if place == len(order) - 2:
            for half, s in forwards:
                swap.scatter_forward(half, s)
    act_copy = pltpu.make_async_copy(act, act_out, in_sems.at[0])
    act_copy.start()

    def weight_grads(left, right, out, base):
        tile = out.shape[0] // shards

        def stage_copy(i, slot):
            rows = pl.ds(pl.multiple_of(i * tile, tile), tile)
            return pltpu.make_async_copy(stage.at[slot], out.at[rows, :], stage_sems.at[slot])

        def step(i, carry):
            slot = lax.rem(i, 2)

            @pl.when(i >= 2)
            def _():
                stage_copy(i, slot).wait()

            cols = pl.ds(pl.multiple_of(i * tile, tile), tile)
            stage[slot] = dot_tn(left[:, cols], right[...]).astype(LOW)
            stage_copy(i, slot).start()
            return carry

        lax.fori_loop(0, shards, step, 0)
        for slot in range(2):
            stage_copy(slot, slot).wait()

    weight_grads(grad, act, gd_out, 0)
    for sub in range(SUBS):
        local = pl.ds(sub * swap.sub, swap.sub)
        d_hidden = swap.scatter_result(sub)
        resid = resid_ref[local, :]
        c = lax.rsqrt(jnp.mean(resid * resid, axis=-1, keepdims=True) + NORM_EPS)
        unit = resid * c
        partial = jnp.sum(d_hidden * unit, axis=0, keepdims=True)
        if sub == 0:
            gain_part_ref[...] = partial
        else:
            gain_part_ref[...] += partial
        g = d_hidden * gain_ref[...]
        d_resid = grad[swap.rows(0, sub), :].astype(F32) + c * (
            g - unit * jnp.mean(g * unit, axis=-1, keepdims=True)
        )
        d_resid_ref[local, :] = d_resid
        dest[swap.rows(0, sub), :] = d_resid.astype(LOW)
        swap.gather_start(sub)
    weight_grads(hidden, dg, gg_out, 0)
    for half, r, sub in swap.gather_steps():
        swap.gather_pass(half, r, sub)
    weight_grads(hidden, du, gu_out, 0)
    swap.scatter_end()
    swap.gather_end()
    low_copy = pltpu.make_async_copy(dest, low_out, out_sems.at[0])
    low_copy.start()
    act_copy.wait()
    low_copy.wait()


def feed(count, dp_count, hidden, d_out_low, w_gate, w_up, w_down, resid, gain):
    rows, width = hidden.shape
    units = w_gate.shape[1]
    swap = Swap(count, rows, width)
    grad_shape = jax.ShapeDtypeStruct((width, units), LOW)
    return pl.pallas_call(
        functools.partial(feed_kernel, swap, dp_count),
        out_shape=(
            jax.ShapeDtypeStruct((rows, units), LOW),
            grad_shape,
            grad_shape,
            grad_shape,
            jax.ShapeDtypeStruct((swap.block, width), F32),
            jax.ShapeDtypeStruct((rows, width), LOW),
            jax.ShapeDtypeStruct((1, width), F32),
        ),
        in_specs=[any_spec()] * 5 + [vmem_spec()] * 2,
        out_specs=(any_spec(),) * 4 + (vmem_spec(), any_spec(), vmem_spec()),
        scratch_shapes=[
            pltpu.VMEM((rows, width), LOW),
            pltpu.VMEM((rows, width), LOW),
            pltpu.VMEM((width, units), LOW),
            pltpu.VMEM((width, units), LOW),
            pltpu.VMEM((units, width), LOW),
            pltpu.VMEM((rows, units), LOW),
            pltpu.VMEM((rows, units), LOW),
            pltpu.VMEM((rows, units), LOW),
            pltpu.VMEM((rows, width), LOW),
            pltpu.VMEM((rows, width), LOW),
            pltpu.VMEM((2, width // dp_count, units), LOW),
            pltpu.SemaphoreType.DMA((5,)),
            pltpu.SemaphoreType.DMA((2,)),
            pltpu.SemaphoreType.DMA((1,)),
            *swap.scratch(),
        ],
        compiler_params=kernel_params(1),
        name="feed",
    )(hidden, d_out_low, w_gate, w_up, w_down, resid, gain[None, :])


def on_device(
    tensor_count,
    dp_count,
    tokens,
    lengths,
    in_gain,
    w_query,
    w_key,
    w_value,
    query_gain,
    key_gain,
    w_out,
    post_gain,
    w_gate,
    w_up,
    w_down,
    out_grad,
):
    row_count = tokens.shape[0]
    slot_len = row_count
    head_width = query_gain.shape[0]
    q_heads = w_query.shape[1] // head_width
    kv_heads = w_key.shape[1] // head_width
    group_size = q_heads // kv_heads
    block_len = min(512, slot_len)
    block_count = slot_len // block_len
    share = row_count // tensor_count
    score_scale = head_width ** (-0.5)
    length = lengths[0]
    tensor_me = lax.axis_index("tensor")

    def own_rows(matrix):
        return lax.dynamic_slice_in_dim(matrix, tensor_me * share, share, axis=0)

    position = jnp.arange(row_count, dtype=jnp.int32)
    valid_rows = (position < length).astype(F32)[:, None]
    inputs = tokens.astype(F32)
    normed = (unit_rows(inputs) * in_gain).astype(LOW)
    q_raw = dot_nn(normed, w_query)
    k_raw = dot_nn(normed, w_key)
    values_low = dot_nn(normed, w_value).astype(LOW).reshape(row_count, kv_heads, head_width)
    cosine, sine_table = rotary(head_width, slot_len)

    def prepare(query_in, key_in, q_gain, k_gain):
        query_heads = norm_rows(query_in.reshape(row_count, q_heads, head_width), q_gain)
        key_heads = norm_rows(key_in.reshape(row_count, kv_heads, head_width), k_gain)
        return (rotate(query_heads, cosine, sine_table), rotate(key_heads, cosine, sine_table))

    (query_rot, key_rot), prep_back = jax.vjp(prepare, q_raw, k_raw, query_gain, key_gain)
    query_low = query_rot.astype(LOW).reshape(row_count, kv_heads, group_size, head_width)
    keys_low = key_rot.astype(LOW)
    log_totals = []
    heads = []
    for block in range(block_count):
        rows = slice(block * block_len, (block + 1) * block_len)
        key_end = (block + 1) * block_len
        scores = masked_scores(
            query_low[rows], keys_low[:key_end], length, block * block_len, score_scale
        )
        row_peak = jnp.max(scores, axis=-1, keepdims=True)
        exponent = jnp.exp(scores - row_peak)
        row_total = jnp.sum(exponent, axis=-1, keepdims=True)
        probs_low = (exponent / row_total).astype(LOW)
        head_blk = (
            jnp.einsum("cgqk,kcd->qcgd", probs_low, values_low[:key_end], preferred_element_type=F32)
            .reshape(block_len, q_heads * head_width)
            .astype(LOW)
        )
        log_totals.append(row_peak + jnp.log(row_total))
        heads.append(head_blk)
    heads_low = jnp.concatenate(heads, axis=0)
    resid, hidden = out_sum(tensor_count, heads_low, w_out, own_rows(tokens), post_gain)
    d_out_low = (out_grad.astype(F32) * valid_rows).astype(LOW)
    act, grad_gate, grad_up, grad_down, d_resid, resid_low, post_gain_part = feed(
        tensor_count, dp_count, hidden, d_out_low, w_gate, w_up, w_down, resid, post_gain
    )
    mixed = lax.psum(dot_nn(act, w_down).astype(LOW), "tensor")
    resid_all = lax.all_gather(resid.astype(LOW), "tensor", tiled=True).astype(F32)
    output = (valid_rows * (resid_all + mixed.astype(F32))).astype(LOW)

    def over_dp(grad):
        return lax.psum_scatter(grad, "dp", scatter_dimension=0, tiled=True).astype(F32)

    grad_down = over_dp(grad_down).T
    grad_gate = over_dp(grad_gate)
    grad_up = over_dp(grad_up)
    q_pieces = [None] * block_count
    key_acc = jnp.zeros((slot_len, kv_heads, head_width), F32)
    value_acc = jnp.zeros((slot_len, kv_heads, head_width), F32)
    d_heads = dot_nt(resid_low, w_out).astype(LOW).reshape(row_count, kv_heads, group_size, head_width)
    for block in range(block_count):
        rows = slice(block * block_len, (block + 1) * block_len)
        key_end = (block + 1) * block_len
        query_blk = query_low[rows]
        key_blk = keys_low[:key_end]
        value_blk = values_low[:key_end]
        grad_blk = d_heads[rows]
        scores = masked_scores(query_blk, key_blk, length, block * block_len, score_scale)
        probs = jnp.exp(scores - log_totals[block])
        probs_low = probs.astype(LOW)
        d_probs = jnp.einsum("qcgd,kcd->cgqk", grad_blk, value_blk, preferred_element_type=F32)
        row_delta = jnp.sum(probs * d_probs, axis=-1, keepdims=True)
        d_scores = (probs * (d_probs - row_delta)).astype(LOW)
        q_pieces[block] = (
            jnp.einsum("cgqk,kcd->qcgd", d_scores, key_blk, preferred_element_type=F32)
            * score_scale
        )
        key_acc = key_acc.at[:key_end].add(
            jnp.einsum("cgqk,qcgd->kcd", d_scores, query_blk, preferred_element_type=F32)
            * score_scale
        )
        value_acc = value_acc.at[:key_end].add(
            jnp.einsum("cgqk,qcgd->kcd", probs_low, grad_blk, preferred_element_type=F32)
        )
    d_query_rot = jnp.concatenate(q_pieces, axis=0).reshape(row_count, q_heads, head_width)
    d_value = value_acc.reshape(row_count, kv_heads * head_width).astype(LOW)
    d_q_raw, d_k_raw, query_gain_part, key_gain_part = prep_back((d_query_rot, key_acc))
    d_query = d_q_raw.astype(LOW).reshape(row_count, -1)
    d_key = d_k_raw.astype(LOW).reshape(row_count, -1)
    normed_part = (
        dot_nt(d_query, w_query) + dot_nt(d_key, w_key) + dot_nt(d_value, w_value)
    ).astype(LOW)
    d_normed = own_rows(lax.psum(normed_part, "tensor")).astype(F32)
    in_unit, in_back = jax.vjp(unit_rows, own_rows(tokens).astype(F32))
    in_gain_part = jnp.sum(d_normed * in_unit, axis=0)
    in_rows = (d_resid + in_back(d_normed * in_gain)[0]).astype(LOW)
    in_grad = lax.all_gather(in_rows, "tensor", tiled=True)
    grad_out = over_dp(dot_tn(resid_low, heads_low).astype(LOW)).T
    grad_query = over_dp(dot_tn(normed, d_query).astype(LOW))
    grad_key = over_dp(dot_tn(normed, d_key).astype(LOW))
    grad_value = over_dp(dot_tn(normed, d_value).astype(LOW))
    grad_in_gain, grad_query_gain, grad_key_gain, grad_post_gain = lax.psum(
        (in_gain_part, query_gain_part, key_gain_part, post_gain_part[0]), ("dp", "tensor")
    )
    return (
        output,
        in_grad,
        grad_in_gain,
        grad_query,
        grad_key,
        grad_value,
        grad_query_gain,
        grad_key_gain,
        grad_out,
        grad_post_gain,
        grad_gate,
        grad_up,
        grad_down,
    )


def solution(mesh):
    tensor_count, dp_count = mesh.shape["tensor"], mesh.shape["dp"]

    def layer(*args):
        return on_device(tensor_count, dp_count, *args)

    return jax.shard_map(
        layer,
        mesh=mesh,
        in_specs=(
            P("dp", None),
            P("dp"),
            P(),
            P(None, "tensor"),
            P(None, "tensor"),
            P(None, "tensor"),
            P(),
            P(),
            P("tensor", None),
            P(),
            P(None, "tensor"),
            P(None, "tensor"),
            P("tensor", None),
            P("dp", None),
        ),
        out_specs=(
            P("dp", None),
            P("dp", None),
            P(),
            P("dp", "tensor"),
            P("dp", "tensor"),
            P("dp", "tensor"),
            P(),
            P(),
            P("tensor", "dp"),
            P(),
            P("dp", "tensor"),
            P("dp", "tensor"),
            P("tensor", "dp"),
        ),
        check_vma=False,
    )
```

```python
import functools

import jax
import jax.numpy as jnp
from jax import lax
from jax.experimental import pallas as pl
from jax.experimental.pallas import tpu as pltpu
from jax.sharding import PartitionSpec as P

NORM_EPS = 1e-06
ROPE_BASE = 1000000.0
MASK_FILL = -1e30
LOW = jnp.bfloat16
F32 = jnp.float32
MESH = pl.DeviceIdType.MESH
VMEM_BYTES = 63 * 1024 * 1024
SUBS = 2


def unit_rows(matrix):
    return matrix * lax.rsqrt(jnp.mean(matrix * matrix, axis=-1, keepdims=True) + NORM_EPS)


def norm_rows(matrix, scale_gain):
    return unit_rows(matrix) * scale_gain


def rotary(head_width, row_count):
    half_width = head_width // 2
    inv_freq = ROPE_BASE ** (-2.0 * jnp.arange(half_width, dtype=F32) / head_width)
    angles = jnp.arange(row_count, dtype=F32)[:, None] * inv_freq[None, :]
    return (jnp.cos(angles), jnp.sin(angles))


def rotate(matrix, cosine, sine_table):
    half_width = matrix.shape[-1] // 2
    first_half = matrix[..., :half_width]
    second_half = matrix[..., half_width:]
    cos_part = cosine[:, None, :]
    sin_part = sine_table[:, None, :]
    return jnp.concatenate(
        [
            first_half * cos_part - second_half * sin_part,
            second_half * cos_part + first_half * sin_part,
        ],
        axis=-1,
    )


def dot_nn(left, right):
    return jnp.dot(left, right, preferred_element_type=F32)


def dot_tn(left, right):
    return lax.dot_general(left, right, (((0,), (0,)), ((), ())), preferred_element_type=F32)


def dot_nt(left, right):
    return lax.dot_general(left, right, (((1,), (1,)), ((), ())), preferred_element_type=F32)


def masked_scores(query_blk, key_blk, length, offset, score_scale):
    scores = (
        jnp.einsum("qcgd,kcd->cgqk", query_blk, key_blk, preferred_element_type=F32) * score_scale
    )
    q_pos = offset + jnp.arange(query_blk.shape[0], dtype=jnp.int32)
    k_pos = jnp.arange(key_blk.shape[0], dtype=jnp.int32)
    allowed = (k_pos[None, :] <= q_pos[:, None]) & (k_pos[None, :] < length)
    return jnp.where(allowed, scores, MASK_FILL)


class Swap:
    def __init__(self, count, rows, width):
        self.count, self.width = count, width
        self.bits = count.bit_length() - 1
        self.block = rows // count
        self.sub = self.block // SUBS
        self.half = width // 2
        self.orders = [list(range(self.bits)), list(range(self.bits))[::-1]]
        self.slots = []
        for order in self.orders:
            slot = {}
            for step in range(self.bits):
                for r in range(count):
                    if not any(r >> b & 1 for b in order[: step + 1]):
                        slot[step, r] = len(slot)
            self.slots.append(slot)

    def landing(self):
        return pltpu.VMEM((2, self.count - 1, self.block, self.half), LOW)

    def semaphores(self):
        n = self.count
        return [
            pltpu.SemaphoreType.DMA((2, n, SUBS)),
            pltpu.SemaphoreType.DMA((2, n, SUBS)),
            pltpu.SemaphoreType.DMA((2, n * self.bits, SUBS)),
            pltpu.SemaphoreType.DMA((2, n, SUBS)),
        ]

    def bind(self, part, recv, dest, sems, own=None):
        self.part, self.recv, self.dest, self.sems = part, recv, dest, sems
        self.own = dest if own is None else own
        self.me = lax.axis_index("tensor")
        return self

    def near(self, bit):
        own = (self.me // 2**bit) % 2
        return self.me + (1 - 2 * own) * 2**bit

    def rows(self, r, sub=None):
        owner = self.me
        for bit in range(self.bits):
            if r >> bit & 1:
                own = (self.me // 2**bit) % 2
                owner = owner + (1 - 2 * own) * 2**bit
        start = owner * self.block
        if sub is None:
            return pl.ds(pl.multiple_of(start, self.block), self.block)
        return pl.ds(pl.multiple_of(start + sub * self.sub, self.sub), self.sub)

    def columns(self, half):
        return pl.ds(half * self.half, self.half)

    def signal(self, sem):
        for bit in range(self.bits):
            pl.semaphore_signal(
                sem, inc=1, device_id={"tensor": self.near(bit)}, device_id_type=MESH
            )

    def first(self, half, r):
        return next(k for k, bit in enumerate(self.orders[half]) if r >> bit & 1)

    def scatter_copy(self, half, r, sub):
        step = self.first(half, r)
        bit = self.orders[half][step]
        slot = self.slots[half][step, r ^ (1 << bit)]
        return pltpu.make_async_remote_copy(
            src_ref=self.part.at[self.rows(r, sub), self.columns(half)],
            dst_ref=self.recv.at[half, slot, pl.ds(sub * self.sub, self.sub)],
            send_sem=self.sems[0].at[half, r, sub],
            recv_sem=self.sems[1].at[half, slot, sub],
            device_id={"tensor": self.near(bit)},
            device_id_type=MESH,
        )

    def scatter_wait(self, half, step, r, sub):
        slot = self.slots[half][step, r]
        ref = self.recv.at[half, slot, pl.ds(sub * self.sub, self.sub)]
        pltpu.make_async_copy(ref, ref, self.sems[1].at[half, slot, sub]).wait()
        return ref

    def scatter_start(self, r):
        for sub in range(SUBS):
            for half in range(2):
                if self.first(half, r) == 0:
                    self.scatter_copy(half, r, sub).start()

    def scatter_forward(self, half, r):
        step = self.first(half, r)
        for sub in range(SUBS):
            where = self.rows(r, sub), self.columns(half)
            total = self.part[where].astype(F32)
            for j in range(step):
                total = total + self.scatter_wait(half, j, r, sub)[...].astype(F32)
            self.part[where] = total.astype(LOW)
            self.scatter_copy(half, r, sub).start()

    def forwards(self):
        todo = [
            (self.first(half, r), half, r)
            for half in range(2)
            for r in range(1, self.count)
            if self.first(half, r) > 0
        ]
        return [(half, r) for _, half, r in sorted(todo)]

    def scatter_result(self, sub):
        total = []
        for half in range(2):
            value = self.part[self.rows(0, sub), self.columns(half)].astype(F32)
            for j in range(self.bits):
                value = value + self.scatter_wait(half, j, 0, sub)[...].astype(F32)
            total.append(value)
        return jnp.concatenate(total, axis=1)

    def scatter_end(self):
        for half in range(2):
            for r in range(1, self.count):
                for sub in range(SUBS):
                    self.scatter_copy(half, r, sub).wait_send()

    def last(self, half, r):
        order = self.orders[half][::-1]
        return max([-1] + [j for j, bit in enumerate(order) if r >> bit & 1])

    def gather_copy(self, half, r, step, sub):
        bit = self.orders[half][::-1][step]
        where = self.rows(r, sub), self.columns(half)
        return pltpu.make_async_remote_copy(
            src_ref=self.dest.at[where] if r else self.own.at[where],
            dst_ref=self.dest.at[where],
            send_sem=self.sems[2].at[half, r * self.bits + step, sub],
            recv_sem=self.sems[3].at[half, r ^ (1 << bit), sub],
            device_id={"tensor": self.near(bit)},
            device_id_type=MESH,
        )

    def gather_start(self, sub):
        for step in range(self.bits):
            for half in range(2):
                self.gather_copy(half, 0, step, sub).start()

    def gather_wait(self, half, r, sub):
        ref = self.dest.at[self.rows(r, sub), self.columns(half)]
        pltpu.make_async_copy(ref, ref, self.sems[3].at[half, r, sub]).wait()

    def gather_steps(self):
        todo = [
            (self.last(half, r), sub, bin(r).count("1"), half, r)
            for half in range(2)
            for r in range(1, self.count)
            for sub in range(SUBS)
        ]
        return [(half, r, sub) for _, sub, _, half, r in sorted(todo)]

    def gather_pass(self, half, r, sub):
        self.gather_wait(half, r, sub)
        for step in range(self.last(half, r) + 1, self.bits):
            self.gather_copy(half, r, step, sub).start()

    def gather_early(self):
        return [it for it in self.gather_steps() if self.last(it[0], it[1]) < self.bits - 1]

    def gather_late(self):
        return [it for it in self.gather_steps() if self.last(it[0], it[1]) == self.bits - 1]

    def gather_end(self):
        for half in range(2):
            for r in range(self.count):
                for step in range(self.last(half, r) + 1, self.bits):
                    for sub in range(SUBS):
                        self.gather_copy(half, r, step, sub).wait_send()

    def order(self):
        return sorted(range(self.count), key=lambda r: (-bin(r).count("1"), r))


def tiled(total, size, body):
    count = total // size

    def step(i, carry):
        body(pl.ds(pl.multiple_of(i * size, size), size))
        return carry

    lax.fori_loop(0, count, step, 0)


def any_spec():
    return pl.BlockSpec(memory_space=pl.ANY)


def vmem_spec():
    return pl.BlockSpec(memory_space=pltpu.VMEM)


def kernel_params(identity):
    return pltpu.CompilerParams(
        collective_id=identity, has_side_effects=True, vmem_limit_bytes=VMEM_BYTES
    )


def out_kernel(
    swap, heads_ref, w_ref, x_ref, gain_ref, resid_ref, hidden_ref, part, dest, local_sem, recv, *sems
):
    swap.bind(part, recv, dest, sems)
    barrier = pltpu.get_barrier_semaphore()
    swap.signal(barrier)
    pl.semaphore_wait(barrier, swap.bits)
    for r in swap.order():
        rows = swap.rows(r)

        def columns(cols):
            part[rows, cols] = dot_nn(heads_ref[rows, :], w_ref[:, cols]).astype(LOW)

        tiled(swap.width, 512, columns)
        if r:
            swap.scatter_start(r)
    for half, r in swap.forwards():
        swap.scatter_forward(half, r)
    for sub in range(SUBS):
        local = pl.ds(sub * swap.sub, swap.sub)
        resid = x_ref[local, :].astype(F32) + swap.scatter_result(sub)
        resid_ref[local, :] = resid
        dest[swap.rows(0, sub), :] = (unit_rows(resid) * gain_ref[...]).astype(LOW)
        swap.gather_start(sub)
    for half, r, sub in swap.gather_steps():
        swap.gather_pass(half, r, sub)
    swap.scatter_end()
    swap.gather_end()
    copy = pltpu.make_async_copy(dest, hidden_ref, local_sem)
    copy.start()
    copy.wait()


def out_sum(count, heads, w_out, x_rows, gain):
    rows, width = heads.shape[0], w_out.shape[1]
    swap = Swap(count, rows, width)
    return pl.pallas_call(
        functools.partial(out_kernel, swap),
        out_shape=(
            jax.ShapeDtypeStruct((swap.block, width), F32),
            jax.ShapeDtypeStruct((rows, width), LOW),
        ),
        in_specs=[vmem_spec()] * 4,
        out_specs=(vmem_spec(), any_spec()),
        scratch_shapes=[
            pltpu.VMEM((rows, width), LOW),
            pltpu.VMEM((rows, width), LOW),
            pltpu.SemaphoreType.DMA,
            swap.landing(),
            *swap.semaphores(),
        ],
        compiler_params=kernel_params(0),
        name="out_sum",
    )(heads, w_out, x_rows, gain[None, :])


class Line:
    def __init__(self, count, groups, tile, width):
        self.count, self.groups, self.tile, self.width = count, groups, tile, width
        self.places = count // 2

    def outputs(self):
        shape = (self.tile, self.width)
        return [
            jax.ShapeDtypeStruct((self.groups, self.places) + shape, LOW),
            jax.ShapeDtypeStruct((self.groups, self.places) + shape, LOW),
            jax.ShapeDtypeStruct((self.groups, self.places + 1) + shape, LOW),
        ]

    def semaphores(self):
        g, n = self.groups, self.places
        return [
            pltpu.SemaphoreType.DMA((g, n)),
            pltpu.SemaphoreType.DMA((g, n)),
            pltpu.SemaphoreType.DMA((2,)),
            pltpu.SemaphoreType.DMA((2, g, n)),
            pltpu.SemaphoreType.DMA((g, n + 1)),
            pltpu.SemaphoreType.DMA((6,)),
        ]

    def bind(self, core_land, acc, land, stage, extra, sems):
        self.core_land, self.acc, self.land = core_land, acc, land
        self.stage, self.extra = stage, extra
        (
            self.core_send,
            self.core_recv,
            self.stage_sem,
            self.line_send,
            self.line_recv,
            self.local_sem,
        ) = sems
        self.me = lax.axis_index("dp")
        self.place = self.me // 2
        self.core = self.me % 2
        self.other = self.me + 1 - 2 * self.core
        self.before = []
        return self

    def signal(self, sem):
        pl.semaphore_signal(sem, inc=1, device_id={"dp": self.other}, device_id_type=MESH)

        @pl.when(self.place > 0)
        def _():
            pl.semaphore_signal(sem, inc=1, device_id={"dp": self.me - 2}, device_id_type=MESH)

        @pl.when(self.place < self.places - 1)
        def _():
            pl.semaphore_signal(sem, inc=1, device_id={"dp": self.me + 2}, device_id_type=MESH)

    def peers(self):
        ends = (self.places - 1 - self.place) // (self.places - 1) + self.place // (self.places - 1)
        return 3 - ends

    def core_copy(self, group, i, slot):
        return pltpu.make_async_remote_copy(
            src_ref=self.stage.at[slot],
            dst_ref=self.core_land.at[group, i],
            send_sem=self.core_send.at[group, i],
            recv_sem=self.core_recv.at[group, i],
            device_id={"dp": self.other},
            device_id_type=MESH,
        )

    def fill(self, group, tile_of):
        def away(i, carry):
            slot = lax.rem(i, 2)

            @pl.when(i >= 2)
            def _():
                self.core_copy(group, i - 2, slot).wait_send()

            self.stage[slot] = tile_of(2 * i + 1 - self.core).astype(LOW)
            self.core_copy(group, i, slot).start()
            return carry

        lax.fori_loop(0, self.places, away, 0)
        for i in range(max(0, self.places - 2), self.places):
            self.core_copy(group, i, i % 2).wait_send()

        def store(i, slot):
            return pltpu.make_async_copy(
                self.stage.at[slot], self.acc.at[group, i], self.stage_sem.at[slot]
            )

        def home(i, carry):
            slot = lax.rem(i, 2)
            landed = self.core_land.at[group, i]
            pltpu.make_async_copy(landed, landed, self.core_recv.at[group, i]).wait()
            fetch = pltpu.make_async_copy(landed, self.extra, self.local_sem.at[0])
            fetch.start()

            @pl.when(i >= 2)
            def _():
                store(i - 2, slot).wait()

            value = tile_of(2 * i + self.core)
            fetch.wait()
            self.stage[slot] = (value + self.extra[...].astype(F32)).astype(LOW)
            store(i, slot).start()
            return carry

        lax.fori_loop(0, self.places, home, 0)
        for i in range(max(0, self.places - 2), self.places):
            store(i, i % 2).wait()
        self.ends(group, "start")

    def line_copy(self, group, way, j, source):
        if way == 0:
            slot, to = j, self.me + 2
        else:
            final = 1 - jnp.minimum(self.place - 1 - j, 1)
            slot, to = j + final * (self.places - j), self.me - 2
        return pltpu.make_async_remote_copy(
            src_ref=source,
            dst_ref=self.land.at[group, slot],
            send_sem=self.line_send.at[way, group, j],
            recv_sem=self.line_recv.at[group, slot],
            device_id={"dp": to},
            device_id_type=MESH,
        )

    def ends(self, group, act):
        n = self.places

        @pl.when(self.place == 0)
        def _():
            for j in range(n - 1, 0, -1):
                copy = self.line_copy(group, 0, j, self.acc.at[group, j])
                copy.start() if act == "start" else copy.wait_send()

        @pl.when(self.place == n - 1)
        def _():
            for j in range(n - 1):
                copy = self.line_copy(group, 1, j, self.acc.at[group, j])
                copy.start() if act == "start" else copy.wait_send()

    def landed(self, group, slot):
        ref = self.land.at[group, slot]
        pltpu.make_async_copy(ref, ref, self.line_recv.at[group, slot]).wait()
        return ref

    def on_way(self, step, way):
        far = self.place if way == 0 else self.places - 1 - self.place
        index = self.places - 1 - step + self.place if way == 0 else step - far
        return jnp.logical_and(far >= 1, far <= step), index

    def settle(self, lines):
        for group, step in self.before:
            for way in range(2):
                active, j = self.on_way(step, way)

                @pl.when(active)
                def _(way=way, j=j, group=group):
                    self.line_copy(group, way, j, lines.at[way, 0]).wait_send()

        self.before = []

    def tick(self, group, step, lines):
        self.settle(lines)
        for way in range(2):
            active, j = self.on_way(step, way)

            @pl.when(active)
            def _(way=way, j=j):
                here = pltpu.make_async_copy(
                    self.acc.at[group, j], lines.at[way, 0], self.local_sem.at[2 * way]
                )
                here.start()
                there = pltpu.make_async_copy(
                    self.landed(group, j), lines.at[way, 1], self.local_sem.at[2 * way + 1]
                )
                there.start()
                here.wait()
                there.wait()
                lines[way, 0] = (
                    lines[way, 0].astype(F32) + lines[way, 1].astype(F32)
                ).astype(LOW)
                self.line_copy(group, way, j, lines.at[way, 0]).start()

        self.before = [(group, step)]

    def finish(self, group, lines, total):
        self.settle(lines)
        n = self.places
        here = pltpu.make_async_copy(
            self.acc.at[group, self.place], lines.at[0, 0], self.local_sem.at[0]
        )
        here.start()
        here.wait()
        total[...] = lines[0, 0].astype(F32)

        @pl.when(self.place > 0)
        def _():
            there = pltpu.make_async_copy(
                self.landed(group, self.place), lines.at[0, 1], self.local_sem.at[1]
            )
            there.start()
            there.wait()
            total[...] += lines[0, 1].astype(F32)

        @pl.when(self.place < n - 1)
        def _():
            there = pltpu.make_async_copy(
                self.landed(group, n), lines.at[1, 1], self.local_sem.at[2]
            )
            there.start()
            there.wait()
            total[...] += lines[1, 1].astype(F32)


def head_back(grad, raw, cosine, sine, gain):
    width = raw.shape[-1]
    turned = grad * cosine - pltpu.roll(grad, width // 2, 1) * sine
    scale = lax.rsqrt(jnp.mean(raw * raw, axis=-1, keepdims=True) + NORM_EPS)
    unit = raw * scale
    gain_sum = jnp.sum(turned * unit, axis=0, keepdims=True)
    inner = turned * gain
    return scale * (inner - unit * jnp.mean(inner * unit, axis=-1, keepdims=True)), gain_sum


def rows_back(d_unit, rows, scale):
    unit = rows * scale
    return scale * (d_unit - unit * jnp.mean(d_unit * unit, axis=-1, keepdims=True))


def inverse_norm(rows):
    return lax.rsqrt(jnp.mean(rows * rows, axis=-1, keepdims=True) + NORM_EPS)


def back_kernel(plan, *refs):
    swap3, swap2, swap4, line, sizes = plan
    q_block, head_width, pairs, group_size = sizes
    refs = iter(refs)

    def take(count):
        return [next(refs) for _ in range(count)]

    (
        length_ref,
        hidden_hbm,
        grad_hbm,
        wg_hbm,
        wu_hbm,
        wd_hbm,
        resid_ref,
        post_gain_ref,
        in_gain_ref,
        query_gain_ref,
        key_gain_ref,
        valid_ref,
        lse_ref,
        x_hbm,
        q_hbm,
        k_hbm,
        v_hbm,
        heads_hbm,
        normed_hbm,
        q_raw_hbm,
        k_raw_hbm,
        cos_hbm,
        sin_hbm,
        w_out_hbm,
        w_query_hbm,
        w_key_hbm,
        w_value_hbm,
    ) = take(27)
    (
        output,
        in_grad,
        post_part,
        in_part,
        query_part,
        key_part,
        down_out,
        gate_out,
        up_out,
        query_out,
        key_out,
        value_out,
        proj_out,
        core_land,
        acc,
        land,
    ) = take(16)
    hidden, grad, act, dg, du, part, low, d_resid, stage, extra, recv = take(11)
    in_sems, own_sems, final_sems, free_sem = take(4)
    sems3, sems2, sems4 = take(4), take(4), take(4)
    swap3.bind(part, recv, low, sems3)
    swap2.bind(part, recv, output, sems2, own=part)
    swap4.bind(grad, recv, in_grad, sems4, own=grad)
    line.bind(core_land, acc, land, stage, extra, take(6))

    units = act.shape[1]
    width = swap3.width
    rows_all, heads_width = q_hbm.shape
    keys_width = k_hbm.shape[1]
    unit_tile = 512 if units % 512 == 0 else 256

    def load(i, src, dst):
        return pltpu.make_async_copy(src, dst, in_sems.at[i])

    def weights(wg, wu, wd):
        loads = [
            load(0, hidden_hbm, hidden),
            load(1, wg_hbm, wg),
            load(2, wu_hbm, wu),
            load(3, grad_hbm, grad),
            load(4, wd_hbm, wd),
        ]
        for item in loads:
            item.start()
        barrier = pltpu.get_barrier_semaphore()
        swap3.signal(barrier)
        line.signal(barrier)
        pl.semaphore_wait(barrier, swap3.bits + line.peers())
        for item in loads:
            item.wait()
        order = swap3.order()
        for spot, r in enumerate(order):
            rows = swap3.rows(r)

            def unit_step(cols):
                gate = dot_nn(hidden[rows, :], wg[:, cols])
                up = dot_nn(hidden[rows, :], wu[:, cols])
                d_act = dot_nt(grad[rows, :], wd[cols, :])
                sig = jax.nn.sigmoid(gate)
                silu = gate * sig
                act[rows, cols] = (silu * up).astype(LOW)
                dg[rows, cols] = (d_act * up * sig * (1.0 + gate * (1.0 - sig))).astype(LOW)
                du[rows, cols] = (d_act * silu).astype(LOW)

            tiled(units, unit_tile, unit_step)

            def back_step(cols):
                part[rows, cols] = (
                    dot_nt(dg[rows, :], wg[cols, :]) + dot_nt(du[rows, :], wu[cols, :])
                ).astype(LOW)

            tiled(width, 512, back_step)
            if r:
                swap3.scatter_start(r)
            if spot == len(order) - 2:
                for half, s in swap3.forwards():
                    swap3.scatter_forward(half, s)

        def tile_cols(i):
            return pl.ds(pl.multiple_of(i * line.tile, line.tile), line.tile)

        line.fill(0, lambda i: dot_tn(grad[:, tile_cols(i)], act[...]))
        for sub in range(SUBS):
            local = pl.ds(sub * swap3.sub, swap3.sub)
            d_hidden = swap3.scatter_result(sub)
            resid = resid_ref[local, :]
            c = inverse_norm(resid)
            partial = jnp.sum(d_hidden * (resid * c), axis=0, keepdims=True)
            if sub == 0:
                post_part[...] = partial
            else:
                post_part[...] += partial
            value = grad[swap3.rows(0, sub), :].astype(F32) + rows_back(
                d_hidden * post_gain_ref[...], resid, c
            )
            d_resid[local, :] = value
            low[swap3.rows(0, sub), :] = value.astype(LOW)
            swap3.gather_start(sub)
        swap3.scatter_end()
        early = swap3.gather_early()
        for spot, r in enumerate(order):
            rows = swap3.rows(r)

            def mix_step(cols):
                part[rows, cols] = dot_nn(act[rows, :], wd[:, cols]).astype(LOW)

            tiled(width, 512, mix_step)
            if spot == 1:
                for item in early[: len(early) // 2]:
                    swap3.gather_pass(*item)
        for item in early[len(early) // 2 :]:
            swap3.gather_pass(*item)

    def rest(lines, total, turned, w_out, w_query, w_key, w_value, q_raw, k_raw, cosine, sine, dk, dv):
        def tile_cols(i):
            return pl.ds(pl.multiple_of(i * line.tile, line.tile), line.tile)

        loads = [
            load(5, w_out_hbm, w_out),
            load(6, w_query_hbm, w_query),
            load(7, w_key_hbm, w_key),
            load(8, w_value_hbm, w_value),
            load(9, q_raw_hbm, q_raw),
            load(10, k_raw_hbm, k_raw),
            load(11, cos_hbm, cosine),
            load(12, sin_hbm, sine),
        ]
        q_at = pl.ds(0, heads_width)
        k_at = pl.ds(heads_width, keys_width)
        v_at = pl.ds(heads_width + keys_width, keys_width)
        o_at = pl.ds(heads_width + 2 * keys_width, heads_width)
        loads += [
            load(0, q_hbm, act.at[:, q_at]),
            load(1, k_hbm, act.at[:, k_at]),
            load(2, v_hbm, act.at[:, v_at]),
            load(3, heads_hbm, act.at[:, o_at]),
        ]
        for item in loads:
            item.start()
        line.fill(1, lambda i: dot_tn(hidden[:, tile_cols(i)], dg[...]))
        line.tick(0, 1, lines)
        line.fill(2, lambda i: dot_tn(hidden[:, tile_cols(i)], du[...]))
        normed_load = load(4, normed_hbm, hidden)
        normed_load.start()
        for item in swap3.gather_late():
            swap3.gather_pass(*item)
        swap3.gather_end()
        order = swap2.order()
        for r in order[:-1]:
            swap2.scatter_start(r)
        for item in loads:
            item.wait()

        def d_head_step(rows):
            dg[rows, o_at] = dot_nt(low[rows, :], w_out[...]).astype(LOW)

        tiled(rows_all, 256, d_head_step)
        x_load = load(5, x_hbm, w_out.at[pl.ds(0, swap4.block)])
        x_load.start()
        line.tick(0, 2, lines)
        length = length_ref[0]
        score_scale = head_width ** (-0.5)
        lanes = group_size * q_block

        def stacked(ref, rows, base):
            return jnp.concatenate(
                [
                    ref[rows, pl.ds(base + i * head_width, head_width)]
                    for i in range(group_size)
                ],
                axis=0,
            )

        def pair(c):
            first = c * group_size * head_width
            for block in range(rows_all // q_block):
                rows = pl.ds(block * q_block, q_block)
                end = (block + 1) * q_block
                q2 = stacked(act, rows, first)
                do2 = stacked(dg, rows, heads_width + 2 * keys_width + first)
                keys = act[0:end, pl.ds(heads_width + c * head_width, head_width)]
                values = act[0:end, pl.ds(heads_width + keys_width + c * head_width, head_width)]
                scores = dot_nt(keys, q2) * score_scale
                k_pos = lax.broadcasted_iota(jnp.int32, (end, lanes), 0)
                q_pos = block * q_block + lax.rem(
                    lax.broadcasted_iota(jnp.int32, (1, lanes), 1), q_block
                )
                allowed = k_pos < jnp.minimum(q_pos + 1, length)
                probs = jnp.where(allowed, jnp.exp(scores - lse_ref[c, block]), 0.0)
                d_probs = dot_nt(values, do2)
                delta = jnp.sum(probs * d_probs, axis=0, keepdims=True)
                d_scores = (probs * (d_probs - delta)).astype(LOW)
                d_value = dot_nn(probs.astype(LOW), do2)
                d_key = dot_nn(d_scores, q2)
                if block:
                    dv[0 : end - q_block, :] += d_value[: end - q_block]
                    dk[0 : end - q_block, :] += d_key[: end - q_block]
                dv[end - q_block : end, :] = d_value[end - q_block :]
                dk[end - q_block : end, :] = d_key[end - q_block :]
                d_query = (dot_tn(keys, d_scores) * score_scale).T
                for i in range(group_size):
                    at = pl.ds(first + i * head_width, head_width)
                    value, gain_sum = head_back(
                        d_query[i * q_block : (i + 1) * q_block],
                        q_raw[rows, at],
                        cosine[rows, :],
                        sine[rows, :],
                        query_gain_ref[...],
                    )
                    dg[rows, at] = value.astype(LOW)
                    if c == 0 and block == 0 and i == 0:
                        query_part[...] = gain_sum
                    else:
                        query_part[...] += gain_sum
            value, gain_sum = head_back(
                dk[...] * score_scale,
                k_raw[:, pl.ds(c * head_width, head_width)],
                cosine[...],
                sine[...],
                key_gain_ref[...],
            )
            dg[:, pl.ds(heads_width + c * head_width, head_width)] = value.astype(LOW)
            if c == 0:
                key_part[...] = gain_sum
            else:
                key_part[...] += gain_sum
            dg[:, pl.ds(heads_width + keys_width + c * head_width, head_width)] = dv[...].astype(LOW)

        for c in range(pairs):
            pair(c)
            if c == 0:
                store_group(0, lines, total, turned)
        for half, r in swap2.forwards():
            swap2.scatter_forward(half, r)
        for r in order:
            rows = swap4.rows(r)

            def normed_step(cols):
                grad[rows, cols] = (
                    dot_nt(dg[rows, q_at], w_query[cols, :])
                    + dot_nt(dg[rows, k_at], w_key[cols, :])
                    + dot_nt(dg[rows, v_at], w_value[cols, :])
                ).astype(LOW)

            tiled(width, 512, normed_step)
        for sub in range(SUBS):
            local = pl.ds(sub * swap2.sub, swap2.sub)
            mixed = swap2.scatter_result(sub)
            part[swap2.rows(0, sub), :] = (
                valid_ref[local, :] * (resid_ref[local, :] + mixed)
            ).astype(LOW)
        swap2.signal(free_sem)
        pl.semaphore_wait(free_sem, swap2.bits)
        for r in order[:-1]:
            swap4.scatter_start(r)
        own2 = [
            pltpu.make_async_copy(
                part.at[swap2.rows(0, sub), :], output.at[swap2.rows(0, sub), :], own_sems.at[0, sub]
            )
            for sub in range(SUBS)
        ]
        for item in own2:
            item.start()
        normed_load.wait()
        line.tick(1, 1, lines)

        def last_tile(i):
            cols = tile_cols(i)
            return jnp.concatenate(
                [
                    dot_tn(hidden[:, cols], dg[:, pl.ds(0, heads_width + 2 * keys_width)]),
                    dot_tn(low[:, cols], act[:, o_at]),
                ],
                axis=1,
            )

        line.fill(3, last_tile)
        for half, r in swap4.forwards():
            swap4.scatter_forward(half, r)
        line.tick(1, 2, lines)
        own4 = []
        x_load.wait()
        for sub in range(SUBS):
            local = pl.ds(sub * swap4.sub, swap4.sub)
            d_normed = swap4.scatter_result(sub)
            x = w_out[local, :].astype(F32)
            c = inverse_norm(x)
            partial = jnp.sum(d_normed * (x * c), axis=0, keepdims=True)
            if sub == 0:
                in_part[...] = partial
            else:
                in_part[...] += partial
            value = d_resid[local, :] + rows_back(d_normed * in_gain_ref[...], x, c)
            grad[swap4.rows(0, sub), :] = value.astype(LOW)
            swap4.gather_start(sub)
            own4.append(
                pltpu.make_async_copy(
                    grad.at[swap4.rows(0, sub), :],
                    in_grad.at[swap4.rows(0, sub), :],
                    own_sems.at[1, sub],
                )
            )
            own4[-1].start()
        for sub in range(SUBS):
            swap2.gather_start(sub)
        store_group(1, lines, total, turned)
        for item in swap4.gather_early():
            swap4.gather_pass(*item)
        for item in swap2.gather_early():
            swap2.gather_pass(*item)
        line.tick(2, 1, lines)
        line.tick(2, 2, lines)
        store_group(2, lines, total, turned)
        for swap in (swap4, swap2):
            for item in swap.gather_late():
                swap.gather_pass(*item)
        for step in range(1, line.places - 1):
            line.tick(3, step, lines)
        store_group(3, lines, total, turned)
        for item in own2 + own4:
            item.wait()
        for swap in (swap2, swap4):
            swap.scatter_end()
            swap.gather_end()
        for group in range(line.groups):
            line.ends(group, "wait")

    def store_group(group, lines, total, turned):
        line.finish(group, lines, total)
        proj = heads_width + 2 * keys_width
        if group == 0:
            turned[...] = total[...].T
            copies = [(turned, down_out)]
        elif group == 3:
            turned[0:heads_width, :] = total[:, pl.ds(proj, heads_width)].T
            copies = [
                (total.at[:, pl.ds(0, heads_width)], query_out),
                (total.at[:, pl.ds(heads_width, keys_width)], key_out),
                (total.at[:, pl.ds(heads_width + keys_width, keys_width)], value_out),
                (turned.at[pl.ds(0, heads_width), :], proj_out),
            ]
        else:
            copies = [(total, (gate_out, up_out)[group - 1])]
        copies = [
            pltpu.make_async_copy(src, dst, final_sems.at[i])
            for i, (src, dst) in enumerate(copies)
        ]
        for copy in copies:
            copy.start()
        for copy in copies:
            copy.wait()

    pl.run_scoped(
        weights,
        pltpu.VMEM((width, units), LOW),
        pltpu.VMEM((width, units), LOW),
        pltpu.VMEM((units, width), LOW),
    )
    pl.run_scoped(
        rest,
        pltpu.VMEM((2, 2, line.tile, line.width), LOW),
        pltpu.VMEM((line.tile, line.width), F32),
        pltpu.VMEM((line.width, line.tile), F32),
        pltpu.VMEM((heads_width, width), LOW),
        pltpu.VMEM((width, heads_width), LOW),
        pltpu.VMEM((width, keys_width), LOW),
        pltpu.VMEM((width, keys_width), LOW),
        pltpu.VMEM((rows_all, heads_width), F32),
        pltpu.VMEM((rows_all, keys_width), F32),
        pltpu.VMEM((rows_all, head_width), F32),
        pltpu.VMEM((rows_all, head_width), F32),
        pltpu.VMEM((rows_all, head_width), F32),
        pltpu.VMEM((rows_all, head_width), F32),
    )


def back(
    counts, sizes, length, hidden, d_out_low, feed_weights, resid, gains, valid_rows, x_rows, lse,
    attended, tables, attn_weights,
):
    tensor_count, dp_count = counts
    rows, width = hidden.shape
    units = feed_weights[0].shape[1]
    heads_width = attn_weights[0].shape[0]
    keys_width = attn_weights[2].shape[1]
    head_width = sizes[1]
    tile = width // dp_count
    swaps = [Swap(tensor_count, rows, width) for _ in range(3)]
    line = Line(dp_count, 4, tile, units)
    vec = jax.ShapeDtypeStruct((1, width), F32)
    head_vec = jax.ShapeDtypeStruct((1, head_width), F32)
    out_shape = (
        jax.ShapeDtypeStruct((rows, width), LOW),
        jax.ShapeDtypeStruct((rows, width), LOW),
        vec,
        vec,
        head_vec,
        head_vec,
        jax.ShapeDtypeStruct((units, tile), F32),
        jax.ShapeDtypeStruct((tile, units), F32),
        jax.ShapeDtypeStruct((tile, units), F32),
        jax.ShapeDtypeStruct((tile, heads_width), F32),
        jax.ShapeDtypeStruct((tile, keys_width), F32),
        jax.ShapeDtypeStruct((tile, keys_width), F32),
        jax.ShapeDtypeStruct((heads_width, tile), F32),
        *line.outputs(),
    )
    wide = pltpu.VMEM((rows, width), LOW)
    inner = pltpu.VMEM((rows, units), LOW)
    sems = [item for swap in swaps for item in swap.semaphores()]
    return pl.pallas_call(
        functools.partial(back_kernel, (*swaps, line, sizes)),
        out_shape=out_shape,
        in_specs=[pl.BlockSpec(memory_space=pltpu.SMEM)]
        + [any_spec()] * 5
        + [vmem_spec()] * 7
        + [any_spec()] * 14,
        out_specs=(any_spec(),) * 2 + (vmem_spec(),) * 4 + (any_spec(),) * 10,
        scratch_shapes=[
            wide,
            wide,
            inner,
            inner,
            inner,
            wide,
            wide,
            pltpu.VMEM((swaps[0].block, width), F32),
            pltpu.VMEM((2, tile, units), LOW),
            pltpu.VMEM((tile, units), LOW),
            swaps[0].landing(),
            pltpu.SemaphoreType.DMA((13,)),
            pltpu.SemaphoreType.DMA((2, SUBS)),
            pltpu.SemaphoreType.DMA((4,)),
            pltpu.SemaphoreType.REGULAR,
            *sems,
            *line.semaphores(),
        ],
        compiler_params=kernel_params(1),
        name="back",
    )(
        length,
        hidden,
        d_out_low,
        *feed_weights,
        resid,
        *gains,
        valid_rows,
        lse,
        x_rows,
        *attended,
        *tables,
        *attn_weights,
    )[:13]


def rope_tables(head_width, row_count):
    half_width = head_width // 2
    inv_freq = ROPE_BASE ** (-2.0 * jnp.arange(half_width, dtype=F32) / head_width)
    angles = jnp.arange(row_count, dtype=F32)[:, None] * inv_freq[None, :]
    cosine, sine = jnp.cos(angles), jnp.sin(angles)
    return jnp.concatenate([cosine, cosine], axis=1), jnp.concatenate([-sine, sine], axis=1)


def on_device(
    tensor_count,
    dp_count,
    tokens,
    lengths,
    in_gain,
    w_query,
    w_key,
    w_value,
    query_gain,
    key_gain,
    w_out,
    post_gain,
    w_gate,
    w_up,
    w_down,
    out_grad,
):
    row_count = tokens.shape[0]
    slot_len = row_count
    head_width = query_gain.shape[0]
    q_heads = w_query.shape[1] // head_width
    kv_heads = w_key.shape[1] // head_width
    group_size = q_heads // kv_heads
    block_len = min(512, slot_len)
    block_count = slot_len // block_len
    q_block = 128
    share = row_count // tensor_count
    score_scale = head_width ** (-0.5)
    length = lengths[0]
    tensor_me = lax.axis_index("tensor")

    def own_rows(matrix):
        return lax.dynamic_slice_in_dim(matrix, tensor_me * share, share, axis=0)

    position = jnp.arange(row_count, dtype=jnp.int32)
    valid_rows = (position < length).astype(F32)[:, None]
    inputs = tokens.astype(F32)
    normed = (unit_rows(inputs) * in_gain).astype(LOW)
    q_raw = dot_nn(normed, w_query)
    k_raw = dot_nn(normed, w_key)
    values_low = dot_nn(normed, w_value).astype(LOW)
    value_heads = values_low.reshape(row_count, kv_heads, head_width)
    tables = rope_tables(head_width, slot_len)

    def prepare(raw, heads, gain):
        normed_heads = norm_rows(raw.reshape(row_count, heads, head_width), gain)
        half = head_width // 2
        other = jnp.concatenate([normed_heads[..., half:], normed_heads[..., :half]], axis=-1)
        turned = normed_heads * tables[0][:, None] + other * tables[1][:, None]
        return turned.astype(LOW)

    query_low = prepare(q_raw, q_heads, query_gain)
    keys_low = prepare(k_raw, kv_heads, key_gain)
    query_groups = query_low.reshape(row_count, kv_heads, group_size, head_width)
    log_totals = []
    heads = []
    for block in range(block_count):
        rows = slice(block * block_len, (block + 1) * block_len)
        key_end = (block + 1) * block_len
        scores = masked_scores(
            query_groups[rows], keys_low[:key_end], length, block * block_len, score_scale
        )
        row_peak = jnp.max(scores, axis=-1, keepdims=True)
        exponent = jnp.exp(scores - row_peak)
        row_total = jnp.sum(exponent, axis=-1, keepdims=True)
        probs_low = (exponent / row_total).astype(LOW)
        head_blk = (
            jnp.einsum("cgqk,kcd->qcgd", probs_low, value_heads[:key_end], preferred_element_type=F32)
            .reshape(block_len, q_heads * head_width)
            .astype(LOW)
        )
        log_totals.append((row_peak + jnp.log(row_total))[..., 0])
        heads.append(head_blk)
    heads_low = jnp.concatenate(heads, axis=0)
    lse = (
        jnp.concatenate(log_totals, axis=2)
        .reshape(kv_heads, group_size, row_count // q_block, q_block)
        .transpose(0, 2, 1, 3)
        .reshape(kv_heads, row_count // q_block, 1, group_size * q_block)
    )
    resid, hidden = out_sum(tensor_count, heads_low, w_out, own_rows(tokens), post_gain)
    d_out_low = (out_grad.astype(F32) * valid_rows).astype(LOW)
    (
        output,
        in_grad,
        post_part,
        in_part,
        query_part,
        key_part,
        grad_down,
        grad_gate,
        grad_up,
        grad_query,
        grad_key,
        grad_value,
        grad_out,
    ) = back(
        (tensor_count, dp_count),
        (q_block, head_width, kv_heads, group_size),
        lengths,
        hidden,
        d_out_low,
        (w_gate, w_up, w_down),
        resid,
        (post_gain[None], in_gain[None], query_gain[None], key_gain[None]),
        own_rows(valid_rows),
        own_rows(tokens),
        lse,
        (
            query_low.reshape(row_count, -1),
            keys_low.reshape(row_count, -1),
            values_low,
            heads_low,
            normed,
            q_raw,
            k_raw,
        ),
        tables,
        (w_out, w_query, w_key, w_value),
    )
    grad_in_gain, grad_query_gain, grad_key_gain, grad_post_gain = lax.psum(
        (in_part[0], query_part[0], key_part[0], post_part[0]), ("dp", "tensor")
    )
    return (
        output,
        in_grad,
        grad_in_gain,
        grad_query,
        grad_key,
        grad_value,
        grad_query_gain,
        grad_key_gain,
        grad_out,
        grad_post_gain,
        grad_gate,
        grad_up,
        grad_down,
    )


def solution(mesh):
    tensor_count, dp_count = mesh.shape["tensor"], mesh.shape["dp"]

    def layer(*args):
        return on_device(tensor_count, dp_count, *args)

    return jax.shard_map(
        layer,
        mesh=mesh,
        in_specs=(
            P("dp", None),
            P("dp"),
            P(),
            P(None, "tensor"),
            P(None, "tensor"),
            P(None, "tensor"),
            P(),
            P(),
            P("tensor", None),
            P(),
            P(None, "tensor"),
            P(None, "tensor"),
            P("tensor", None),
            P("dp", None),
        ),
        out_specs=(
            P("dp", None),
            P("dp", None),
            P(),
            P("dp", "tensor"),
            P("dp", "tensor"),
            P("dp", "tensor"),
            P(),
            P(),
            P("tensor", "dp"),
            P(),
            P("dp", "tensor"),
            P("dp", "tensor"),
            P("tensor", "dp"),
        ),
        check_vma=False,
    )
```

```python
import functools

import jax
import jax.numpy as jnp
import numpy as np
from jax import lax
from jax.experimental import pallas as pl
from jax.experimental.pallas import tpu as pltpu
from jax.sharding import PartitionSpec as P

NORM_EPS = 1e-06
ROPE_BASE = 1000000.0
MASK_FILL = -1e30
LOW = jnp.bfloat16
F32 = jnp.float32
MESH = pl.DeviceIdType.MESH
VMEM_BYTES = 63 * 1024 * 1024
CHUNK = 256
KEYS = 256


def unit_rows(matrix):
    return matrix * lax.rsqrt(jnp.mean(matrix * matrix, axis=-1, keepdims=True) + NORM_EPS)


def dot_nn(left, right):
    return jnp.dot(left, right, preferred_element_type=F32)


def dot_tn(left, right):
    return lax.dot_general(left, right, (((0,), (0,)), ((), ())), preferred_element_type=F32)


def dot_nt(left, right):
    return lax.dot_general(left, right, (((1,), (1,)), ((), ())), preferred_element_type=F32)


class Swap:
    def __init__(self, count, rows, width):
        self.count, self.width = count, width
        self.bits = count.bit_length() - 1
        self.chunk = min(CHUNK, rows)
        self.chunks = rows // self.chunk
        self.block = self.chunk // count
        self.half = width // 2
        self.orders = [list(range(self.bits)), list(range(self.bits))[::-1]]
        self.slots = []
        for order in self.orders:
            slot = {}
            for step in range(self.bits):
                for r in range(count):
                    if not any(r >> b & 1 for b in order[: step + 1]):
                        slot[step, r] = len(slot)
            self.slots.append(slot)

    def landing(self):
        return pltpu.VMEM((2, self.count - 1, self.chunks * self.block, self.half), LOW)

    def semaphores(self):
        n, c = self.count, self.chunks
        return [
            pltpu.SemaphoreType.DMA((2, n, c)),
            pltpu.SemaphoreType.DMA((2, n, c)),
            pltpu.SemaphoreType.DMA((2, n * self.bits, c)),
            pltpu.SemaphoreType.DMA((2, n, c)),
        ]

    def bind(self, part, recv, dest, sems, own=None):
        self.part, self.recv, self.dest, self.sems = part, recv, dest, sems
        self.own = dest if own is None else own
        self.me = lax.axis_index("tensor")
        return self

    def near(self, bit):
        own = (self.me // 2**bit) % 2
        return self.me + (1 - 2 * own) * 2**bit

    def rows(self, r, c):
        owner = self.me
        for bit in range(self.bits):
            if r >> bit & 1:
                owner = owner + (1 - 2 * ((self.me // 2**bit) % 2)) * 2**bit
        return pl.ds(pl.multiple_of(c * self.chunk + owner * self.block, self.block), self.block)

    def local(self, c):
        return pl.ds(c * self.block, self.block)

    def columns(self, half):
        return pl.ds(half * self.half, self.half)

    def signal(self, sem):
        for bit in range(self.bits):
            pl.semaphore_signal(
                sem, inc=1, device_id={"tensor": self.near(bit)}, device_id_type=MESH
            )

    def order(self):
        return sorted(range(1, self.count), key=lambda r: (-bin(r).count("1"), r))

    def first(self, half, r):
        return next(k for k, bit in enumerate(self.orders[half]) if r >> bit & 1)

    def scatter_copy(self, half, r, c):
        step = self.first(half, r)
        bit = self.orders[half][step]
        slot = self.slots[half][step, r ^ (1 << bit)]
        return pltpu.make_async_remote_copy(
            src_ref=self.part.at[self.rows(r, c), self.columns(half)],
            dst_ref=self.recv.at[half, slot, self.local(c)],
            send_sem=self.sems[0].at[half, r, c],
            recv_sem=self.sems[1].at[half, slot, c],
            device_id={"tensor": self.near(bit)},
            device_id_type=MESH,
        )

    def scatter_wait(self, half, step, r, c):
        slot = self.slots[half][step, r]
        ref = self.recv.at[half, slot, self.local(c)]
        pltpu.make_async_copy(ref, ref, self.sems[1].at[half, slot, c]).wait()
        return ref

    def scatter_start(self, c):
        for r in self.order():
            for half in range(2):
                if self.first(half, r) == 0:
                    self.scatter_copy(half, r, c).start()

    def scatter_forward(self, c):
        todo = [
            (self.first(half, r), half, r)
            for half in range(2)
            for r in range(1, self.count)
            if self.first(half, r) > 0
        ]
        for step, half, r in sorted(todo):
            where = self.rows(r, c), self.columns(half)
            total = self.part[where].astype(F32)
            for j in range(step):
                total = total + self.scatter_wait(half, j, r, c)[...].astype(F32)
            self.part[where] = total.astype(LOW)
            self.scatter_copy(half, r, c).start()

    def scatter_result(self, c):
        total = []
        for half in range(2):
            value = self.part[self.rows(0, c), self.columns(half)].astype(F32)
            for j in range(self.bits):
                value = value + self.scatter_wait(half, j, 0, c)[...].astype(F32)
            total.append(value)
        return jnp.concatenate(total, axis=1)

    def scatter_end(self, c):
        for half in range(2):
            for r in range(1, self.count):
                self.scatter_copy(half, r, c).wait_send()

    def last(self, half, r):
        order = self.orders[half][::-1]
        return max([-1] + [j for j, bit in enumerate(order) if r >> bit & 1])

    def gather_copy(self, half, r, step, c):
        bit = self.orders[half][::-1][step]
        where = self.rows(r, c), self.columns(half)
        return pltpu.make_async_remote_copy(
            src_ref=self.dest.at[where] if r else self.own.at[where],
            dst_ref=self.dest.at[where],
            send_sem=self.sems[2].at[half, r * self.bits + step, c],
            recv_sem=self.sems[3].at[half, r ^ (1 << bit), c],
            device_id={"tensor": self.near(bit)},
            device_id_type=MESH,
        )

    def gather_start(self, c):
        for step in range(self.bits):
            for half in range(2):
                self.gather_copy(half, 0, step, c).start()

    def gather_pass(self, c, late):
        todo = [
            (self.last(half, r), bin(r).count("1"), half, r)
            for half in range(2)
            for r in range(1, self.count)
        ]
        for step, _, half, r in sorted(todo):
            if (step == self.bits - 1) != late:
                continue
            ref = self.dest.at[self.rows(r, c), self.columns(half)]
            pltpu.make_async_copy(ref, ref, self.sems[3].at[half, r, c]).wait()
            for later in range(step + 1, self.bits):
                self.gather_copy(half, r, later, c).start()

    def gather_end(self, c):
        for half in range(2):
            for r in range(self.count):
                for step in range(self.last(half, r) + 1, self.bits):
                    self.gather_copy(half, r, step, c).wait_send()


class Line:
    def __init__(self, count, groups, tile, width):
        self.count, self.groups, self.tile, self.width = count, groups, tile, width
        self.places = count // 2

    def outputs(self):
        shape = (self.tile, self.width)
        return [
            jax.ShapeDtypeStruct((self.groups, self.places) + shape, LOW),
            jax.ShapeDtypeStruct((self.groups, self.places) + shape, LOW),
            jax.ShapeDtypeStruct((self.groups, self.places + 1) + shape, LOW),
        ]

    def semaphores(self):
        g, n = self.groups, self.places
        return [
            pltpu.SemaphoreType.DMA((g, n)),
            pltpu.SemaphoreType.DMA((g, n)),
            pltpu.SemaphoreType.DMA((2,)),
            pltpu.SemaphoreType.DMA((2, g, n)),
            pltpu.SemaphoreType.DMA((g, n + 1)),
            pltpu.SemaphoreType.DMA((6,)),
        ]

    def bind(self, core_land, acc, land, stage, extra, sems):
        self.core_land, self.acc, self.land = core_land, acc, land
        self.stage, self.extra = stage, extra
        (
            self.core_send,
            self.core_recv,
            self.stage_sem,
            self.line_send,
            self.line_recv,
            self.local_sem,
        ) = sems
        self.me = lax.axis_index("dp")
        self.place = self.me // 2
        self.core = self.me % 2
        self.other = self.me + 1 - 2 * self.core
        self.before = []
        return self

    def signal(self, sem):
        @pl.when(self.place > 0)
        def _():
            pl.semaphore_signal(sem, inc=1, device_id={"dp": self.me - 2}, device_id_type=MESH)

        @pl.when(self.place < self.places - 1)
        def _():
            pl.semaphore_signal(sem, inc=1, device_id={"dp": self.me + 2}, device_id_type=MESH)

    def peers(self):
        ends = (self.places - 1 - self.place) // (self.places - 1) + self.place // (self.places - 1)
        return 2 - ends

    def core_copy(self, group, i, slot):
        return pltpu.make_async_remote_copy(
            src_ref=self.stage.at[slot],
            dst_ref=self.core_land.at[group, i],
            send_sem=self.core_send.at[group, i],
            recv_sem=self.core_recv.at[group, i],
            device_id={"dp": self.other},
            device_id_type=MESH,
        )

    def fill(self, group, tile_of):
        def away(i, carry):
            slot = lax.rem(i, 2)

            @pl.when(i >= 2)
            def _():
                self.core_copy(group, i - 2, slot).wait_send()

            for cols, value in tile_of(2 * i + 1 - self.core):
                self.stage[slot, :, cols] = value.astype(LOW)
            self.core_copy(group, i, slot).start()
            return carry

        lax.fori_loop(0, self.places, away, 0)
        for i in range(max(0, self.places - 2), self.places):
            self.core_copy(group, i, i % 2).wait_send()

        def store(i, slot):
            return pltpu.make_async_copy(
                self.stage.at[slot], self.acc.at[group, i], self.stage_sem.at[slot]
            )

        def home(i, carry):
            slot = lax.rem(i, 2)
            landed = self.core_land.at[group, i]
            pltpu.make_async_copy(landed, landed, self.core_recv.at[group, i]).wait()
            fetch = pltpu.make_async_copy(landed, self.extra, self.local_sem.at[0])
            fetch.start()

            @pl.when(i >= 2)
            def _():
                store(i - 2, slot).wait()

            for spot, (cols, value) in enumerate(tile_of(2 * i + self.core)):
                if spot == 0:
                    fetch.wait()
                self.stage[slot, :, cols] = (value + self.extra[:, cols].astype(F32)).astype(LOW)
            store(i, slot).start()
            return carry

        lax.fori_loop(0, self.places, home, 0)
        for i in range(max(0, self.places - 2), self.places):
            store(i, i % 2).wait()
        self.ends(group, "start")

    def line_copy(self, group, way, j, source):
        if way == 0:
            slot, to = j, self.me + 2
        else:
            final = 1 - jnp.minimum(self.place - 1 - j, 1)
            slot, to = j + final * (self.places - j), self.me - 2
        return pltpu.make_async_remote_copy(
            src_ref=source,
            dst_ref=self.land.at[group, slot],
            send_sem=self.line_send.at[way, group, j],
            recv_sem=self.line_recv.at[group, slot],
            device_id={"dp": to},
            device_id_type=MESH,
        )

    def ends(self, group, act):
        n = self.places

        @pl.when(self.place == 0)
        def _():
            for j in range(n - 1, 0, -1):
                copy = self.line_copy(group, 0, j, self.acc.at[group, j])
                copy.start() if act == "start" else copy.wait_send()

        @pl.when(self.place == n - 1)
        def _():
            for j in range(n - 1):
                copy = self.line_copy(group, 1, j, self.acc.at[group, j])
                copy.start() if act == "start" else copy.wait_send()

    def landed(self, group, slot):
        ref = self.land.at[group, slot]
        pltpu.make_async_copy(ref, ref, self.line_recv.at[group, slot]).wait()
        return ref

    def on_way(self, step, way):
        far = self.place if way == 0 else self.places - 1 - self.place
        index = self.places - 1 - step + self.place if way == 0 else step - far
        return jnp.logical_and(far >= 1, far <= step), index

    def settle(self, lines):
        for group, step in self.before:
            for way in range(2):
                active, j = self.on_way(step, way)

                @pl.when(active)
                def _(way=way, j=j, group=group):
                    self.line_copy(group, way, j, lines.at[way, 0]).wait_send()

        self.before = []

    def tick(self, group, step, lines):
        self.settle(lines)
        for way in range(2):
            active, j = self.on_way(step, way)

            @pl.when(active)
            def _(way=way, j=j):
                here = pltpu.make_async_copy(
                    self.acc.at[group, j], lines.at[way, 0], self.local_sem.at[2 * way]
                )
                here.start()
                there = pltpu.make_async_copy(
                    self.landed(group, j), lines.at[way, 1], self.local_sem.at[2 * way + 1]
                )
                there.start()
                here.wait()
                there.wait()
                lines[way, 0] = (
                    lines[way, 0].astype(F32) + lines[way, 1].astype(F32)
                ).astype(LOW)
                self.line_copy(group, way, j, lines.at[way, 0]).start()

        self.before = [(group, step)]

    def finish(self, group, lines, total):
        self.settle(lines)
        n = self.places
        here = pltpu.make_async_copy(
            self.acc.at[group, self.place], lines.at[0, 0], self.local_sem.at[0]
        )
        here.start()
        here.wait()
        total[...] = lines[0, 0].astype(F32)

        @pl.when(self.place > 0)
        def _():
            there = pltpu.make_async_copy(
                self.landed(group, self.place), lines.at[0, 1], self.local_sem.at[1]
            )
            there.start()
            there.wait()
            total[...] += lines[0, 1].astype(F32)

        @pl.when(self.place < n - 1)
        def _():
            there = pltpu.make_async_copy(
                self.landed(group, n), lines.at[1, 1], self.local_sem.at[2]
            )
            there.start()
            there.wait()
            total[...] += lines[1, 1].astype(F32)


class Spread:
    def __init__(self, counts, length):
        tensor_count, dp_count = counts
        self.length = length
        self.steps = [("tensor", 2**b) for b in range(tensor_count.bit_length() - 1)]
        self.steps += [("dp", 2**b) for b in range(dp_count.bit_length() - 1)]

    def scratch(self):
        n = len(self.steps)
        return [
            pltpu.VMEM((n + 1, 1, self.length), F32),
            pltpu.VMEM((n, 1, self.length), F32),
            pltpu.SemaphoreType.DMA((n,)),
            pltpu.SemaphoreType.DMA((n,)),
        ]

    def bind(self, mine, land, send, recv):
        self.mine, self.land, self.send, self.recv = mine, land, send, recv
        return self

    def partner(self, step):
        axis, size = self.steps[step]
        me = lax.axis_index(axis)
        return {axis: me + (1 - 2 * ((me // size) % 2)) * size}

    def signal(self, sem):
        for step in range(len(self.steps)):
            pl.semaphore_signal(
                sem, inc=1, device_id=self.partner(step), device_id_type=MESH
            )

    def copy(self, step):
        return pltpu.make_async_remote_copy(
            src_ref=self.mine.at[step],
            dst_ref=self.land.at[step],
            send_sem=self.send.at[step],
            recv_sem=self.recv.at[step],
            device_id=self.partner(step),
            device_id_type=MESH,
        )

    def next(self, step):
        self.copy(step).wait()
        self.mine[step + 1] = self.mine[step] + self.land[step]
        if step + 1 < len(self.steps):
            self.copy(step + 1).start()


def tiled(total, size, body):
    count = total // size

    def step(i, carry):
        body(pl.ds(pl.multiple_of(i * size, size), size))
        return carry

    lax.fori_loop(0, count, step, 0)


def any_spec():
    return pl.BlockSpec(memory_space=pl.ANY)


def vmem_spec():
    return pl.BlockSpec(memory_space=pltpu.VMEM)


def kernel_params(identity):
    return pltpu.CompilerParams(
        collective_id=identity, has_side_effects=True, vmem_limit_bytes=VMEM_BYTES
    )


def head_forward(raw, cosine, sine, gain):
    width = raw.shape[-1]
    unit = raw * lax.rsqrt(jnp.mean(raw * raw, axis=-1, keepdims=True) + NORM_EPS) * gain
    return (unit * cosine + pltpu.roll(unit, width // 2, 1) * sine).astype(LOW)


def head_back(grad, raw, cosine, sine, gain):
    width = raw.shape[-1]
    turned = grad * cosine - pltpu.roll(grad, width // 2, 1) * sine
    scale = lax.rsqrt(jnp.mean(raw * raw, axis=-1, keepdims=True) + NORM_EPS)
    unit = raw * scale
    gain_sum = jnp.sum(turned * unit, axis=0, keepdims=True)
    inner = turned * gain
    return scale * (inner - unit * jnp.mean(inner * unit, axis=-1, keepdims=True)), gain_sum


def rows_back(d_unit, rows, scale):
    unit = rows * scale
    return scale * (d_unit - unit * jnp.mean(d_unit * unit, axis=-1, keepdims=True))


def inverse_norm(rows):
    return lax.rsqrt(jnp.mean(rows * rows, axis=-1, keepdims=True) + NORM_EPS)


def layer_kernel(plan, *refs):
    swap1, swap3, swap2, swap4, line, spread, sizes = plan
    q_block, head_width, pairs, group_size = sizes
    refs = iter(refs)

    def take(count):
        return [next(refs) for _ in range(count)]

    length_ref, in_gain_ref, post_gain_ref, query_gain_ref, key_gain_ref = take(5)
    tokens_hbm, grad_hbm, cos_hbm, sin_hbm = take(4)
    w_query_hbm, w_key_hbm, w_value_hbm, w_out_hbm = take(4)
    wg_hbm, wu_hbm, wd_hbm = take(3)
    output, in_grad, gains_out = take(3)
    down_out, gate_out, up_out, query_out, key_out, value_out, proj_out = take(7)
    core_land, acc, land, normed_hbm, heads_hbm, q_raw_hbm, k_raw_hbm, resid_hbm = take(8)
    hidden, grad, act, dg, du, part, low, resid, stage, extra, flip, recv = take(12)
    w_query, w_key, w_value, w_out, cosine, sine, lse = take(7)
    in_sems, token_sems, front_sems, own_sems, final_sems, free_sem = take(6)
    swap1.bind(part, recv, hidden, take(4))
    swap3.bind(part, recv, low, take(4))
    swap2.bind(part, recv, output, take(4), own=part)
    swap4.bind(grad, recv, in_grad, take(4), own=grad)
    line.bind(core_land, acc, land, stage, extra, take(6))
    spread.bind(*take(4))

    rows_all, units = act.shape
    width = swap1.width
    heads_width, keys_width = w_query.shape[1], w_key.shape[1]
    unit_tile = 256
    chunk, chunks = swap1.chunk, swap1.chunks
    score_scale = head_width ** (-0.5)
    lanes = group_size * q_block
    length = length_ref[0]
    post_part = spread.mine.at[0, :, pl.ds(0, width)]
    in_part = spread.mine.at[0, :, pl.ds(width, width)]
    query_part = spread.mine.at[0, :, pl.ds(2 * width, head_width)]
    key_part = spread.mine.at[0, :, pl.ds(2 * width + head_width, head_width)]
    q_at = pl.ds(0, heads_width)
    k_at = pl.ds(heads_width, keys_width)
    v_at = pl.ds(heads_width + keys_width, keys_width)
    o_at = pl.ds(heads_width + 2 * keys_width, heads_width)

    def head_at(base, i):
        return pl.ds(base.start + i * head_width, head_width)

    def load(i, src, dst):
        return pltpu.make_async_copy(src, dst, in_sems.at[i])

    def chunk_rows(c):
        return pl.ds(c * chunk, chunk)

    def valid(rows):
        return rows.start + lax.broadcasted_iota(jnp.int32, (rows.size, 1), 0) < length

    def stacked(ref, rows, base, c):
        return jnp.concatenate(
            [ref[rows, head_at(base, c * group_size + i)] for i in range(group_size)], axis=0
        )

    def allowed_of(block, start, stop):
        k_pos = start + lax.broadcasted_iota(jnp.int32, (stop - start, lanes), 0)
        q_pos = block * q_block + lax.rem(
            lax.broadcasted_iota(jnp.int32, (1, lanes), 1), q_block
        )
        return k_pos < jnp.minimum(q_pos + 1, length)

    def tile_cols(i):
        return pl.ds(pl.multiple_of(i * line.tile, line.tile), line.tile)

    def products(left, right, cuts):
        def tile_of(i):
            flip[...] = left[:, tile_cols(i)].T
            for start in range(*cuts):
                cols = pl.ds(start, cuts[2])
                yield cols, dot_nn(flip[...], right[:, cols])

        return tile_of

    def add_to(ref, value, first):
        if first:
            ref[...] = value
        else:
            ref[...] += value


    def front(wd, wg, wu, q_raw, k_raw):
        attn_loads = [
            load(0, w_query_hbm, w_query),
            load(1, w_key_hbm, w_key),
            load(2, w_value_hbm, w_value),
            load(3, cos_hbm, cosine),
            load(4, sin_hbm, sine),
            load(5, w_out_hbm, w_out),
        ]
        feed_loads = [
            load(6, wg_hbm, wg),
            load(7, wu_hbm, wu),
            load(8, grad_hbm, grad),
            load(9, wd_hbm, wd),
        ]
        token_loads = [
            pltpu.make_async_copy(
                tokens_hbm.at[chunk_rows(c)], low.at[chunk_rows(c)], token_sems.at[c]
            )
            for c in range(chunks)
        ]
        for item in token_loads[:1] + attn_loads + token_loads[1:] + feed_loads:
            item.start()
        barrier = pltpu.get_barrier_semaphore()
        spread.signal(barrier)
        line.signal(barrier)
        pl.semaphore_wait(barrier, len(spread.steps) + line.peers())

        def front_store(i, src, dst):
            return pltpu.make_async_copy(src, dst, front_sems.at[i])

        raw_stores = []

        def attend(c):
            rows = chunk_rows(c)
            token_loads[c].wait()

            def norm_step(local):
                at = pl.ds(c * chunk + local.start, local.size)
                x = low[at, :].astype(F32)
                hidden[at, :] = (unit_rows(x) * in_gain_ref[...]).astype(LOW)

            tiled(chunk, 32, norm_step)
            store = front_store(0, hidden.at[rows], normed_hbm.at[rows])
            store.start()
            if c == 0:
                for item in attn_loads:
                    item.wait()
            for item in raw_stores:
                item.wait()
            raw_stores.clear()
            q_raw[...] = dot_nn(hidden[rows, :], w_query[...])
            k_raw[...] = dot_nn(hidden[rows, :], w_key[...])
            du[rows, v_at] = dot_nn(hidden[rows, :], w_value[...]).astype(LOW)
            for raw, base, gain in ((q_raw, q_at, query_gain_ref), (k_raw, k_at, key_gain_ref)):
                for i in range(base.size // head_width):
                    du[rows, head_at(base, i)] = head_forward(
                        raw[:, pl.ds(i * head_width, head_width)],
                        cosine[rows, :],
                        sine[rows, :],
                        gain[...],
                    )
            raw_stores.append(front_store(1, q_raw, q_raw_hbm.at[rows]))
            raw_stores.append(front_store(2, k_raw, k_raw_hbm.at[rows]))
            for item in raw_stores:
                item.start()
            for pair in range(pairs):
                for piece in range(chunk // q_block):
                    block = c * (chunk // q_block) + piece
                    q_rows = pl.ds(block * q_block, q_block)
                    end = (block + 1) * q_block
                    queries = stacked(du, q_rows, q_at, pair)
                    peak = total = sums = None
                    for start in range(0, end, KEYS):
                        stop = min(start + KEYS, end)
                        scores = dot_nt(du[start:stop, head_at(k_at, pair)], queries) * score_scale
                        scores = jnp.where(allowed_of(block, start, stop), scores, MASK_FILL)
                        top = jnp.max(scores, axis=0, keepdims=True)
                        new_peak = top if peak is None else jnp.maximum(peak, top)
                        exponent = jnp.exp(scores - new_peak)
                        add = jnp.sum(exponent, axis=0, keepdims=True)
                        more = dot_tn(du[start:stop, head_at(v_at, pair)], exponent.astype(LOW))
                        if peak is None:
                            total, sums = add, more
                        else:
                            shrink = jnp.exp(peak - new_peak)
                            total, sums = total * shrink + add, sums * shrink + more
                        peak = new_peak
                    lse[pair, block] = peak + jnp.log(total)
                    value = (sums * (1.0 / total)).T
                    for i in range(group_size):
                        du[q_rows, head_at(o_at, pair * group_size + i)] = value[
                            i * q_block : (i + 1) * q_block
                        ].astype(LOW)

            def project(cols):
                part[rows, cols] = dot_nn(du[rows, o_at], w_out[:, cols]).astype(LOW)

            tiled(width, 512, project)
            store.wait()
            swap1.scatter_start(c)

        def settle(c):
            value = low[swap1.rows(0, c), :].astype(F32) + swap1.scatter_result(c)
            resid[swap1.local(c), :] = value
            front_store(4 + c, resid.at[swap1.local(c)], resid_hbm.at[swap1.local(c)]).start()
            hidden[swap1.rows(0, c), :] = (unit_rows(value) * post_gain_ref[...]).astype(LOW)
            swap1.gather_start(c)

        def feed_in(c):
            rows = chunk_rows(c)

            def mask_step(local):
                at = pl.ds(c * chunk + local.start, local.size)
                grad[at, :] = jnp.where(valid(at), grad[at, :], jnp.zeros((), LOW))

            tiled(chunk, 32, mask_step)

            def unit_step(cols):
                gate = dot_nn(hidden[rows, :], wg[:, cols])
                up = dot_nn(hidden[rows, :], wu[:, cols])
                d_act = dot_nt(grad[rows, :], wd[cols, :])
                sig = jax.nn.sigmoid(gate)
                silu = gate * sig
                act[rows, cols] = (silu * up).astype(LOW)
                dg[rows, cols] = (d_act * up * sig * (1.0 + gate * (1.0 - sig))).astype(LOW)
                du[rows, cols] = (d_act * silu).astype(LOW)

            tiled(units, unit_tile, unit_step)

        def feed_back(c):
            rows = chunk_rows(c)
            swap1.scatter_end(c)

            def back_step(cols):
                part[rows, cols] = (
                    dot_nt(dg[rows, :], wg[cols, :]) + dot_nt(du[rows, :], wu[cols, :])
                ).astype(LOW)

            tiled(width, 512, back_step)

        for c in range(chunks + 1):
            if c < chunks:
                attend(c)
            if c >= 1 and c - 1 < chunks - 1:
                swap1.scatter_forward(c - 1)
                settle(c - 1)
            if c >= 2 and c - 2 < chunks - 2:
                swap1.gather_pass(c - 2, False)
        heads_store = front_store(3, du, heads_hbm)
        heads_store.start()
        resid_stores = [
            front_store(4 + c, resid.at[swap1.local(c)], resid_hbm.at[swap1.local(c)])
            for c in range(chunks)
        ]
        for item in raw_stores + feed_loads + [heads_store]:
            item.wait()
        last = chunks - 1
        swap1.gather_pass(0, True)
        feed_in(0)
        swap1.scatter_forward(last)
        settle(last)
        swap1.gather_pass(last - 1, False)
        feed_back(0)
        swap1.gather_pass(1, True)
        feed_in(1)
        swap1.gather_pass(last, False)
        feed_back(1)
        for c in range(2, chunks):
            swap1.gather_pass(c, True)
            if c == last:
                for early in range(last):
                    swap3.scatter_start(early)
            feed_in(c)
            if c < last:
                feed_back(c)
        line.fill(0, products(grad, act, (0, units, unit_tile)))
        for c in range(last):
            swap3.scatter_forward(c)
        feed_back(last)
        swap3.scatter_start(last)
        for c in range(chunks):
            swap1.gather_end(c)
            resid_stores[c].wait()


    def middle(wd, lines):
        def settle3(c):
            d_hidden = swap3.scatter_result(c)
            rows = resid[swap3.local(c), :]
            scale = inverse_norm(rows)
            add_to(post_part, jnp.sum(d_hidden * (rows * scale), axis=0, keepdims=True), c == 0)
            value = grad[swap3.rows(0, c), :].astype(F32) + rows_back(
                d_hidden * post_gain_ref[...], rows, scale
            )
            resid[swap3.local(c), :] = value
            low[swap3.rows(0, c), :] = value.astype(LOW)
            swap3.gather_start(c)

        def mix(c):
            swap3.scatter_end(c)
            rows = chunk_rows(c)

            def mix_step(cols):
                part[rows, cols] = dot_nn(act[rows, :], wd[:, cols]).astype(LOW)

            tiled(width, 512, mix_step)

        last = chunks - 1
        for c in range(last):
            settle3(c)
        line.fill(1, products(hidden, dg, (0, units, unit_tile)))
        swap3.scatter_forward(last)
        settle3(last)
        for c in range(last):
            swap3.gather_pass(c, False)
        line.tick(0, 1, lines)
        for c in range(chunks):
            mix(c)
        swap3.gather_pass(last, False)
        line.settle(lines)

    def rest(lines, total, turned, base, q_raw, k_raw, dk, dv):
        raw_loads = [
            load(1, q_raw_hbm, q_raw),
            load(2, k_raw_hbm, k_raw),
            load(3, resid_hbm, base),
        ]
        for item in raw_loads:
            item.start()
        act_load = load(0, heads_hbm, act)
        act_load.start()
        line.fill(2, products(hidden, du, (0, units, unit_tile)))
        normed_load = load(4, normed_hbm, hidden)
        normed_load.start()
        line.tick(0, 2, lines)
        for c in range(chunks):
            swap3.gather_pass(c, True)
            swap2.scatter_start(c)
        act_load.wait()

        def d_head_step(rows):
            dg[rows, o_at] = dot_nt(low[rows, :], w_out[...]).astype(LOW)

        tiled(rows_all, chunk, d_head_step)
        x_loads = [
            pltpu.make_async_copy(
                tokens_hbm.at[swap4.rows(0, c)], w_out.at[swap4.local(c)], token_sems.at[c]
            )
            for c in range(chunks)
        ]
        for item in x_loads:
            item.start()
        for item in raw_loads:
            item.wait()

        def pair_back(pair):
            for block in range(rows_all // q_block):
                rows = pl.ds(block * q_block, q_block)
                end = (block + 1) * q_block
                q2 = stacked(act, rows, q_at, pair)
                do2 = stacked(dg, rows, o_at, pair)
                keys = act[0:end, head_at(k_at, pair)]
                values = act[0:end, head_at(v_at, pair)]
                scores = dot_nt(keys, q2) * score_scale
                probs = jnp.where(
                    allowed_of(block, 0, end), jnp.exp(scores - lse[pair, block]), 0.0
                )
                d_probs = dot_nt(values, do2)
                delta = jnp.sum(probs * d_probs, axis=0, keepdims=True)
                d_scores = (probs * (d_probs - delta)).astype(LOW)
                d_value = dot_nn(probs.astype(LOW), do2)
                d_key = dot_nn(d_scores, q2)
                if block:
                    dv[0 : end - q_block, :] += d_value[: end - q_block]
                    dk[0 : end - q_block, :] += d_key[: end - q_block]
                dv[end - q_block : end, :] = d_value[end - q_block :]
                dk[end - q_block : end, :] = d_key[end - q_block :]
                d_query = (dot_tn(keys, d_scores) * score_scale).T
                for i in range(group_size):
                    head = pair * group_size + i
                    value, gain_sum = head_back(
                        d_query[i * q_block : (i + 1) * q_block],
                        q_raw[rows, pl.ds(head * head_width, head_width)],
                        cosine[rows, :],
                        sine[rows, :],
                        query_gain_ref[...],
                    )
                    dg[rows, head_at(q_at, head)] = value.astype(LOW)
                    add_to(query_part, gain_sum, head == 0 and block == 0)
            value, gain_sum = head_back(
                dk[...] * score_scale,
                k_raw[:, pl.ds(pair * head_width, head_width)],
                cosine[...],
                sine[...],
                key_gain_ref[...],
            )
            dg[:, head_at(k_at, pair)] = value.astype(LOW)
            add_to(key_part, gain_sum, pair == 0)
            dg[:, head_at(v_at, pair)] = dv[...].astype(LOW)

        store_group(0, lines, total, turned)
        for pair in range(pairs):
            pair_back(pair)
            if pair == 0:
                for c in range(chunks):
                    swap2.scatter_forward(c)
        line.tick(1, 1, lines)
        for c in range(chunks):
            rows = chunk_rows(c)

            def normed_step(cols):
                grad[rows, cols] = (
                    dot_nt(dg[rows, q_at], w_query[cols, :])
                    + dot_nt(dg[rows, k_at], w_key[cols, :])
                    + dot_nt(dg[rows, v_at], w_value[cols, :])
                ).astype(LOW)

            tiled(width, 512, normed_step)
        for c in range(chunks):
            rows = swap2.rows(0, c)
            mixed = swap2.scatter_result(c)
            part[rows, :] = jnp.where(valid(rows), base[swap2.local(c), :] + mixed, 0.0).astype(
                LOW
            )
        swap2.signal(free_sem)
        pl.semaphore_wait(free_sem, swap2.bits)
        for c in range(chunks):
            swap4.scatter_start(c)

        def own_stores(which, source, target, swap):
            return [
                pltpu.make_async_copy(
                    source.at[swap.rows(0, c), :],
                    target.at[swap.rows(0, c), :],
                    own_sems.at[which, c],
                )
                for c in range(chunks)
            ]

        own2 = own_stores(0, part, output, swap2)
        own4 = own_stores(1, grad, in_grad, swap4)
        for item in own2:
            item.start()
        normed_load.wait()
        line.tick(1, 2, lines)

        from_normed = products(hidden, dg, (0, o_at.start, heads_width))
        from_low = products(low, act, (o_at.start, units, heads_width))

        def last_tile(i):
            yield from from_normed(i)
            yield from from_low(i)

        line.fill(3, last_tile)
        for c in range(chunks):
            swap4.scatter_forward(c)
        store_group(1, lines, total, turned)
        for item in x_loads:
            item.wait()
        for c in range(chunks):
            local = swap4.local(c)
            d_normed = swap4.scatter_result(c)
            x = w_out[local, :].astype(F32)
            scale = inverse_norm(x)
            add_to(in_part, jnp.sum(d_normed * (x * scale), axis=0, keepdims=True), c == 0)
            value = resid[local, :] + rows_back(d_normed * in_gain_ref[...], x, scale)
            grad[swap4.rows(0, c), :] = value.astype(LOW)
            swap4.gather_start(c)
            own4[c].start()
        steps = len(spread.steps)
        spread.copy(0).start()
        for c in range(chunks):
            swap4.gather_pass(c, False)
        line.tick(2, 1, lines)
        for c in range(chunks):
            swap2.gather_start(c)
        spread.next(0)
        spread.next(1)
        for c in range(chunks):
            swap2.gather_pass(c, False)
        line.tick(2, 2, lines)
        for step in range(2, steps):
            spread.next(step)
        gains_out[...] = spread.mine[steps]
        for c in range(chunks):
            swap4.gather_pass(c, True)
        store_group(2, lines, total, turned)
        for c in range(chunks):
            swap2.gather_pass(c, True)
        for step in range(1, line.places - 1):
            line.tick(3, step, lines)
        store_group(3, lines, total, turned)
        for item in own2 + own4:
            item.wait()
        for c in range(chunks):
            swap3.gather_end(c)
            for swap in (swap2, swap4):
                swap.scatter_end(c)
                swap.gather_end(c)
        for group in range(line.groups):
            line.ends(group, "wait")

    def store_group(group, lines, total, turned):
        line.finish(group, lines, total)
        if group == 0:
            turned[...] = total[...].T
            copies = [(turned, down_out)]
        elif group == 3:
            turned[0:heads_width, :] = total[:, o_at].T
            copies = [
                (total.at[:, q_at], query_out),
                (total.at[:, k_at], key_out),
                (total.at[:, v_at], value_out),
                (turned.at[pl.ds(0, heads_width), :], proj_out),
            ]
        else:
            copies = [(total, (gate_out, up_out)[group - 1])]
        copies = [
            pltpu.make_async_copy(src, dst, final_sems.at[i])
            for i, (src, dst) in enumerate(copies)
        ]
        for copy in copies:
            copy.start()
        for copy in copies:
            copy.wait()

    def both(wd):
        pl.run_scoped(
            functools.partial(front, wd),
            pltpu.VMEM((width, units), LOW),
            pltpu.VMEM((width, units), LOW),
            pltpu.VMEM((chunk, heads_width), F32),
            pltpu.VMEM((chunk, keys_width), F32),
        )
        pl.run_scoped(functools.partial(middle, wd), lines)

    lines = pltpu.VMEM((2, 2, line.tile, line.width), LOW)
    pl.run_scoped(both, pltpu.VMEM((units, width), LOW))
    pl.run_scoped(
        rest,
        lines,
        pltpu.VMEM((line.tile, line.width), F32),
        pltpu.VMEM((line.width, line.tile), F32),
        pltpu.VMEM(resid.shape, F32),
        pltpu.VMEM((rows_all, heads_width), F32),
        pltpu.VMEM((rows_all, keys_width), F32),
        pltpu.VMEM((rows_all, head_width), F32),
        pltpu.VMEM((rows_all, head_width), F32),
    )


def layer_call(counts, sizes, length, gains, tokens, out_grad, tables, attn_weights, feed_weights):
    tensor_count, dp_count = counts
    q_block, head_width, pairs, group_size = sizes
    rows, width = tokens.shape
    units = feed_weights[0].shape[1]
    heads_width, keys_width = attn_weights[0].shape[1], attn_weights[1].shape[1]
    tile = width // dp_count
    swaps = [Swap(tensor_count, rows, width) for _ in range(4)]
    line = Line(dp_count, 4, tile, units)
    spread = Spread(counts, 2 * width + 2 * head_width)
    chunks = swaps[0].chunks
    wide = jax.ShapeDtypeStruct((rows, width), LOW)
    out_shape = (
        wide,
        wide,
        jax.ShapeDtypeStruct((1, spread.length), F32),
        jax.ShapeDtypeStruct((units, tile), F32),
        jax.ShapeDtypeStruct((tile, units), F32),
        jax.ShapeDtypeStruct((tile, units), F32),
        jax.ShapeDtypeStruct((tile, heads_width), F32),
        jax.ShapeDtypeStruct((tile, keys_width), F32),
        jax.ShapeDtypeStruct((tile, keys_width), F32),
        jax.ShapeDtypeStruct((heads_width, tile), F32),
        *line.outputs(),
        wide,
        jax.ShapeDtypeStruct((rows, 2 * heads_width + 2 * keys_width), LOW),
        jax.ShapeDtypeStruct((rows, heads_width), F32),
        jax.ShapeDtypeStruct((rows, keys_width), F32),
        jax.ShapeDtypeStruct((chunks * swaps[0].block, width), F32),
    )
    big = pltpu.VMEM((rows, width), LOW)
    inner = pltpu.VMEM((rows, units), LOW)
    return pl.pallas_call(
        functools.partial(layer_kernel, (*swaps, line, spread, sizes)),
        out_shape=out_shape,
        in_specs=[pl.BlockSpec(memory_space=pltpu.SMEM)] + [vmem_spec()] * 4 + [any_spec()] * 11,
        out_specs=(any_spec(),) * 2 + (vmem_spec(),) + (any_spec(),) * 15,
        scratch_shapes=[
            big,
            big,
            inner,
            inner,
            inner,
            big,
            big,
            pltpu.VMEM((chunks * swaps[0].block, width), F32),
            pltpu.VMEM((2, tile, units), LOW),
            pltpu.VMEM((tile, units), LOW),
            pltpu.VMEM((tile, rows), LOW),
            swaps[0].landing(),
            pltpu.VMEM((width, heads_width), LOW),
            pltpu.VMEM((width, keys_width), LOW),
            pltpu.VMEM((width, keys_width), LOW),
            pltpu.VMEM((heads_width, width), LOW),
            pltpu.VMEM((rows, head_width), F32),
            pltpu.VMEM((rows, head_width), F32),
            pltpu.VMEM((pairs, rows // q_block, 1, group_size * q_block), F32),
            pltpu.SemaphoreType.DMA((10,)),
            pltpu.SemaphoreType.DMA((chunks,)),
            pltpu.SemaphoreType.DMA((4 + chunks,)),
            pltpu.SemaphoreType.DMA((2, chunks)),
            pltpu.SemaphoreType.DMA((4,)),
            pltpu.SemaphoreType.REGULAR,
            *[item for swap in swaps for item in swap.semaphores()],
            *line.semaphores(),
            *spread.scratch(),
        ],
        compiler_params=kernel_params(0),
        name="layer",
    )(length, *gains, tokens, out_grad, *tables, *attn_weights, *feed_weights)[:10]


def rope_tables(head_width, row_count):
    half_width = head_width // 2
    inv_freq = ROPE_BASE ** (-2.0 * np.arange(half_width, dtype=np.float32) / head_width)
    angles = np.arange(row_count, dtype=np.float32)[:, None] * inv_freq.astype(np.float32)[None, :]
    cosine, sine = np.cos(angles), np.sin(angles)
    tables = np.concatenate([cosine, cosine], 1), np.concatenate([-sine, sine], 1)
    return tuple(jnp.asarray(table, F32) for table in tables)


def on_device(
    tensor_count,
    dp_count,
    tokens,
    lengths,
    in_gain,
    w_query,
    w_key,
    w_value,
    query_gain,
    key_gain,
    w_out,
    post_gain,
    w_gate,
    w_up,
    w_down,
    out_grad,
):
    head_width = query_gain.shape[0]
    pairs = w_key.shape[1] // head_width
    group_size = w_query.shape[1] // w_key.shape[1]
    q_block = min(128, tokens.shape[0])
    (
        output,
        in_grad,
        gains,
        grad_down,
        grad_gate,
        grad_up,
        grad_query,
        grad_key,
        grad_value,
        grad_out,
    ) = layer_call(
        (tensor_count, dp_count),
        (q_block, head_width, pairs, group_size),
        lengths,
        (in_gain[None], post_gain[None], query_gain[None], key_gain[None]),
        tokens,
        out_grad,
        rope_tables(head_width, tokens.shape[0]),
        (w_query, w_key, w_value, w_out),
        (w_gate, w_up, w_down),
    )
    width = tokens.shape[1]
    cuts = (width, 2 * width, 2 * width + head_width)
    grad_post_gain, grad_in_gain, grad_query_gain, grad_key_gain = jnp.split(gains[0], cuts)
    return (
        output,
        in_grad,
        grad_in_gain,
        grad_query,
        grad_key,
        grad_value,
        grad_query_gain,
        grad_key_gain,
        grad_out,
        grad_post_gain,
        grad_gate,
        grad_up,
        grad_down,
    )


def solution(mesh):
    tensor_count, dp_count = mesh.shape["tensor"], mesh.shape["dp"]

    def layer(*args):
        return on_device(tensor_count, dp_count, *args)

    return jax.shard_map(
        layer,
        mesh=mesh,
        in_specs=(
            P("dp", None),
            P("dp"),
            P(),
            P(None, "tensor"),
            P(None, "tensor"),
            P(None, "tensor"),
            P(),
            P(),
            P("tensor", None),
            P(),
            P(None, "tensor"),
            P(None, "tensor"),
            P("tensor", None),
            P("dp", None),
        ),
        out_specs=(
            P("dp", None),
            P("dp", None),
            P(),
            P("dp", "tensor"),
            P("dp", "tensor"),
            P("dp", "tensor"),
            P(),
            P(),
            P("tensor", "dp"),
            P(),
            P("dp", "tensor"),
            P("dp", "tensor"),
            P("tensor", "dp"),
        ),
        check_vma=False,
    )
```

```python
import functools

import jax
import jax.numpy as jnp
import numpy as np
from jax import lax
from jax.experimental import pallas as pl
from jax.experimental.pallas import tpu as pltpu
from jax.sharding import PartitionSpec as P

NORM_EPS = 1e-06
ROPE_BASE = 1000000.0
MASK_FILL = -1e30
LOW = jnp.bfloat16
F32 = jnp.float32
MESH = pl.DeviceIdType.MESH
VMEM_BYTES = 65408 * 1024
CHUNK = 256
KEYS = 256
AWAY = 3


def unit_rows(matrix):
    return matrix * lax.rsqrt(jnp.mean(matrix * matrix, axis=-1, keepdims=True) + NORM_EPS)


def dot_nn(left, right):
    return jnp.dot(left, right, preferred_element_type=F32)


def dot_tn(left, right):
    return lax.dot_general(left, right, (((0,), (0,)), ((), ())), preferred_element_type=F32)


def dot_nt(left, right):
    return lax.dot_general(left, right, (((1,), (1,)), ((), ())), preferred_element_type=F32)


class Swap:
    def __init__(self, count, rows, width):
        self.count, self.width = count, width
        self.bits = count.bit_length() - 1
        self.chunk = min(CHUNK, rows)
        self.chunks = rows // self.chunk
        self.block = self.chunk // count
        self.half = width // 2
        self.orders = [list(range(self.bits)), list(range(self.bits))[::-1]]
        self.slots = []
        for order in self.orders:
            slot = {}
            for step in range(self.bits):
                for r in range(count):
                    if not any(r >> b & 1 for b in order[: step + 1]):
                        slot[step, r] = len(slot)
            self.slots.append(slot)

    def landing(self):
        return pltpu.VMEM((2, self.count - 1, self.chunks * self.block, self.half), LOW)

    def semaphores(self):
        n, c = self.count, self.chunks
        return [
            pltpu.SemaphoreType.DMA((2, n, c)),
            pltpu.SemaphoreType.DMA((2, n, c)),
            pltpu.SemaphoreType.DMA((2, n * self.bits, c)),
            pltpu.SemaphoreType.DMA((2, n, c)),
        ]

    def bind(self, part, recv, dest, sems, own=None):
        self.part, self.recv, self.dest, self.sems = part, recv, dest, sems
        self.own = dest if own is None else own
        self.me = lax.axis_index("tensor")
        return self

    def near(self, bit):
        own = (self.me // 2**bit) % 2
        return self.me + (1 - 2 * own) * 2**bit

    def rows(self, r, c):
        owner = self.me
        for bit in range(self.bits):
            if r >> bit & 1:
                owner = owner + (1 - 2 * ((self.me // 2**bit) % 2)) * 2**bit
        return pl.ds(pl.multiple_of(c * self.chunk + owner * self.block, self.block), self.block)

    def local(self, c):
        return pl.ds(c * self.block, self.block)

    def columns(self, half):
        return pl.ds(half * self.half, self.half)

    def signal(self, sem):
        for bit in range(self.bits):
            pl.semaphore_signal(
                sem, inc=1, device_id={"tensor": self.near(bit)}, device_id_type=MESH
            )

    def order(self):
        return sorted(range(1, self.count), key=lambda r: (-bin(r).count("1"), r))

    def first(self, half, r):
        return next(k for k, bit in enumerate(self.orders[half]) if r >> bit & 1)

    def scatter_copy(self, half, r, c):
        step = self.first(half, r)
        bit = self.orders[half][step]
        slot = self.slots[half][step, r ^ (1 << bit)]
        return pltpu.make_async_remote_copy(
            src_ref=self.part.at[self.rows(r, c), self.columns(half)],
            dst_ref=self.recv.at[half, slot, self.local(c)],
            send_sem=self.sems[0].at[half, r, c],
            recv_sem=self.sems[1].at[half, slot, c],
            device_id={"tensor": self.near(bit)},
            device_id_type=MESH,
        )

    def scatter_wait(self, half, step, r, c):
        slot = self.slots[half][step, r]
        ref = self.recv.at[half, slot, self.local(c)]
        pltpu.make_async_copy(ref, ref, self.sems[1].at[half, slot, c]).wait()
        return ref

    def scatter_start(self, c):
        for r in self.order():
            for half in range(2):
                if self.first(half, r) == 0:
                    self.scatter_copy(half, r, c).start()

    def scatter_forward(self, c):
        todo = [
            (self.first(half, r), half, r)
            for half in range(2)
            for r in range(1, self.count)
            if self.first(half, r) > 0
        ]
        for step, half, r in sorted(todo):
            where = self.rows(r, c), self.columns(half)
            total = self.part[where].astype(F32)
            for j in range(step):
                total = total + self.scatter_wait(half, j, r, c)[...].astype(F32)
            self.part[where] = total.astype(LOW)
            self.scatter_copy(half, r, c).start()

    def scatter_result(self, c):
        total = []
        for half in range(2):
            value = self.part[self.rows(0, c), self.columns(half)].astype(F32)
            for j in range(self.bits):
                value = value + self.scatter_wait(half, j, 0, c)[...].astype(F32)
            total.append(value)
        return jnp.concatenate(total, axis=1)

    def scatter_end(self, c):
        for half in range(2):
            for r in range(1, self.count):
                self.scatter_copy(half, r, c).wait_send()

    def last(self, half, r):
        order = self.orders[half][::-1]
        return max([-1] + [j for j, bit in enumerate(order) if r >> bit & 1])

    def gather_copy(self, half, r, step, c):
        bit = self.orders[half][::-1][step]
        where = self.rows(r, c), self.columns(half)
        return pltpu.make_async_remote_copy(
            src_ref=self.dest.at[where] if r else self.own.at[where],
            dst_ref=self.dest.at[where],
            send_sem=self.sems[2].at[half, r * self.bits + step, c],
            recv_sem=self.sems[3].at[half, r ^ (1 << bit), c],
            device_id={"tensor": self.near(bit)},
            device_id_type=MESH,
        )

    def gather_start(self, c):
        for step in range(self.bits):
            for half in range(2):
                self.gather_copy(half, 0, step, c).start()

    def gather_pass(self, c, late):
        todo = [
            (self.last(half, r), bin(r).count("1"), half, r)
            for half in range(2)
            for r in range(1, self.count)
        ]
        for step, _, half, r in sorted(todo):
            if (step == self.bits - 1) != late:
                continue
            ref = self.dest.at[self.rows(r, c), self.columns(half)]
            pltpu.make_async_copy(ref, ref, self.sems[3].at[half, r, c]).wait()
            for later in range(step + 1, self.bits):
                self.gather_copy(half, r, later, c).start()

    def gather_end(self, c):
        for half in range(2):
            for r in range(self.count):
                for step in range(self.last(half, r) + 1, self.bits):
                    self.gather_copy(half, r, step, c).wait_send()


class Line:
    def __init__(self, count, groups, tile, width):
        self.count, self.groups, self.tile, self.width = count, groups, tile, width
        self.places = count // 2

    def outputs(self):
        shape = (self.tile, self.width)
        return [
            jax.ShapeDtypeStruct((self.groups, self.places) + shape, LOW),
            jax.ShapeDtypeStruct((self.groups, self.places) + shape, LOW),
            jax.ShapeDtypeStruct((self.groups, self.places + 1) + shape, LOW),
        ]

    def semaphores(self):
        g, n = self.groups, self.places
        return [
            pltpu.SemaphoreType.DMA((g, n)),
            pltpu.SemaphoreType.DMA((g, n)),
            pltpu.SemaphoreType.DMA((2,)),
            pltpu.SemaphoreType.DMA((2, g, n)),
            pltpu.SemaphoreType.DMA((g, n + 1)),
            pltpu.SemaphoreType.DMA((6,)),
        ]

    def bind(self, core_land, acc, land, sems):
        self.core_land, self.acc, self.land = core_land, acc, land
        (
            self.core_send,
            self.core_recv,
            self.store_sem,
            self.line_send,
            self.line_recv,
            self.local_sem,
        ) = sems
        self.me = lax.axis_index("dp")
        self.place = self.me // 2
        self.core = self.me % 2
        self.other = self.me + 1 - 2 * self.core
        return self

    def signal(self, sem):
        @pl.when(self.place > 0)
        def _():
            pl.semaphore_signal(sem, inc=1, device_id={"dp": self.me - 2}, device_id_type=MESH)

        @pl.when(self.place < self.places - 1)
        def _():
            pl.semaphore_signal(sem, inc=1, device_id={"dp": self.me + 2}, device_id_type=MESH)

    def peers(self):
        ends = (self.places - 1 - self.place) // (self.places - 1) + self.place // (self.places - 1)
        return 2 - ends

    def core_copy(self, group, i, source):
        return pltpu.make_async_remote_copy(
            src_ref=source,
            dst_ref=self.core_land.at[group, i],
            send_sem=self.core_send.at[group, i],
            recv_sem=self.core_recv.at[group, i],
            device_id={"dp": self.other},
            device_id_type=MESH,
        )

    def fill(self, group, tile_of, away, away_slots, home, spots):
        n = self.places
        low_side = 1 - self.place // ((n + 1) // 2)

        def which(i):
            return i + low_side * (n - 1 - 2 * i)

        def send(i, carry):
            slot = lax.rem(i, away_slots)

            @pl.when(i >= away_slots)
            def _():
                self.core_copy(group, which(i - away_slots), away(slot)).wait_send()

            for cols, value in tile_of(2 * which(i) + 1 - self.core):
                away(slot)[:, cols] = value.astype(LOW)
            self.core_copy(group, which(i), away(slot)).start()
            return carry

        lax.fori_loop(0, n, send, 0)

        def store(i):
            slot = lax.rem(i, 2)
            return pltpu.make_async_copy(
                home(slot), self.acc.at[group, which(i)], self.store_sem.at[slot]
            )

        def fetch(i):
            slot = lax.rem(i, 2)
            return pltpu.make_async_copy(
                self.core_land.at[group, which(i)], home(2 + slot), self.local_sem.at[slot]
            )

        def arrive(i):
            landed = self.core_land.at[group, which(i)]
            pltpu.make_async_copy(landed, landed, self.core_recv.at[group, which(i)]).wait()
            fetch(i).start()

        arrive(0)

        def done(i):
            store(i).wait()
            j = which(i)
            for way, end in ((0, 0), (1, n - 1)):

                @pl.when(jnp.logical_and(self.place == end, i < spots))
                def _(way=way):
                    self.line_copy(group, way, j, self.acc.at[group, j]).start()

        def keep(i, carry):
            slot = lax.rem(i, 2)

            @pl.when(i + 1 < n)
            def _():
                arrive(i + 1)

            for spot, (cols, value) in enumerate(tile_of(2 * which(i) + self.core)):
                if spot == 0:
                    fetch(i).wait()
                home(slot)[:, cols] = (value + home(2 + slot)[:, cols].astype(F32)).astype(LOW)

            @pl.when(i >= 1)
            def _():
                done(i - 1)

            store(i).start()
            return carry

        lax.fori_loop(0, n, keep, 0)
        done(n - 1)
        for i in range(max(0, n - away_slots), n):
            self.core_copy(group, which(i), away(i % away_slots)).wait_send()

    def line_copy(self, group, way, j, source):
        if way == 0:
            slot, to = j, self.me + 2
        else:
            final = 1 - jnp.minimum(self.place - 1 - j, 1)
            slot, to = j + final * (self.places - j), self.me - 2
        return pltpu.make_async_remote_copy(
            src_ref=source,
            dst_ref=self.land.at[group, slot],
            send_sem=self.line_send.at[way, group, j],
            recv_sem=self.line_recv.at[group, slot],
            device_id={"dp": to},
            device_id_type=MESH,
        )

    def ends(self, group, act, spots):
        n = self.places

        @pl.when(self.place == 0)
        def _():
            for spot in spots:
                j = n - 1 - spot
                copy = self.line_copy(group, 0, j, self.acc.at[group, j])
                copy.start() if act == "start" else copy.wait_send()

        @pl.when(self.place == n - 1)
        def _():
            for j in spots:
                copy = self.line_copy(group, 1, j, self.acc.at[group, j])
                copy.start() if act == "start" else copy.wait_send()

    def landed(self, group, slot):
        ref = self.land.at[group, slot]
        pltpu.make_async_copy(ref, ref, self.line_recv.at[group, slot]).wait()
        return ref

    def on_way(self, step, way):
        far = self.place if way == 0 else self.places - 1 - self.place
        index = self.places - 1 - step + self.place if way == 0 else step - far
        return jnp.logical_and(far >= 1, far <= step), index

    def tick(self, group, step, lines):
        ways = [self.on_way(step, way) for way in range(2)]

        def here(way):
            return pltpu.make_async_copy(
                self.acc.at[group, ways[way][1]], lines.at[way, 0], self.local_sem.at[2 * way]
            )

        def there(way):
            return pltpu.make_async_copy(
                self.land.at[group, ways[way][1]], lines.at[way, 1], self.local_sem.at[2 * way + 1]
            )

        def back(way):
            return pltpu.make_async_copy(
                lines.at[way, 0], self.acc.at[group, ways[way][1]], self.local_sem.at[2 * way]
            )

        def come(way):
            here(way).start()
            self.landed(group, ways[way][1])
            there(way).start()

        def add(way):
            here(way).wait()
            there(way).wait()
            lines[way, 0] = (lines[way, 0].astype(F32) + lines[way, 1].astype(F32)).astype(LOW)
            back(way).start()

        def go(way):
            back(way).wait()
            j = ways[way][1]
            self.line_copy(group, way, j, self.acc.at[group, j]).start()

        for act in (come, add, go):
            for way in range(2):
                pl.when(ways[way][0])(functools.partial(act, way))

    def end(self, group):
        for step in range(1, self.places - 1):
            for way in range(2):
                active, j = self.on_way(step, way)

                @pl.when(active)
                def _(way=way, j=j):
                    self.line_copy(group, way, j, self.acc.at[group, j]).wait_send()

        self.ends(group, "wait", range(self.places - 1))

    def finish(self, group, lines, total):
        n = self.places
        sides = [(self.place > 0, self.place, 1), (self.place < n - 1, n, 2)]
        here = pltpu.make_async_copy(
            self.acc.at[group, self.place], lines.at[0, 0], self.local_sem.at[0]
        )
        here.start()

        def there(slot, spot):
            return pltpu.make_async_copy(
                self.land.at[group, slot], lines.at[spot // 2, spot % 2], self.local_sem.at[spot]
            )

        def come(slot, spot):
            self.landed(group, slot)
            there(slot, spot).start()

        def add(slot, spot):
            there(slot, spot).wait()
            total[...] += lines[spot // 2, spot % 2].astype(F32)

        for present, slot, spot in sides:
            pl.when(present)(functools.partial(come, slot, spot))
        here.wait()
        total[...] = lines[0, 0].astype(F32)
        for present, slot, spot in sides:
            pl.when(present)(functools.partial(add, slot, spot))


class Spread:
    def __init__(self, counts, length):
        tensor_count, dp_count = counts
        self.length, self.places = length, dp_count // 2
        self.steps = [("tensor", 2**b) for b in range(tensor_count.bit_length() - 1)]
        self.steps.append(("dp", 1))

    def scratch(self):
        n = len(self.steps)
        return [
            pltpu.VMEM((n + 1, 1, self.length), F32),
            pltpu.VMEM((n, 1, self.length), F32),
            pltpu.VMEM((self.places, 1, self.length), F32),
            pltpu.SemaphoreType.DMA((n,)),
            pltpu.SemaphoreType.DMA((n,)),
            pltpu.SemaphoreType.DMA((2, self.places)),
            pltpu.SemaphoreType.DMA((self.places,)),
        ]

    def bind(self, mine, land, far, send, recv, far_send, far_recv):
        self.mine, self.land, self.far = mine, land, far
        self.send, self.recv, self.far_send, self.far_recv = send, recv, far_send, far_recv
        self.me = lax.axis_index("dp")
        self.place = self.me // 2
        return self

    def partner(self, step):
        axis, size = self.steps[step]
        me = lax.axis_index(axis)
        return {axis: me + (1 - 2 * ((me // size) % 2)) * size}

    def signal(self, sem):
        for step in range(len(self.steps)):
            pl.semaphore_signal(
                sem, inc=1, device_id=self.partner(step), device_id_type=MESH
            )

    def copy(self, step):
        return pltpu.make_async_remote_copy(
            src_ref=self.mine.at[step],
            dst_ref=self.land.at[step],
            send_sem=self.send.at[step],
            recv_sem=self.recv.at[step],
            device_id=self.partner(step),
            device_id_type=MESH,
        )

    def next(self, step):
        self.copy(step).wait()
        self.mine[step + 1] = self.mine[step] + self.land[step]
        if step + 1 < len(self.steps):
            self.copy(step + 1).start()

    def far_copy(self, way, place):
        return pltpu.make_async_remote_copy(
            src_ref=self.far.at[place],
            dst_ref=self.far.at[place],
            send_sem=self.far_send.at[way, place],
            recv_sem=self.far_recv.at[place],
            device_id={"dp": self.me + 2 - 4 * way},
            device_id_type=MESH,
        )

    def pass_on(self, hops, act):
        n = self.places
        for way in range(2):
            place = self.place - hops if way == 0 else self.place + hops
            here = place >= 0 if way == 0 else place < n
            onward = self.place < n - 1 if way == 0 else self.place > 0
            if hops and act == "start":

                @pl.when(here)
                def _(place=place):
                    ref = self.far.at[place]
                    pltpu.make_async_copy(ref, ref, self.far_recv.at[place]).wait()

            @pl.when(jnp.logical_and(here, onward))
            def _(place=place, way=way):
                copy = self.far_copy(way, place)
                copy.start() if act == "start" else copy.wait_send()

    def far_start(self):
        self.far[self.place] = self.mine[len(self.steps)]
        self.pass_on(0, "start")

    def result(self):
        total = self.far[0]
        for place in range(1, self.places):
            total = total + self.far[place]
        return total

    def end(self):
        for hops in range(self.places - 1):
            self.pass_on(hops, "end")


def unrolled(total, size, body):
    for start in range(0, total, size):
        body(pl.ds(start, size))


def tiled(total, size, body):
    count = total // size

    def step(i, carry):
        body(pl.ds(pl.multiple_of(i * size, size), size))
        return carry

    lax.fori_loop(0, count, step, 0)


def any_spec():
    return pl.BlockSpec(memory_space=pl.ANY)


def vmem_spec():
    return pl.BlockSpec(memory_space=pltpu.VMEM)


def kernel_params(identity):
    return pltpu.CompilerParams(
        collective_id=identity, has_side_effects=True, vmem_limit_bytes=VMEM_BYTES
    )


def head_forward(raw, cosine, sine, gain):
    width = raw.shape[-1]
    unit = raw * lax.rsqrt(jnp.mean(raw * raw, axis=-1, keepdims=True) + NORM_EPS) * gain
    return (unit * cosine + pltpu.roll(unit, width // 2, 1) * sine).astype(LOW)


def head_back(grad, raw, cosine, sine, gain):
    width = raw.shape[-1]
    turned = grad * cosine - pltpu.roll(grad, width // 2, 1) * sine
    scale = lax.rsqrt(jnp.mean(raw * raw, axis=-1, keepdims=True) + NORM_EPS)
    unit = raw * scale
    gain_sum = jnp.sum(turned * unit, axis=0, keepdims=True)
    inner = turned * gain
    return scale * (inner - unit * jnp.mean(inner * unit, axis=-1, keepdims=True)), gain_sum


def rows_back(d_unit, rows, scale):
    unit = rows * scale
    return scale * (d_unit - unit * jnp.mean(d_unit * unit, axis=-1, keepdims=True))


def inverse_norm(rows):
    return lax.rsqrt(jnp.mean(rows * rows, axis=-1, keepdims=True) + NORM_EPS)


def layer_kernel(plan, *refs):
    swap1, swap3, swap2, swap4, line, spread, sizes = plan
    q_block, head_width, pairs, group_size = sizes
    refs = iter(refs)

    def take(count):
        return [next(refs) for _ in range(count)]

    length_ref, in_gain_ref, post_gain_ref, query_gain_ref, key_gain_ref = take(5)
    tokens_hbm, grad_hbm, cos_hbm, sin_hbm = take(4)
    w_query_hbm, w_key_hbm, w_value_hbm, w_out_hbm = take(4)
    wg_hbm, wu_hbm, wd_hbm = take(3)
    output, in_grad, gains_out = take(3)
    down_out, gate_out, up_out, query_out, key_out, value_out, proj_out = take(7)
    core_land, acc, land, normed_hbm, heads_hbm, q_raw_hbm, k_raw_hbm, resid_hbm = take(8)
    hidden, grad, act, dg, du, part, low, resid, flip, recv = take(10)
    w_query, w_key, w_value, w_out, cosine, sine, lse = take(7)
    in_sems, token_sems, front_sems, own_sems, final_sems, free_sem = take(6)
    swap1.bind(part, recv, hidden, take(4))
    swap3.bind(part, recv, low, take(4))
    swap2.bind(part, recv, output, take(4), own=part)
    swap4.bind(grad, recv, in_grad, take(4), own=grad)
    line.bind(core_land, acc, land, take(6))
    spread.bind(*take(7))

    rows_all, units = act.shape
    width = swap1.width
    heads_width, keys_width = w_query.shape[1], w_key.shape[1]
    unit_tile = 256
    chunk, chunks = swap1.chunk, swap1.chunks
    score_scale = head_width ** (-0.5)
    lanes = group_size * q_block
    length = length_ref[0]
    post_part = spread.mine.at[0, :, pl.ds(0, width)]
    in_part = spread.mine.at[0, :, pl.ds(width, width)]
    query_part = spread.mine.at[0, :, pl.ds(2 * width, head_width)]
    key_part = spread.mine.at[0, :, pl.ds(2 * width + head_width, head_width)]
    q_at = pl.ds(0, heads_width)
    k_at = pl.ds(heads_width, keys_width)
    v_at = pl.ds(heads_width + keys_width, keys_width)
    o_at = pl.ds(heads_width + 2 * keys_width, heads_width)

    def head_at(base, i):
        return pl.ds(base.start + i * head_width, head_width)

    def load(i, src, dst):
        return pltpu.make_async_copy(src, dst, in_sems.at[i])

    def chunk_rows(c):
        return pl.ds(c * chunk, chunk)

    def valid(rows):
        return rows.start + lax.broadcasted_iota(jnp.int32, (rows.size, 1), 0) < length

    def stacked(ref, rows, base, c):
        return jnp.concatenate(
            [ref[rows, head_at(base, c * group_size + i)] for i in range(group_size)], axis=0
        )

    def allowed_of(block, start, stop):
        k_pos = start + lax.broadcasted_iota(jnp.int32, (stop - start, lanes), 0)
        q_pos = block * q_block + lax.rem(
            lax.broadcasted_iota(jnp.int32, (1, lanes), 1), q_block
        )
        return k_pos < jnp.minimum(q_pos + 1, length)

    def tile_cols(i):
        return pl.ds(pl.multiple_of(i * line.tile, line.tile), line.tile)

    def products(left, right, cuts):
        def tile_of(i):
            flip[...] = left[:, tile_cols(i)].T
            for start in range(*cuts):
                cols = pl.ds(start, cuts[2])
                yield cols, dot_nn(flip[...], right[:, cols])

        return tile_of

    middle_step = line.places // 2

    def tick(group, half, lines):
        for step in (range(1, middle_step), range(middle_step, line.places - 1))[half]:
            line.tick(group, step, lines)

    def add_to(ref, value, first):
        if first:
            ref[...] = value
        else:
            ref[...] += value


    def front(wd, wg, wu, q_raw, k_raw):
        attn_loads = [
            load(0, w_query_hbm, w_query),
            load(1, w_key_hbm, w_key),
            load(2, w_value_hbm, w_value),
            load(3, cos_hbm, cosine),
            load(4, sin_hbm, sine),
            load(5, w_out_hbm, w_out),
        ]
        feed_loads = [
            load(6, wg_hbm, wg),
            load(7, wu_hbm, wu),
            load(8, grad_hbm, grad),
            load(9, wd_hbm, wd),
        ]
        token_loads = [
            pltpu.make_async_copy(
                tokens_hbm.at[chunk_rows(c)], low.at[chunk_rows(c)], token_sems.at[c]
            )
            for c in range(chunks)
        ]
        for item in token_loads[:1] + attn_loads + token_loads[1:] + feed_loads:
            item.start()
        barrier = pltpu.get_barrier_semaphore()
        spread.signal(barrier)
        line.signal(barrier)
        pl.semaphore_wait(barrier, len(spread.steps) + line.peers())

        def front_store(i, src, dst):
            return pltpu.make_async_copy(src, dst, front_sems.at[i])

        raw_stores = []

        def attend(c):
            rows = chunk_rows(c)
            token_loads[c].wait()

            def norm_step(local):
                at = pl.ds(c * chunk + local.start, local.size)
                x = low[at, :].astype(F32)
                hidden[at, :] = (unit_rows(x) * in_gain_ref[...]).astype(LOW)

            tiled(chunk, 32, norm_step)
            store = front_store(0, hidden.at[rows], normed_hbm.at[rows])
            store.start()
            if c == 0:
                for item in attn_loads:
                    item.wait()
            for item in raw_stores:
                item.wait()
            raw_stores.clear()
            q_raw[...] = dot_nn(hidden[rows, :], w_query[...])
            k_raw[...] = dot_nn(hidden[rows, :], w_key[...])
            du[rows, v_at] = dot_nn(hidden[rows, :], w_value[...]).astype(LOW)
            for raw, base, gain in ((q_raw, q_at, query_gain_ref), (k_raw, k_at, key_gain_ref)):
                for i in range(base.size // head_width):
                    du[rows, head_at(base, i)] = head_forward(
                        raw[:, pl.ds(i * head_width, head_width)],
                        cosine[rows, :],
                        sine[rows, :],
                        gain[...],
                    )
            raw_stores.append(front_store(1, q_raw, q_raw_hbm.at[rows]))
            raw_stores.append(front_store(2, k_raw, k_raw_hbm.at[rows]))
            for item in raw_stores:
                item.start()
            for pair in range(pairs):
                for piece in range(chunk // q_block):
                    block = c * (chunk // q_block) + piece
                    q_rows = pl.ds(block * q_block, q_block)
                    end = (block + 1) * q_block
                    queries = stacked(du, q_rows, q_at, pair)
                    peak = total = sums = None
                    for start in range(0, end, KEYS):
                        stop = min(start + KEYS, end)
                        scores = dot_nt(du[start:stop, head_at(k_at, pair)], queries) * score_scale
                        scores = jnp.where(allowed_of(block, start, stop), scores, MASK_FILL)
                        top = jnp.max(scores, axis=0, keepdims=True)
                        new_peak = top if peak is None else jnp.maximum(peak, top)
                        exponent = jnp.exp(scores - new_peak)
                        add = jnp.sum(exponent, axis=0, keepdims=True)
                        more = dot_tn(du[start:stop, head_at(v_at, pair)], exponent.astype(LOW))
                        if peak is None:
                            total, sums = add, more
                        else:
                            shrink = jnp.exp(peak - new_peak)
                            total, sums = total * shrink + add, sums * shrink + more
                        peak = new_peak
                    lse[pair, block] = peak + jnp.log(total)
                    value = (sums * (1.0 / total)).T
                    for i in range(group_size):
                        du[q_rows, head_at(o_at, pair * group_size + i)] = value[
                            i * q_block : (i + 1) * q_block
                        ].astype(LOW)

            def project(cols):
                part[rows, cols] = dot_nn(du[rows, o_at], w_out[:, cols]).astype(LOW)

            unrolled(width, 512, project)
            store.wait()
            swap1.scatter_start(c)

        def settle(c):
            value = low[swap1.rows(0, c), :].astype(F32) + swap1.scatter_result(c)
            resid[swap1.local(c), :] = value
            front_store(4 + c, resid.at[swap1.local(c)], resid_hbm.at[swap1.local(c)]).start()
            hidden[swap1.rows(0, c), :] = (unit_rows(value) * post_gain_ref[...]).astype(LOW)
            swap1.gather_start(c)

        def feed_in(c):
            rows = chunk_rows(c)

            def mask_step(local):
                at = pl.ds(c * chunk + local.start, local.size)
                grad[at, :] = jnp.where(valid(at), grad[at, :], jnp.zeros((), LOW))

            tiled(chunk, 32, mask_step)

            def unit_step(cols):
                gate = dot_nn(hidden[rows, :], wg[:, cols])
                up = dot_nn(hidden[rows, :], wu[:, cols])
                d_act = dot_nt(grad[rows, :], wd[cols, :])
                sig = jax.nn.sigmoid(gate)
                silu = gate * sig
                act[rows, cols] = (silu * up).astype(LOW)
                dg[rows, cols] = (d_act * up * sig * (1.0 + gate * (1.0 - sig))).astype(LOW)
                du[rows, cols] = (d_act * silu).astype(LOW)

            unrolled(units, unit_tile, unit_step)

        def feed_back(c):
            rows = chunk_rows(c)

            def back_step(cols):
                part[rows, cols] = (
                    dot_nt(dg[rows, :], wg[cols, :]) + dot_nt(du[rows, :], wu[cols, :])
                ).astype(LOW)

            unrolled(width, 512, back_step)

        last = chunks - 1
        for c in range(chunks):
            attend(c)
            if c >= 1:
                swap1.scatter_forward(c - 1)
                if c < last:
                    settle(c - 1)
            if 2 <= c < last:
                swap1.gather_pass(c - 2, False)
        heads_store = front_store(3, du, heads_hbm)
        heads_store.start()
        resid_stores = [
            front_store(4 + c, resid.at[swap1.local(c)], resid_hbm.at[swap1.local(c)])
            for c in range(chunks)
        ]
        for item in raw_stores + feed_loads:
            item.wait()
        if last >= 2:
            swap1.gather_pass(last - 2, False)
        heads_store.wait()
        fed = 0
        if last >= 1:
            swap1.gather_pass(0, True)
            feed_in(0)
            settle(last - 1)
            fed = 1
        swap1.scatter_forward(last)
        if last >= 2:
            swap1.gather_pass(1, True) if last > 2 else None
            feed_in(1) if last > 2 else None
            fed = 2 if last > 2 else 1
        if last >= 1:
            swap1.gather_pass(last - 1, False)
        settle(last)
        swap1.gather_pass(last, False)
        for c in range(fed, chunks):
            swap1.gather_pass(c, True)
            feed_in(c)

        def slot_of(ref):
            def slot(i):
                start = i * line.tile
                if not isinstance(i, int):
                    start = pl.multiple_of(start, line.tile)
                return ref.at[pl.ds(start, line.tile), pl.ds(0, units)]

            return slot

        for c in range(chunks):
            swap1.scatter_end(c)
        line.fill(
            0,
            products(grad, act, (0, units, unit_tile)),
            slot_of(low),
            AWAY,
            slot_of(part),
            line.places - 1,
        )
        for c in range(chunks):
            feed_back(c)
            swap3.scatter_start(c)
            if c:
                swap3.scatter_forward(c - 1)
        for c in range(chunks):
            swap1.gather_end(c)
            resid_stores[c].wait()


    def fill(group, tile_of, lines, stage, spots):
        line.fill(
            group,
            tile_of,
            lambda slot: stage.at[slot],
            AWAY,
            lambda slot: lines.at[slot // 2, lax.rem(slot, 2)],
            spots,
        )

    def middle(wd, lines, stage):
        def settle3(c):
            d_hidden = swap3.scatter_result(c)
            rows = resid[swap3.local(c), :]
            scale = inverse_norm(rows)
            add_to(post_part, jnp.sum(d_hidden * (rows * scale), axis=0, keepdims=True), c == 0)
            value = grad[swap3.rows(0, c), :].astype(F32) + rows_back(
                d_hidden * post_gain_ref[...], rows, scale
            )
            resid[swap3.local(c), :] = value
            low[swap3.rows(0, c), :] = value.astype(LOW)
            swap3.gather_start(c)

        def mix(c):
            swap3.scatter_end(c)
            rows = chunk_rows(c)

            def mix_step(cols):
                part[rows, cols] = dot_nn(act[rows, :], wd[:, cols]).astype(LOW)

            unrolled(width, 512, mix_step)

        last = chunks - 1
        settle3(0)
        tick(0, 0, lines)
        for c in range(1, last):
            settle3(c)
            if c == 1:
                swap3.scatter_forward(last)
        if last >= 1:
            swap3.gather_pass(0, False)
        fill(1, products(hidden, dg, (0, units, unit_tile)), lines, stage, line.places - 1)
        tick(0, 1, lines)
        if last >= 1:
            settle3(last)
        for c in range(1, last):
            swap3.gather_pass(c, False)
        for c in range(chunks):
            mix(c)
        swap3.gather_pass(last, False)

    def rest(lines, stage, total, turned, base, q_raw, k_raw, dk, dv):
        raw_loads = [
            load(1, q_raw_hbm, q_raw),
            load(2, k_raw_hbm, k_raw),
            load(3, resid_hbm, base),
        ]
        act_load = load(0, heads_hbm, act)
        for item in raw_loads + [act_load]:
            item.start()
        for c in range(chunks):
            swap3.gather_pass(c, True)
            swap2.scatter_start(c)
            if c == chunks // 2 - 1:
                tick(1, 0, lines)
        fill(2, products(hidden, du, (0, units, unit_tile)), lines, stage, line.places - 1)
        normed_load = load(4, normed_hbm, hidden)
        normed_load.start()
        tick(1, 1, lines)
        swap2.scatter_forward(0)
        store_group(0, lines, total, turned)
        act_load.wait()

        def d_head_step(rows):
            dg[rows, o_at] = dot_nt(low[rows, :], w_out[...]).astype(LOW)

        unrolled(rows_all, chunk, d_head_step)
        x_loads = [
            pltpu.make_async_copy(
                tokens_hbm.at[swap4.rows(0, c)], w_out.at[swap4.local(c)], token_sems.at[c]
            )
            for c in range(chunks)
        ]
        for item in x_loads:
            item.start()
        for item in raw_loads:
            item.wait()

        def pair_back(pair):
            for block in range(rows_all // q_block):
                rows = pl.ds(block * q_block, q_block)
                end = (block + 1) * q_block
                q2 = stacked(act, rows, q_at, pair)
                do2 = stacked(dg, rows, o_at, pair)
                keys = act[0:end, head_at(k_at, pair)]
                values = act[0:end, head_at(v_at, pair)]
                scores = dot_nt(keys, q2) * score_scale
                probs = jnp.where(
                    allowed_of(block, 0, end), jnp.exp(scores - lse[pair, block]), 0.0
                )
                d_probs = dot_nt(values, do2)
                delta = jnp.sum(probs * d_probs, axis=0, keepdims=True)
                d_scores = (probs * (d_probs - delta)).astype(LOW)
                d_value = dot_nn(probs.astype(LOW), do2)
                d_key = dot_nn(d_scores, q2)
                if block:
                    dv[0 : end - q_block, :] += d_value[: end - q_block]
                    dk[0 : end - q_block, :] += d_key[: end - q_block]
                dv[end - q_block : end, :] = d_value[end - q_block :]
                dk[end - q_block : end, :] = d_key[end - q_block :]
                d_query = (dot_tn(keys, d_scores) * score_scale).T
                for i in range(group_size):
                    head = pair * group_size + i
                    value, gain_sum = head_back(
                        d_query[i * q_block : (i + 1) * q_block],
                        q_raw[rows, pl.ds(head * head_width, head_width)],
                        cosine[rows, :],
                        sine[rows, :],
                        query_gain_ref[...],
                    )
                    dg[rows, head_at(q_at, head)] = value.astype(LOW)
                    add_to(query_part, gain_sum, head == 0 and block == 0)
            value, gain_sum = head_back(
                dk[...] * score_scale,
                k_raw[:, pl.ds(pair * head_width, head_width)],
                cosine[...],
                sine[...],
                key_gain_ref[...],
            )
            dg[:, head_at(k_at, pair)] = value.astype(LOW)
            add_to(key_part, gain_sum, pair == 0)
            dg[:, head_at(v_at, pair)] = dv[...].astype(LOW)

        def own_stores(which, source, target, swap):
            return [
                pltpu.make_async_copy(
                    source.at[swap.rows(0, c), :],
                    target.at[swap.rows(0, c), :],
                    own_sems.at[which, c],
                )
                for c in range(chunks)
            ]

        own2 = own_stores(0, part, output, swap2)
        own4 = own_stores(1, grad, in_grad, swap4)

        def settle2(c):
            rows = swap2.rows(0, c)
            mixed = swap2.scatter_result(c)
            part[rows, :] = jnp.where(valid(rows), base[swap2.local(c), :] + mixed, 0.0).astype(
                LOW
            )
            own2[c].start()

        soon = chunks // 2
        for c in range(1, soon):
            swap2.scatter_forward(c)
        for pair in range(pairs):
            if pair == pairs - 1:
                for c in range(soon, chunks):
                    swap2.scatter_forward(c)
                for c in range(soon):
                    settle2(c)
                    swap2.gather_start(c)
            pair_back(pair)
        for c in range(chunks):
            rows = chunk_rows(c)

            def normed_step(cols):
                grad[rows, cols] = (
                    dot_nt(dg[rows, q_at], w_query[cols, :])
                    + dot_nt(dg[rows, k_at], w_key[cols, :])
                    + dot_nt(dg[rows, v_at], w_value[cols, :])
                ).astype(LOW)

            unrolled(width, 512, normed_step)
        for c in range(soon, chunks):
            settle2(c)
        swap2.signal(free_sem)
        pl.semaphore_wait(free_sem, swap2.bits)
        for c in range(chunks):
            swap4.scatter_start(c)

        tick(2, 0, lines)
        normed_load.wait()
        from_normed = products(hidden, dg, (0, o_at.start, heads_width))
        from_low = products(low, act, (o_at.start, units, heads_width))

        def last_tile(i):
            yield from from_normed(i)
            yield from from_low(i)

        fill(3, last_tile, lines, stage, line.places - 1)
        for c in range(chunks):
            swap4.scatter_forward(c)
            if c == soon - 1:
                tick(2, 1, lines)
                for early in range(soon):
                    swap2.gather_pass(early, False)
        store_group(1, lines, total, turned)
        for item in x_loads:
            item.wait()
        for c in range(chunks):
            local = swap4.local(c)
            d_normed = swap4.scatter_result(c)
            x = w_out[local, :].astype(F32)
            scale = inverse_norm(x)
            add_to(in_part, jnp.sum(d_normed * (x * scale), axis=0, keepdims=True), c == 0)
            value = resid[local, :] + rows_back(d_normed * in_gain_ref[...], x, scale)
            grad[swap4.rows(0, c), :] = value.astype(LOW)
            if c == chunks - 1:
                spread.copy(0).start()
            swap4.gather_start(c)
            own4[c].start()
        steps = len(spread.steps)
        for c in range(chunks):
            swap4.gather_pass(c, False)
            if c >= soon:
                swap2.gather_start(c)
            if c == 0:
                store_group(2, lines, total, turned)
            if c == soon:
                tick(3, 0, lines)
        spread.next(0)
        tick(3, 1, lines)
        for step in range(1, steps):
            spread.next(step)
        spread.far_start()
        for c in range(soon, chunks):
            swap2.gather_pass(c, False)
        for step in range(1, line.places - 1):
            spread.pass_on(step, "start")
        for swap in (swap4, swap2):
            for c in range(chunks):
                swap.gather_pass(c, True)
        store_group(3, lines, total, turned)
        spread.pass_on(line.places - 1, "start")
        gains_out[...] = spread.result()
        for item in own2 + own4:
            item.wait()
        for c in range(chunks):
            swap3.gather_end(c)
            for swap in (swap2, swap4):
                swap.scatter_end(c)
                swap.gather_end(c)
        for group in range(line.groups):
            line.end(group)
        spread.end()

    def store_group(group, lines, total, turned):
        line.finish(group, lines, total)
        if group == 0:
            turned[...] = total[...].T
            copies = [(turned, down_out)]
        elif group == 3:
            turned[0:heads_width, :] = total[:, o_at].T
            copies = [
                (total.at[:, q_at], query_out),
                (total.at[:, k_at], key_out),
                (total.at[:, v_at], value_out),
                (turned.at[pl.ds(0, heads_width), :], proj_out),
            ]
        else:
            copies = [(total, (gate_out, up_out)[group - 1])]
        copies = [
            pltpu.make_async_copy(src, dst, final_sems.at[i])
            for i, (src, dst) in enumerate(copies)
        ]
        for copy in copies:
            copy.start()
        for copy in copies:
            copy.wait()

    def both(wd):
        pl.run_scoped(
            functools.partial(front, wd),
            pltpu.VMEM((width, units), LOW),
            pltpu.VMEM((width, units), LOW),
            pltpu.VMEM((chunk, heads_width), F32),
            pltpu.VMEM((chunk, keys_width), F32),
        )
        pl.run_scoped(functools.partial(middle, wd), lines, stage)

    lines = pltpu.VMEM((2, 2, line.tile, line.width), LOW)
    stage = pltpu.VMEM((AWAY, line.tile, line.width), LOW)
    pl.run_scoped(both, pltpu.VMEM((units, width), LOW))
    pl.run_scoped(
        rest,
        lines,
        stage,
        pltpu.VMEM((line.tile, line.width), F32),
        pltpu.VMEM((line.width, line.tile), F32),
        pltpu.VMEM(resid.shape, F32),
        pltpu.VMEM((rows_all, heads_width), F32),
        pltpu.VMEM((rows_all, keys_width), F32),
        pltpu.VMEM((rows_all, head_width), F32),
        pltpu.VMEM((rows_all, head_width), F32),
    )


def layer_call(counts, sizes, length, gains, tokens, out_grad, tables, attn_weights, feed_weights):
    tensor_count, dp_count = counts
    q_block, head_width, pairs, group_size = sizes
    rows, width = tokens.shape
    units = feed_weights[0].shape[1]
    heads_width, keys_width = attn_weights[0].shape[1], attn_weights[1].shape[1]
    tile = width // dp_count
    swaps = [Swap(tensor_count, rows, width) for _ in range(4)]
    line = Line(dp_count, 4, tile, units)
    spread = Spread(counts, 2 * width + 2 * head_width)
    chunks = swaps[0].chunks
    wide = jax.ShapeDtypeStruct((rows, width), LOW)
    out_shape = (
        wide,
        wide,
        jax.ShapeDtypeStruct((1, spread.length), F32),
        jax.ShapeDtypeStruct((units, tile), F32),
        jax.ShapeDtypeStruct((tile, units), F32),
        jax.ShapeDtypeStruct((tile, units), F32),
        jax.ShapeDtypeStruct((tile, heads_width), F32),
        jax.ShapeDtypeStruct((tile, keys_width), F32),
        jax.ShapeDtypeStruct((tile, keys_width), F32),
        jax.ShapeDtypeStruct((heads_width, tile), F32),
        *line.outputs(),
        wide,
        jax.ShapeDtypeStruct((rows, 2 * heads_width + 2 * keys_width), LOW),
        jax.ShapeDtypeStruct((rows, heads_width), F32),
        jax.ShapeDtypeStruct((rows, keys_width), F32),
        jax.ShapeDtypeStruct((chunks * swaps[0].block, width), F32),
    )
    big = pltpu.VMEM((rows, width), LOW)
    inner = pltpu.VMEM((rows, units), LOW)
    return pl.pallas_call(
        functools.partial(layer_kernel, (*swaps, line, spread, sizes)),
        out_shape=out_shape,
        in_specs=[pl.BlockSpec(memory_space=pltpu.SMEM)] + [vmem_spec()] * 4 + [any_spec()] * 11,
        out_specs=(any_spec(),) * 2 + (vmem_spec(),) + (any_spec(),) * 15,
        scratch_shapes=[
            big,
            big,
            inner,
            inner,
            inner,
            big,
            big,
            pltpu.VMEM((chunks * swaps[0].block, width), F32),
            pltpu.VMEM((tile, rows), LOW),
            swaps[0].landing(),
            pltpu.VMEM((width, heads_width), LOW),
            pltpu.VMEM((width, keys_width), LOW),
            pltpu.VMEM((width, keys_width), LOW),
            pltpu.VMEM((heads_width, width), LOW),
            pltpu.VMEM((rows, head_width), F32),
            pltpu.VMEM((rows, head_width), F32),
            pltpu.VMEM((pairs, rows // q_block, 1, group_size * q_block), F32),
            pltpu.SemaphoreType.DMA((10,)),
            pltpu.SemaphoreType.DMA((chunks,)),
            pltpu.SemaphoreType.DMA((4 + chunks,)),
            pltpu.SemaphoreType.DMA((2, chunks)),
            pltpu.SemaphoreType.DMA((4,)),
            pltpu.SemaphoreType.REGULAR,
            *[item for swap in swaps for item in swap.semaphores()],
            *line.semaphores(),
            *spread.scratch(),
        ],
        compiler_params=kernel_params(0),
        name="layer",
    )(length, *gains, tokens, out_grad, *tables, *attn_weights, *feed_weights)[:10]


def rope_tables(head_width, row_count):
    half_width = head_width // 2
    inv_freq = ROPE_BASE ** (-2.0 * np.arange(half_width, dtype=np.float32) / head_width)
    angles = np.arange(row_count, dtype=np.float32)[:, None] * inv_freq.astype(np.float32)[None, :]
    cosine, sine = np.cos(angles), np.sin(angles)
    tables = np.concatenate([cosine, cosine], 1), np.concatenate([-sine, sine], 1)
    return tuple(jnp.asarray(table, F32) for table in tables)


def on_device(
    tensor_count,
    dp_count,
    tokens,
    lengths,
    in_gain,
    w_query,
    w_key,
    w_value,
    query_gain,
    key_gain,
    w_out,
    post_gain,
    w_gate,
    w_up,
    w_down,
    out_grad,
):
    head_width = query_gain.shape[0]
    pairs = w_key.shape[1] // head_width
    group_size = w_query.shape[1] // w_key.shape[1]
    q_block = min(128, tokens.shape[0])
    (
        output,
        in_grad,
        gains,
        grad_down,
        grad_gate,
        grad_up,
        grad_query,
        grad_key,
        grad_value,
        grad_out,
    ) = layer_call(
        (tensor_count, dp_count),
        (q_block, head_width, pairs, group_size),
        lengths,
        (in_gain[None], post_gain[None], query_gain[None], key_gain[None]),
        tokens,
        out_grad,
        rope_tables(head_width, tokens.shape[0]),
        (w_query, w_key, w_value, w_out),
        (w_gate, w_up, w_down),
    )
    width = tokens.shape[1]
    cuts = (width, 2 * width, 2 * width + head_width)
    grad_post_gain, grad_in_gain, grad_query_gain, grad_key_gain = jnp.split(gains[0], cuts)
    return (
        output,
        in_grad,
        grad_in_gain,
        grad_query,
        grad_key,
        grad_value,
        grad_query_gain,
        grad_key_gain,
        grad_out,
        grad_post_gain,
        grad_gate,
        grad_up,
        grad_down,
    )


def solution(mesh):
    tensor_count, dp_count = mesh.shape["tensor"], mesh.shape["dp"]

    def layer(*args):
        return on_device(tensor_count, dp_count, *args)

    return jax.shard_map(
        layer,
        mesh=mesh,
        in_specs=(
            P("dp", None),
            P("dp"),
            P(),
            P(None, "tensor"),
            P(None, "tensor"),
            P(None, "tensor"),
            P(),
            P(),
            P("tensor", None),
            P(),
            P(None, "tensor"),
            P(None, "tensor"),
            P("tensor", None),
            P("dp", None),
        ),
        out_specs=(
            P("dp", None),
            P("dp", None),
            P(),
            P("dp", "tensor"),
            P("dp", "tensor"),
            P("dp", "tensor"),
            P(),
            P(),
            P("tensor", "dp"),
            P(),
            P("dp", "tensor"),
            P("dp", "tensor"),
            P("tensor", "dp"),
        ),
        check_vma=False,
    )
```

```python
import functools

import jax
import jax.numpy as jnp
import numpy as np
from jax import lax
from jax.experimental import pallas as pl
from jax.experimental.pallas import tpu as pltpu
from jax.sharding import PartitionSpec as P

NORM_EPS = 1e-06
ROPE_BASE = 1000000.0
MASK_FILL = -1e30
LOW = jnp.bfloat16
F32 = jnp.float32
MESH = pl.DeviceIdType.MESH
VMEM_BYTES = 65408 * 1024
CHUNK = 256
KEYS = 256
AWAY = 3


def unit_rows(matrix):
    return matrix * lax.rsqrt(jnp.mean(matrix * matrix, axis=-1, keepdims=True) + NORM_EPS)


def dot_nn(left, right):
    return jnp.dot(left, right, preferred_element_type=F32)


def dot_tn(left, right):
    return lax.dot_general(left, right, (((0,), (0,)), ((), ())), preferred_element_type=F32)


def dot_nt(left, right):
    return lax.dot_general(left, right, (((1,), (1,)), ((), ())), preferred_element_type=F32)


class Swap:
    def __init__(self, count, rows, width):
        self.count, self.width = count, width
        self.bits = count.bit_length() - 1
        self.chunk = min(CHUNK, rows)
        self.chunks = rows // self.chunk
        self.block = self.chunk // count
        self.half = width // 2
        self.orders = [list(range(self.bits)), list(range(self.bits))[::-1]]
        self.slots = []
        for order in self.orders:
            slot = {}
            for step in range(self.bits):
                for r in range(count):
                    if not any(r >> b & 1 for b in order[: step + 1]):
                        slot[step, r] = len(slot)
            self.slots.append(slot)

    def landing(self):
        return pltpu.VMEM((2, self.count - 1, self.chunks * self.block, self.half), LOW)

    def semaphores(self):
        n, c = self.count, self.chunks
        return [
            pltpu.SemaphoreType.DMA((2, n, c)),
            pltpu.SemaphoreType.DMA((2, n, c)),
            pltpu.SemaphoreType.DMA((2, n * self.bits, c)),
            pltpu.SemaphoreType.DMA((2, n, c)),
        ]

    def bind(self, part, recv, dest, sems, own=None):
        self.part, self.recv, self.dest, self.sems = part, recv, dest, sems
        self.own = dest if own is None else own
        self.me = lax.axis_index("tensor")
        return self

    def near(self, bit):
        own = (self.me // 2**bit) % 2
        return self.me + (1 - 2 * own) * 2**bit

    def rows(self, r, c):
        owner = self.me
        for bit in range(self.bits):
            if r >> bit & 1:
                owner = owner + (1 - 2 * ((self.me // 2**bit) % 2)) * 2**bit
        return pl.ds(pl.multiple_of(c * self.chunk + owner * self.block, self.block), self.block)

    def local(self, c):
        return pl.ds(c * self.block, self.block)

    def columns(self, half):
        return pl.ds(half * self.half, self.half)

    def signal(self, sem):
        for bit in range(self.bits):
            pl.semaphore_signal(
                sem, inc=1, device_id={"tensor": self.near(bit)}, device_id_type=MESH
            )

    def order(self):
        return sorted(range(1, self.count), key=lambda r: (-bin(r).count("1"), r))

    def first(self, half, r):
        return next(k for k, bit in enumerate(self.orders[half]) if r >> bit & 1)

    def scatter_copy(self, half, r, c):
        step = self.first(half, r)
        bit = self.orders[half][step]
        slot = self.slots[half][step, r ^ (1 << bit)]
        return pltpu.make_async_remote_copy(
            src_ref=self.part.at[self.rows(r, c), self.columns(half)],
            dst_ref=self.recv.at[half, slot, self.local(c)],
            send_sem=self.sems[0].at[half, r, c],
            recv_sem=self.sems[1].at[half, slot, c],
            device_id={"tensor": self.near(bit)},
            device_id_type=MESH,
        )

    def scatter_wait(self, half, step, r, c):
        slot = self.slots[half][step, r]
        ref = self.recv.at[half, slot, self.local(c)]
        pltpu.make_async_copy(ref, ref, self.sems[1].at[half, slot, c]).wait()
        return ref

    def scatter_start(self, c):
        for r in self.order():
            for half in range(2):
                if self.first(half, r) == 0:
                    self.scatter_copy(half, r, c).start()

    def scatter_forward(self, c):
        todo = [
            (self.first(half, r), half, r)
            for half in range(2)
            for r in range(1, self.count)
            if self.first(half, r) > 0
        ]
        for step, half, r in sorted(todo):
            where = self.rows(r, c), self.columns(half)
            total = self.part[where].astype(F32)
            for j in range(step):
                total = total + self.scatter_wait(half, j, r, c)[...].astype(F32)
            self.part[where] = total.astype(LOW)
            self.scatter_copy(half, r, c).start()

    def scatter_result(self, c):
        total = []
        for half in range(2):
            value = self.part[self.rows(0, c), self.columns(half)].astype(F32)
            for j in range(self.bits):
                value = value + self.scatter_wait(half, j, 0, c)[...].astype(F32)
            total.append(value)
        return jnp.concatenate(total, axis=1)

    def scatter_end(self, c):
        for half in range(2):
            for r in range(1, self.count):
                self.scatter_copy(half, r, c).wait_send()

    def last(self, half, r):
        order = self.orders[half][::-1]
        return max([-1] + [j for j, bit in enumerate(order) if r >> bit & 1])

    def gather_copy(self, half, r, step, c):
        bit = self.orders[half][::-1][step]
        where = self.rows(r, c), self.columns(half)
        return pltpu.make_async_remote_copy(
            src_ref=self.dest.at[where] if r else self.own.at[where],
            dst_ref=self.dest.at[where],
            send_sem=self.sems[2].at[half, r * self.bits + step, c],
            recv_sem=self.sems[3].at[half, r ^ (1 << bit), c],
            device_id={"tensor": self.near(bit)},
            device_id_type=MESH,
        )

    def gather_start(self, c):
        for step in range(self.bits):
            for half in range(2):
                self.gather_copy(half, 0, step, c).start()

    def gather_pass(self, c, late):
        todo = [
            (self.last(half, r), bin(r).count("1"), half, r)
            for half in range(2)
            for r in range(1, self.count)
        ]
        for step, _, half, r in sorted(todo):
            if (step == self.bits - 1) != late:
                continue
            ref = self.dest.at[self.rows(r, c), self.columns(half)]
            pltpu.make_async_copy(ref, ref, self.sems[3].at[half, r, c]).wait()
            for later in range(step + 1, self.bits):
                self.gather_copy(half, r, later, c).start()

    def gather_end(self, c):
        for half in range(2):
            for r in range(self.count):
                for step in range(self.last(half, r) + 1, self.bits):
                    self.gather_copy(half, r, step, c).wait_send()


class Line:
    def __init__(self, count, groups, tile, width):
        self.count, self.groups, self.tile, self.width = count, groups, tile, width
        self.places = count // 2

    def outputs(self):
        shape = (self.tile, self.width)
        return [
            jax.ShapeDtypeStruct((self.groups, self.places) + shape, LOW),
            jax.ShapeDtypeStruct((self.groups, self.places) + shape, LOW),
            jax.ShapeDtypeStruct((self.groups, self.places + 1) + shape, LOW),
        ]

    def semaphores(self):
        g, n = self.groups, self.places
        return [
            pltpu.SemaphoreType.DMA((g, n)),
            pltpu.SemaphoreType.DMA((g, n)),
            pltpu.SemaphoreType.DMA((2,)),
            pltpu.SemaphoreType.DMA((2, g, n)),
            pltpu.SemaphoreType.DMA((g, n + 1)),
            pltpu.SemaphoreType.DMA((6,)),
        ]

    def bind(self, core_land, acc, land, sems):
        self.core_land, self.acc, self.land = core_land, acc, land
        (
            self.core_send,
            self.core_recv,
            self.store_sem,
            self.line_send,
            self.line_recv,
            self.local_sem,
        ) = sems
        self.me = lax.axis_index("dp")
        self.place = self.me // 2
        self.core = self.me % 2
        self.other = self.me + 1 - 2 * self.core
        return self

    def signal(self, sem):
        @pl.when(self.place > 0)
        def _():
            pl.semaphore_signal(sem, inc=1, device_id={"dp": self.me - 2}, device_id_type=MESH)

        @pl.when(self.place < self.places - 1)
        def _():
            pl.semaphore_signal(sem, inc=1, device_id={"dp": self.me + 2}, device_id_type=MESH)

    def peers(self):
        ends = (self.places - 1 - self.place) // (self.places - 1) + self.place // (self.places - 1)
        return 2 - ends

    def core_copy(self, group, i, source):
        return pltpu.make_async_remote_copy(
            src_ref=source,
            dst_ref=self.core_land.at[group, i],
            send_sem=self.core_send.at[group, i],
            recv_sem=self.core_recv.at[group, i],
            device_id={"dp": self.other},
            device_id_type=MESH,
        )

    def fill(self, group, tile_of, away, away_slots, home, came, spots):
        n = self.places
        low_side = 1 - self.place // ((n + 1) // 2)

        def which(i):
            return i + low_side * (n - 1 - 2 * i)

        def send(i):
            slot = lax.rem(i, away_slots)

            @pl.when(i >= away_slots)
            def _():
                self.core_copy(group, which(i - away_slots), away(slot)).wait_send()

            for cols, value in tile_of(2 * which(i) + 1 - self.core):
                away(slot)[:, cols] = value.astype(LOW)
            self.core_copy(group, which(i), away(slot)).start()

        def store(i):
            slot = lax.rem(i, 2)
            return pltpu.make_async_copy(
                home(slot), self.acc.at[group, which(i)], self.store_sem.at[slot]
            )

        def fetch(i):
            slot = lax.rem(i, 2)
            return pltpu.make_async_copy(
                self.core_land.at[group, which(i)], came(slot), self.local_sem.at[slot]
            )

        def arrive(i):
            landed = self.core_land.at[group, which(i)]
            pltpu.make_async_copy(landed, landed, self.core_recv.at[group, which(i)]).wait()
            fetch(i).start()

        def done(i):
            store(i).wait()
            j = which(i)
            for way, end in ((0, 0), (1, n - 1)):

                @pl.when(jnp.logical_and(self.place == end, i < spots))
                def _(way=way):
                    self.line_copy(group, way, j, self.acc.at[group, j]).start()

        def keep(i):
            slot = lax.rem(i, 2)
            for spot, (cols, value) in enumerate(tile_of(2 * which(i) + self.core)):
                if spot == 0:
                    fetch(i).wait()
                home(slot)[:, cols] = (value + came(slot)[:, cols].astype(F32)).astype(LOW)

            @pl.when(i >= 1)
            def _():
                done(i - 1)

            store(i).start()

        def both(i, carry):
            @pl.when(i < n)
            def _():
                send(i)

            @pl.when(jnp.logical_and(i >= 1, i <= n))
            def _():
                arrive(i - 1)

            @pl.when(i >= 2)
            def _():
                keep(i - 2)

            return carry

        lax.fori_loop(0, n + 2, both, 0)
        done(n - 1)
        for i in range(max(0, n - away_slots), n):
            self.core_copy(group, which(i), away(i % away_slots)).wait_send()

    def line_copy(self, group, way, j, source):
        if way == 0:
            slot, to = j, self.me + 2
        else:
            final = 1 - jnp.minimum(self.place - 1 - j, 1)
            slot, to = j + final * (self.places - j), self.me - 2
        return pltpu.make_async_remote_copy(
            src_ref=source,
            dst_ref=self.land.at[group, slot],
            send_sem=self.line_send.at[way, group, j],
            recv_sem=self.line_recv.at[group, slot],
            device_id={"dp": to},
            device_id_type=MESH,
        )

    def ends(self, group, act, spots):
        n = self.places

        @pl.when(self.place == 0)
        def _():
            for spot in spots:
                j = n - 1 - spot
                copy = self.line_copy(group, 0, j, self.acc.at[group, j])
                copy.start() if act == "start" else copy.wait_send()

        @pl.when(self.place == n - 1)
        def _():
            for j in spots:
                copy = self.line_copy(group, 1, j, self.acc.at[group, j])
                copy.start() if act == "start" else copy.wait_send()

    def landed(self, group, slot):
        ref = self.land.at[group, slot]
        pltpu.make_async_copy(ref, ref, self.line_recv.at[group, slot]).wait()
        return ref

    def on_way(self, step, way):
        far = self.place if way == 0 else self.places - 1 - self.place
        index = self.places - 1 - step + self.place if way == 0 else step - far
        return jnp.logical_and(far >= 1, far <= step), index

    def tick(self, group, step, lines):
        ways = [self.on_way(step, way) for way in range(2)]

        def here(way):
            return pltpu.make_async_copy(
                self.acc.at[group, ways[way][1]], lines.at[way, 0], self.local_sem.at[2 * way]
            )

        def there(way):
            return pltpu.make_async_copy(
                self.land.at[group, ways[way][1]], lines.at[way, 1], self.local_sem.at[2 * way + 1]
            )

        def back(way):
            return pltpu.make_async_copy(
                lines.at[way, 0], self.acc.at[group, ways[way][1]], self.local_sem.at[2 * way]
            )

        def come(way):
            here(way).start()
            self.landed(group, ways[way][1])
            there(way).start()

        def add(way):
            here(way).wait()
            there(way).wait()
            lines[way, 0] = (lines[way, 0].astype(F32) + lines[way, 1].astype(F32)).astype(LOW)
            back(way).start()

        def go(way):
            back(way).wait()
            j = ways[way][1]
            self.line_copy(group, way, j, self.acc.at[group, j]).start()

        for act in (come, add, go):
            for way in range(2):
                pl.when(ways[way][0])(functools.partial(act, way))

    def end(self, group):
        for step in range(1, self.places - 1):
            for way in range(2):
                active, j = self.on_way(step, way)

                @pl.when(active)
                def _(way=way, j=j):
                    self.line_copy(group, way, j, self.acc.at[group, j]).wait_send()

        self.ends(group, "wait", range(self.places - 1))

    def arrived(self, group):
        for present, slot in ((self.place > 0, self.place), (self.place < self.places - 1, self.places)):
            pl.when(present)(lambda slot=slot: self.landed(group, slot) and None)


class Spread:
    def __init__(self, counts, length):
        tensor_count, dp_count = counts
        self.length, self.places = length, dp_count // 2
        self.steps = [("tensor", 2**b) for b in range(tensor_count.bit_length() - 1)]
        self.steps.append(("dp", 1))

    def scratch(self):
        n = len(self.steps)
        return [
            pltpu.VMEM((n + 1, 1, self.length), F32),
            pltpu.VMEM((n, 1, self.length), F32),
            pltpu.VMEM((self.places, 1, self.length), F32),
            pltpu.SemaphoreType.DMA((n,)),
            pltpu.SemaphoreType.DMA((n,)),
            pltpu.SemaphoreType.DMA((2, self.places)),
            pltpu.SemaphoreType.DMA((self.places,)),
        ]

    def bind(self, mine, land, far, send, recv, far_send, far_recv):
        self.mine, self.land, self.far = mine, land, far
        self.send, self.recv, self.far_send, self.far_recv = send, recv, far_send, far_recv
        self.me = lax.axis_index("dp")
        self.place = self.me // 2
        return self

    def partner(self, step):
        axis, size = self.steps[step]
        me = lax.axis_index(axis)
        return {axis: me + (1 - 2 * ((me // size) % 2)) * size}

    def signal(self, sem):
        for step in range(len(self.steps)):
            pl.semaphore_signal(
                sem, inc=1, device_id=self.partner(step), device_id_type=MESH
            )

    def copy(self, step):
        return pltpu.make_async_remote_copy(
            src_ref=self.mine.at[step],
            dst_ref=self.land.at[step],
            send_sem=self.send.at[step],
            recv_sem=self.recv.at[step],
            device_id=self.partner(step),
            device_id_type=MESH,
        )

    def next(self, step):
        self.copy(step).wait()
        self.mine[step + 1] = self.mine[step] + self.land[step]
        if step + 1 < len(self.steps):
            self.copy(step + 1).start()

    def far_copy(self, way, place):
        return pltpu.make_async_remote_copy(
            src_ref=self.far.at[place],
            dst_ref=self.far.at[place],
            send_sem=self.far_send.at[way, place],
            recv_sem=self.far_recv.at[place],
            device_id={"dp": self.me + 2 - 4 * way},
            device_id_type=MESH,
        )

    def pass_on(self, hops, act):
        n = self.places
        for way in range(2):
            place = self.place - hops if way == 0 else self.place + hops
            here = place >= 0 if way == 0 else place < n
            onward = self.place < n - 1 if way == 0 else self.place > 0
            if hops and act == "start":

                @pl.when(here)
                def _(place=place):
                    ref = self.far.at[place]
                    pltpu.make_async_copy(ref, ref, self.far_recv.at[place]).wait()

            @pl.when(jnp.logical_and(here, onward))
            def _(place=place, way=way):
                copy = self.far_copy(way, place)
                copy.start() if act == "start" else copy.wait_send()

    def far_start(self):
        self.far[self.place] = self.mine[len(self.steps)]
        self.pass_on(0, "start")

    def result(self):
        total = self.far[0]
        for place in range(1, self.places):
            total = total + self.far[place]
        return total

    def end(self):
        for hops in range(self.places - 1):
            self.pass_on(hops, "end")


def unrolled(total, size, body):
    for start in range(0, total, size):
        body(pl.ds(start, size))


def tiled(total, size, body):
    count = total // size

    def step(i, carry):
        body(pl.ds(pl.multiple_of(i * size, size), size))
        return carry

    lax.fori_loop(0, count, step, 0)


def any_spec():
    return pl.BlockSpec(memory_space=pl.ANY)


def vmem_spec():
    return pl.BlockSpec(memory_space=pltpu.VMEM)


def kernel_params(identity):
    return pltpu.CompilerParams(
        collective_id=identity, has_side_effects=True, vmem_limit_bytes=VMEM_BYTES
    )


def head_forward(raw, cosine, sine, gain):
    width = raw.shape[-1]
    unit = raw * lax.rsqrt(jnp.mean(raw * raw, axis=-1, keepdims=True) + NORM_EPS) * gain
    return (unit * cosine + pltpu.roll(unit, width // 2, 1) * sine).astype(LOW)


def head_back(grad, raw, cosine, sine, gain):
    width = raw.shape[-1]
    turned = grad * cosine - pltpu.roll(grad, width // 2, 1) * sine
    scale = lax.rsqrt(jnp.mean(raw * raw, axis=-1, keepdims=True) + NORM_EPS)
    unit = raw * scale
    gain_sum = jnp.sum(turned * unit, axis=0, keepdims=True)
    inner = turned * gain
    return scale * (inner - unit * jnp.mean(inner * unit, axis=-1, keepdims=True)), gain_sum


def rows_back(d_unit, rows, scale):
    unit = rows * scale
    return scale * (d_unit - unit * jnp.mean(d_unit * unit, axis=-1, keepdims=True))


def inverse_norm(rows):
    return lax.rsqrt(jnp.mean(rows * rows, axis=-1, keepdims=True) + NORM_EPS)


def layer_kernel(plan, *refs):
    swap1, swap3, swap2, swap4, line, spread, sizes = plan
    q_block, head_width, pairs, group_size = sizes
    refs = iter(refs)

    def take(count):
        return [next(refs) for _ in range(count)]

    length_ref, in_gain_ref, post_gain_ref, query_gain_ref, key_gain_ref = take(5)
    tokens_hbm, grad_hbm, cos_hbm, sin_hbm = take(4)
    w_query_hbm, w_key_hbm, w_value_hbm, w_out_hbm = take(4)
    wg_hbm, wu_hbm, wd_hbm = take(3)
    output, in_grad, gains_out = take(3)
    core_land, acc, land, normed_hbm, heads_hbm, q_raw_hbm, k_raw_hbm, resid_hbm = take(8)
    hidden, grad, act, dg, du, part, low, resid, flip, recv = take(10)
    w_query, w_key, w_value, w_out, cosine, sine, lse = take(7)
    in_sems, token_sems, front_sems, own_sems, free_sem = take(5)
    swap1.bind(part, recv, hidden, take(4))
    swap3.bind(part, recv, low, take(4))
    swap2.bind(part, recv, output, take(4), own=part)
    swap4.bind(grad, recv, in_grad, take(4), own=grad)
    line.bind(core_land, acc, land, take(6))
    spread.bind(*take(7))

    rows_all, units = act.shape
    width = swap1.width
    heads_width, keys_width = w_query.shape[1], w_key.shape[1]
    unit_tile = 256
    chunk, chunks = swap1.chunk, swap1.chunks
    score_scale = head_width ** (-0.5)
    lanes = group_size * q_block
    length = length_ref[0]
    post_part = spread.mine.at[0, :, pl.ds(0, width)]
    in_part = spread.mine.at[0, :, pl.ds(width, width)]
    query_part = spread.mine.at[0, :, pl.ds(2 * width, head_width)]
    key_part = spread.mine.at[0, :, pl.ds(2 * width + head_width, head_width)]
    q_at = pl.ds(0, heads_width)
    k_at = pl.ds(heads_width, keys_width)
    v_at = pl.ds(heads_width + keys_width, keys_width)
    o_at = pl.ds(heads_width + 2 * keys_width, heads_width)

    def head_at(base, i):
        return pl.ds(base.start + i * head_width, head_width)

    def load(i, src, dst):
        return pltpu.make_async_copy(src, dst, in_sems.at[i])

    def chunk_rows(c):
        return pl.ds(c * chunk, chunk)

    def valid(rows):
        return rows.start + lax.broadcasted_iota(jnp.int32, (rows.size, 1), 0) < length

    def stacked(ref, rows, base, c):
        return jnp.concatenate(
            [ref[rows, head_at(base, c * group_size + i)] for i in range(group_size)], axis=0
        )

    def allowed_of(block, start, stop):
        k_pos = start + lax.broadcasted_iota(jnp.int32, (stop - start, lanes), 0)
        q_pos = block * q_block + lax.rem(
            lax.broadcasted_iota(jnp.int32, (1, lanes), 1), q_block
        )
        return k_pos < jnp.minimum(q_pos + 1, length)

    def tile_cols(i):
        return pl.ds(pl.multiple_of(i * line.tile, line.tile), line.tile)

    def products(left, right, cuts):
        def tile_of(i):
            flip[...] = left[:, tile_cols(i)].T
            for start in range(*cuts):
                cols = pl.ds(start, cuts[2])
                yield cols, dot_nn(flip[...], right[:, cols])

        return tile_of

    middle_step = line.places // 2

    def tick(group, half, lines):
        for step in (range(1, middle_step), range(middle_step, line.places - 1))[half]:
            line.tick(group, step, lines)

    def add_to(ref, value, first):
        if first:
            ref[...] = value
        else:
            ref[...] += value


    def front(wd, wg, wu, q_raw, k_raw):
        attn_loads = [
            load(0, w_query_hbm, w_query),
            load(1, w_key_hbm, w_key),
            load(2, w_value_hbm, w_value),
            load(3, cos_hbm, cosine),
            load(4, sin_hbm, sine),
            load(5, w_out_hbm, w_out),
        ]
        feed_loads = [
            load(8, grad_hbm, grad),
            load(9, wd_hbm, wd),
            load(6, wg_hbm, wg),
            load(7, wu_hbm, wu),
        ]
        token_loads = [
            pltpu.make_async_copy(
                tokens_hbm.at[chunk_rows(c)], low.at[chunk_rows(c)], token_sems.at[c]
            )
            for c in range(chunks)
        ]
        for item in token_loads[:1] + attn_loads + token_loads[1:] + feed_loads:
            item.start()
        barrier = pltpu.get_barrier_semaphore()
        spread.signal(barrier)
        line.signal(barrier)
        pl.semaphore_wait(barrier, len(spread.steps) + line.peers())

        def front_store(i, src, dst):
            return pltpu.make_async_copy(src, dst, front_sems.at[i])

        raw_stores = []

        def attend(c):
            rows = chunk_rows(c)
            token_loads[c].wait()

            def norm_step(local):
                at = pl.ds(c * chunk + local.start, local.size)
                x = low[at, :].astype(F32)
                hidden[at, :] = (unit_rows(x) * in_gain_ref[...]).astype(LOW)

            tiled(chunk, 32, norm_step)
            store = front_store(0, hidden.at[rows], normed_hbm.at[rows])
            store.start()
            if c == 0:
                for item in attn_loads:
                    item.wait()
            for item in raw_stores:
                item.wait()
            raw_stores.clear()
            q_raw[...] = dot_nn(hidden[rows, :], w_query[...])
            k_raw[...] = dot_nn(hidden[rows, :], w_key[...])
            du[rows, v_at] = dot_nn(hidden[rows, :], w_value[...]).astype(LOW)
            for raw, base, gain in ((q_raw, q_at, query_gain_ref), (k_raw, k_at, key_gain_ref)):
                for i in range(base.size // head_width):
                    du[rows, head_at(base, i)] = head_forward(
                        raw[:, pl.ds(i * head_width, head_width)],
                        cosine[rows, :],
                        sine[rows, :],
                        gain[...],
                    )
            raw_stores.append(front_store(1, q_raw, q_raw_hbm.at[rows]))
            raw_stores.append(front_store(2, k_raw, k_raw_hbm.at[rows]))
            for item in raw_stores:
                item.start()
            for pair in range(pairs):
                for piece in range(chunk // q_block):
                    block = c * (chunk // q_block) + piece
                    q_rows = pl.ds(block * q_block, q_block)
                    end = (block + 1) * q_block
                    queries = stacked(du, q_rows, q_at, pair)
                    peak = total = sums = None
                    for start in range(0, end, KEYS):
                        stop = min(start + KEYS, end)
                        scores = dot_nt(du[start:stop, head_at(k_at, pair)], queries) * score_scale
                        scores = jnp.where(allowed_of(block, start, stop), scores, MASK_FILL)
                        top = jnp.max(scores, axis=0, keepdims=True)
                        new_peak = top if peak is None else jnp.maximum(peak, top)
                        exponent = jnp.exp(scores - new_peak)
                        add = jnp.sum(exponent, axis=0, keepdims=True)
                        more = dot_tn(du[start:stop, head_at(v_at, pair)], exponent.astype(LOW))
                        if peak is None:
                            total, sums = add, more
                        else:
                            shrink = jnp.exp(peak - new_peak)
                            total, sums = total * shrink + add, sums * shrink + more
                        peak = new_peak
                    lse[pair, block] = peak + jnp.log(total)
                    value = (sums * (1.0 / total)).T
                    for i in range(group_size):
                        du[q_rows, head_at(o_at, pair * group_size + i)] = value[
                            i * q_block : (i + 1) * q_block
                        ].astype(LOW)

            def project(cols):
                part[rows, cols] = dot_nn(du[rows, o_at], w_out[:, cols]).astype(LOW)

            unrolled(width, 512, project)
            store.wait()
            swap1.scatter_start(c)

        def settle(c):
            value = low[swap1.rows(0, c), :].astype(F32) + swap1.scatter_result(c)
            resid[swap1.local(c), :] = value
            front_store(4 + c, resid.at[swap1.local(c)], resid_hbm.at[swap1.local(c)]).start()
            hidden[swap1.rows(0, c), :] = (unit_rows(value) * post_gain_ref[...]).astype(LOW)
            swap1.gather_start(c)

        def feed_ahead(c):
            rows = chunk_rows(c)

            def mask_step(local):
                at = pl.ds(c * chunk + local.start, local.size)
                grad[at, :] = jnp.where(valid(at), grad[at, :], jnp.zeros((), LOW))

            tiled(chunk, 32, mask_step)

            def ahead_step(cols):
                dg[rows, cols] = dot_nt(grad[rows, :], wd[cols, :]).astype(LOW)

            unrolled(units, unit_tile * (2 - units // unit_tile % 2), ahead_step)

        def feed_in(c):
            rows = chunk_rows(c)

            def unit_step(cols):
                gate = dot_nn(hidden[rows, :], wg[:, cols])
                up = dot_nn(hidden[rows, :], wu[:, cols])
                d_act = dg[rows, cols].astype(F32)
                sig = jax.nn.sigmoid(gate)
                silu = gate * sig
                act[rows, cols] = (silu * up).astype(LOW)
                dg[rows, cols] = (d_act * up * sig * (1.0 + gate * (1.0 - sig))).astype(LOW)
                du[rows, cols] = (d_act * silu).astype(LOW)

            unrolled(units, unit_tile, unit_step)

        def feed_back(c):
            rows = chunk_rows(c)

            def back_step(cols):
                part[rows, cols] = (
                    dot_nt(dg[rows, :], wg[cols, :]) + dot_nt(du[rows, :], wu[cols, :])
                ).astype(LOW)

            unrolled(width, 512, back_step)

        last = chunks - 1
        for c in range(chunks):
            attend(c)
            if c >= 1:
                swap1.scatter_forward(c - 1)
            if c == min(1, last):
                for item in feed_loads[:2]:
                    item.wait()
                for ahead in range(chunks):
                    feed_ahead(ahead)
            if 1 <= c < last:
                settle(c - 1)
            if 2 <= c < last:
                swap1.gather_pass(c - 2, False)
        heads_store = front_store(3, du, heads_hbm)
        heads_store.start()
        resid_stores = [
            front_store(4 + c, resid.at[swap1.local(c)], resid_hbm.at[swap1.local(c)])
            for c in range(chunks)
        ]
        for item in raw_stores + feed_loads[2:]:
            item.wait()
        if last >= 2:
            swap1.gather_pass(last - 2, False)
        heads_store.wait()
        fed = 0
        if last >= 1:
            swap1.gather_pass(0, True)
            feed_in(0)
            settle(last - 1)
            fed = 1
        swap1.scatter_forward(last)
        if last > 2:
            swap1.gather_pass(1, True)
            feed_in(1)
            fed = 2
        if last >= 1:
            swap1.gather_pass(last - 1, False)
        settle(last)
        swap1.scatter_end(0)
        if fed:
            feed_back(0)
        swap1.gather_pass(last, False)
        for c in range(fed, chunks):
            swap1.gather_pass(c, True)
            feed_in(c)

        def slot_of(ref, first):
            def slot(i):
                start = (first + i) * line.tile
                if not isinstance(i, int):
                    start = pl.multiple_of(start, line.tile)
                return ref.at[pl.ds(start, line.tile), pl.ds(0, units)]

            return slot

        for c in range(1, chunks):
            swap1.scatter_end(c)
        free = chunk // line.tile
        line.fill(
            0,
            products(grad, act, (0, units, unit_tile)),
            slot_of(low, 0),
            2,
            slot_of(part, free),
            slot_of(low, 2),
            line.places - 1,
        )
        for c in range(chunks):
            if c or not fed:
                feed_back(c)
            swap3.scatter_start(c)
            if c:
                swap3.scatter_forward(c - 1)
        for c in range(chunks):
            swap1.gather_end(c)
            resid_stores[c].wait()


    def fill(group, tile_of, lines, stage, spots):
        line.fill(
            group,
            tile_of,
            lambda slot: stage.at[slot],
            AWAY,
            lambda slot: lines.at[0, slot],
            lambda slot: lines.at[1, slot],
            spots,
        )

    def middle(wd, lines, stage):
        def settle3(c):
            d_hidden = swap3.scatter_result(c)
            rows = resid[swap3.local(c), :]
            scale = inverse_norm(rows)
            add_to(post_part, jnp.sum(d_hidden * (rows * scale), axis=0, keepdims=True), c == 0)
            value = grad[swap3.rows(0, c), :].astype(F32) + rows_back(
                d_hidden * post_gain_ref[...], rows, scale
            )
            resid[swap3.local(c), :] = value
            low[swap3.rows(0, c), :] = value.astype(LOW)
            swap3.gather_start(c)

        def mix(c):
            swap3.scatter_end(c)
            rows = chunk_rows(c)

            def mix_step(cols):
                part[rows, cols] = dot_nn(act[rows, :], wd[:, cols]).astype(LOW)

            unrolled(width, 512, mix_step)

        last = chunks - 1
        settle3(0)
        tick(0, 0, lines)
        for c in range(1, last):
            settle3(c)
            if c == 1:
                swap3.scatter_forward(last)
        if last >= 1:
            swap3.gather_pass(0, False)
        fill(1, products(hidden, dg, (0, units, unit_tile)), lines, stage, line.places - 1)
        tick(0, 1, lines)
        if last >= 1:
            settle3(last)
        for c in range(1, last):
            swap3.gather_pass(c, False)
        for c in range(chunks):
            mix(c)
        swap3.gather_pass(last, False)

    def rest(lines, stage, base, q_raw, k_raw, dk, dv):
        raw_loads = [
            load(1, q_raw_hbm, q_raw),
            load(2, k_raw_hbm, k_raw),
            load(3, resid_hbm, base),
        ]
        act_load = load(0, heads_hbm, act)
        for item in raw_loads + [act_load]:
            item.start()
        for c in range(chunks):
            swap3.gather_pass(c, True)
            swap2.scatter_start(c)
            if c == chunks // 2 - 1:
                tick(1, 0, lines)
        fill(2, products(hidden, du, (0, units, unit_tile)), lines, stage, line.places - 1)
        normed_load = load(4, normed_hbm, hidden)
        normed_load.start()
        tick(1, 1, lines)
        swap2.scatter_forward(0)
        line.arrived(0)
        act_load.wait()

        def d_head_step(rows):
            dg[rows, o_at] = dot_nt(low[rows, :], w_out[...]).astype(LOW)

        unrolled(rows_all, chunk, d_head_step)
        x_loads = [
            pltpu.make_async_copy(
                tokens_hbm.at[swap4.rows(0, c)], w_out.at[swap4.local(c)], token_sems.at[c]
            )
            for c in range(chunks)
        ]
        for item in x_loads:
            item.start()
        for item in raw_loads:
            item.wait()

        def pair_back(pair):
            for block in range(rows_all // q_block):
                rows = pl.ds(block * q_block, q_block)
                end = (block + 1) * q_block
                q2 = stacked(act, rows, q_at, pair)
                do2 = stacked(dg, rows, o_at, pair)
                keys = act[0:end, head_at(k_at, pair)]
                values = act[0:end, head_at(v_at, pair)]
                scores = dot_nt(keys, q2) * score_scale
                probs = jnp.where(
                    allowed_of(block, 0, end), jnp.exp(scores - lse[pair, block]), 0.0
                )
                d_probs = dot_nt(values, do2)
                delta = jnp.sum(probs * d_probs, axis=0, keepdims=True)
                d_scores = (probs * (d_probs - delta)).astype(LOW)
                d_value = dot_nn(probs.astype(LOW), do2)
                d_key = dot_nn(d_scores, q2)
                if block:
                    dv[0 : end - q_block, :] += d_value[: end - q_block]
                    dk[0 : end - q_block, :] += d_key[: end - q_block]
                dv[end - q_block : end, :] = d_value[end - q_block :]
                dk[end - q_block : end, :] = d_key[end - q_block :]
                d_query = (dot_tn(keys, d_scores) * score_scale).T
                for i in range(group_size):
                    head = pair * group_size + i
                    value, gain_sum = head_back(
                        d_query[i * q_block : (i + 1) * q_block],
                        q_raw[rows, pl.ds(head * head_width, head_width)],
                        cosine[rows, :],
                        sine[rows, :],
                        query_gain_ref[...],
                    )
                    dg[rows, head_at(q_at, head)] = value.astype(LOW)
                    add_to(query_part, gain_sum, head == 0 and block == 0)
            value, gain_sum = head_back(
                dk[...] * score_scale,
                k_raw[:, pl.ds(pair * head_width, head_width)],
                cosine[...],
                sine[...],
                key_gain_ref[...],
            )
            dg[:, head_at(k_at, pair)] = value.astype(LOW)
            add_to(key_part, gain_sum, pair == 0)
            dg[:, head_at(v_at, pair)] = dv[...].astype(LOW)

        def own_stores(which, source, target, swap):
            return [
                pltpu.make_async_copy(
                    source.at[swap.rows(0, c), :],
                    target.at[swap.rows(0, c), :],
                    own_sems.at[which, c],
                )
                for c in range(chunks)
            ]

        own2 = own_stores(0, part, output, swap2)
        own4 = own_stores(1, grad, in_grad, swap4)

        def settle2(c):
            rows = swap2.rows(0, c)
            mixed = swap2.scatter_result(c)
            part[rows, :] = jnp.where(valid(rows), base[swap2.local(c), :] + mixed, 0.0).astype(
                LOW
            )
            own2[c].start()

        soon = chunks // 2
        for c in range(1, soon):
            swap2.scatter_forward(c)
        for pair in range(pairs):
            if pair == pairs - 1:
                for c in range(soon, chunks):
                    swap2.scatter_forward(c)
                for c in range(soon):
                    settle2(c)
                    swap2.gather_start(c)
            pair_back(pair)
        for c in range(chunks):
            rows = chunk_rows(c)

            def normed_step(cols):
                grad[rows, cols] = (
                    dot_nt(dg[rows, q_at], w_query[cols, :])
                    + dot_nt(dg[rows, k_at], w_key[cols, :])
                    + dot_nt(dg[rows, v_at], w_value[cols, :])
                ).astype(LOW)

            unrolled(width, 512, normed_step)
        for c in range(soon, chunks):
            settle2(c)
        swap2.signal(free_sem)
        pl.semaphore_wait(free_sem, swap2.bits)
        for c in range(chunks):
            swap4.scatter_start(c)

        tick(2, 0, lines)
        normed_load.wait()
        from_normed = products(hidden, dg, (0, o_at.start, heads_width))
        from_low = products(low, act, (o_at.start, units, heads_width))

        def last_tile(i):
            yield from from_normed(i)
            yield from from_low(i)

        fill(3, last_tile, lines, stage, line.places - 1)
        for c in range(chunks):
            swap4.scatter_forward(c)
            if c == soon - 1:
                tick(2, 1, lines)
                for early in range(soon):
                    swap2.gather_pass(early, False)
        line.arrived(1)
        for item in x_loads:
            item.wait()
        for c in range(chunks):
            local = swap4.local(c)
            d_normed = swap4.scatter_result(c)
            x = w_out[local, :].astype(F32)
            scale = inverse_norm(x)
            add_to(in_part, jnp.sum(d_normed * (x * scale), axis=0, keepdims=True), c == 0)
            value = resid[local, :] + rows_back(d_normed * in_gain_ref[...], x, scale)
            grad[swap4.rows(0, c), :] = value.astype(LOW)
            if c == chunks - 1:
                spread.copy(0).start()
            swap4.gather_start(c)
            own4[c].start()
        steps = len(spread.steps)
        for c in range(chunks):
            swap4.gather_pass(c, False)
            if c >= soon:
                swap2.gather_start(c)
            if c == 0:
                line.arrived(2)
            if c == soon:
                tick(3, 0, lines)
        spread.next(0)
        tick(3, 1, lines)
        for step in range(1, steps):
            spread.next(step)
        spread.far_start()
        for c in range(soon, chunks):
            swap2.gather_pass(c, False)
        for step in range(1, line.places - 1):
            spread.pass_on(step, "start")
        for swap in (swap4, swap2):
            for c in range(chunks):
                swap.gather_pass(c, True)
        line.arrived(3)
        spread.pass_on(line.places - 1, "start")
        gains_out[...] = spread.result()
        for item in own2 + own4:
            item.wait()
        for c in range(chunks):
            swap3.gather_end(c)
            for swap in (swap2, swap4):
                swap.scatter_end(c)
                swap.gather_end(c)
        for group in range(line.groups):
            line.end(group)
        spread.end()

    def both(wd):
        pl.run_scoped(
            functools.partial(front, wd),
            pltpu.VMEM((width, units), LOW),
            pltpu.VMEM((width, units), LOW),
            pltpu.VMEM((chunk, heads_width), F32),
            pltpu.VMEM((chunk, keys_width), F32),
        )
        pl.run_scoped(functools.partial(middle, wd), lines, stage)

    lines = pltpu.VMEM((2, 2, line.tile, line.width), LOW)
    stage = pltpu.VMEM((AWAY, line.tile, line.width), LOW)
    pl.run_scoped(both, pltpu.VMEM((units, width), LOW))
    pl.run_scoped(
        rest,
        lines,
        stage,
        pltpu.VMEM(resid.shape, F32),
        pltpu.VMEM((rows_all, heads_width), F32),
        pltpu.VMEM((rows_all, keys_width), F32),
        pltpu.VMEM((rows_all, head_width), F32),
        pltpu.VMEM((rows_all, head_width), F32),
    )


def layer_call(counts, sizes, length, gains, tokens, out_grad, tables, attn_weights, feed_weights):
    tensor_count, dp_count = counts
    q_block, head_width, pairs, group_size = sizes
    rows, width = tokens.shape
    units = feed_weights[0].shape[1]
    heads_width, keys_width = attn_weights[0].shape[1], attn_weights[1].shape[1]
    tile = width // dp_count
    swaps = [Swap(tensor_count, rows, width) for _ in range(4)]
    line = Line(dp_count, 4, tile, units)
    spread = Spread(counts, 2 * width + 2 * head_width)
    chunks = swaps[0].chunks
    wide = jax.ShapeDtypeStruct((rows, width), LOW)
    out_shape = (
        wide,
        wide,
        jax.ShapeDtypeStruct((1, spread.length), F32),
        *line.outputs(),
        wide,
        jax.ShapeDtypeStruct((rows, 2 * heads_width + 2 * keys_width), LOW),
        jax.ShapeDtypeStruct((rows, heads_width), F32),
        jax.ShapeDtypeStruct((rows, keys_width), F32),
        jax.ShapeDtypeStruct((chunks * swaps[0].block, width), F32),
    )
    big = pltpu.VMEM((rows, width), LOW)
    inner = pltpu.VMEM((rows, units), LOW)
    return pl.pallas_call(
        functools.partial(layer_kernel, (*swaps, line, spread, sizes)),
        out_shape=out_shape,
        in_specs=[pl.BlockSpec(memory_space=pltpu.SMEM)] + [vmem_spec()] * 4 + [any_spec()] * 11,
        out_specs=(any_spec(),) * 2 + (vmem_spec(),) + (any_spec(),) * 8,
        scratch_shapes=[
            big,
            big,
            inner,
            inner,
            inner,
            big,
            big,
            pltpu.VMEM((chunks * swaps[0].block, width), F32),
            pltpu.VMEM((tile, rows), LOW),
            swaps[0].landing(),
            pltpu.VMEM((width, heads_width), LOW),
            pltpu.VMEM((width, keys_width), LOW),
            pltpu.VMEM((width, keys_width), LOW),
            pltpu.VMEM((heads_width, width), LOW),
            pltpu.VMEM((rows, head_width), F32),
            pltpu.VMEM((rows, head_width), F32),
            pltpu.VMEM((pairs, rows // q_block, 1, group_size * q_block), F32),
            pltpu.SemaphoreType.DMA((10,)),
            pltpu.SemaphoreType.DMA((chunks,)),
            pltpu.SemaphoreType.DMA((4 + chunks,)),
            pltpu.SemaphoreType.DMA((2, chunks)),
            pltpu.SemaphoreType.REGULAR,
            *[item for swap in swaps for item in swap.semaphores()],
            *line.semaphores(),
            *spread.scratch(),
        ],
        compiler_params=kernel_params(0),
        name="layer",
    )(length, *gains, tokens, out_grad, *tables, *attn_weights, *feed_weights)[:6]


def results_kernel(sizes, *refs):
    places, pieces, cuts, gain_cuts = sizes
    refs = iter(refs)

    def take(count):
        return [next(refs) for _ in range(count)]

    output, in_grad, gains, acc, land = take(5)
    output_out, in_grad_out = take(2)
    gain_outs = take(len(gain_cuts))
    down_out, gate_out, up_out, query_out, key_out, value_out, proj_out = take(7)
    own, sides, total, turned, held, come_sems, go_sems, load_sems, store_sems = take(9)
    place = lax.axis_index("dp") // 2
    groups, rows = own.shape[0], output.shape[0] // pieces

    come, go = [], []
    for which, (src, dst) in enumerate(((output, output_out), (in_grad, in_grad_out))):
        for i in range(pieces):
            at = pl.ds(i * rows, rows)
            spot = held.at[which, at]
            come.append(pltpu.make_async_copy(src.at[at], spot, come_sems.at[which, i]))
            go.append(pltpu.make_async_copy(spot, dst.at[at], go_sems.at[which, i]))

    def load(group, side):
        if side == 0:
            source, target = acc.at[group, place], own.at[group]
        else:
            slot = place if side == 1 else places
            source, target = land.at[group, slot], sides.at[group, side - 1]
        return pltpu.make_async_copy(source, target, load_sems.at[group, side])

    present = (None, place > 0, place < places - 1)
    for group in range(groups):
        load(group, 0).start()
        for side in (1, 2):
            pl.when(present[side])(lambda group=group, side=side: load(group, side).start())
    for item in come:
        item.start()
    start = 0
    for out, size in zip(gain_outs, gain_cuts):
        out[...] = gains[:, pl.ds(start, size)]
        start += size
    stores = []
    q_at, k_at, v_at, o_at = cuts

    def put(src, dst):
        stores.append(pltpu.make_async_copy(src, dst, store_sems.at[len(stores)]))
        stores[-1].start()

    for group in range(groups):
        load(group, 0).wait()
        total[group] = own[group].astype(F32)
        for side in (1, 2):

            @pl.when(present[side])
            def _(group=group, side=side):
                load(group, side).wait()
                total[group] += sides[group, side - 1].astype(F32)

        for i in range(group * len(come) // groups, (group + 1) * len(come) // groups):
            come[i].wait()
            go[i].start()
        if group == 0:
            turned[...] = total[0].T
            put(turned, down_out)
        elif group == 1:
            put(total.at[1], gate_out)
        elif group == 2:
            put(total.at[2], up_out)
        else:
            put(total.at[3, :, q_at], query_out)
            put(total.at[3, :, k_at], key_out)
            put(total.at[3, :, v_at], value_out)
            proj_out[...] = total[3, :, o_at].T
    for item in stores + go:
        item.wait()


def results(places, head_width, heads_width, keys_width, made):
    output, in_grad, gains, _, acc, land = made
    rows, width = output.shape
    tile, units = acc.shape[2:]
    pieces = 4
    cuts = (
        pl.ds(0, heads_width),
        pl.ds(heads_width, keys_width),
        pl.ds(heads_width + keys_width, keys_width),
        pl.ds(heads_width + 2 * keys_width, heads_width),
    )
    gain_cuts = (width, width, head_width, head_width)
    shapes = [(1, size) for size in gain_cuts]
    shapes += [(units, tile), (tile, units), (tile, units), (tile, heads_width)]
    shapes += [(tile, keys_width), (tile, keys_width), (heads_width, tile)]
    return pl.pallas_call(
        functools.partial(results_kernel, (places, pieces, cuts, gain_cuts)),
        out_shape=(
            jax.ShapeDtypeStruct(output.shape, LOW),
            jax.ShapeDtypeStruct(output.shape, LOW),
            *[jax.ShapeDtypeStruct(shape, F32) for shape in shapes],
        ),
        in_specs=[any_spec()] * 2 + [vmem_spec()] + [any_spec()] * 2,
        out_specs=(any_spec(),) * 2 + (vmem_spec(),) * 4 + (any_spec(),) * 6 + (vmem_spec(),),
        scratch_shapes=[
            pltpu.VMEM((4, tile, units), LOW),
            pltpu.VMEM((4, 2, tile, units), LOW),
            pltpu.VMEM((4, tile, units), F32),
            pltpu.VMEM((units, tile), F32),
            pltpu.VMEM((2, rows, width), LOW),
            pltpu.SemaphoreType.DMA((2, pieces)),
            pltpu.SemaphoreType.DMA((2, pieces)),
            pltpu.SemaphoreType.DMA((4, 3)),
            pltpu.SemaphoreType.DMA((6,)),
        ],
        compiler_params=pltpu.CompilerParams(vmem_limit_bytes=VMEM_BYTES),
        name="results",
    )(output, in_grad, gains, acc, land)


def rope_tables(head_width, row_count):
    half_width = head_width // 2
    inv_freq = ROPE_BASE ** (-2.0 * np.arange(half_width, dtype=np.float32) / head_width)
    angles = np.arange(row_count, dtype=np.float32)[:, None] * inv_freq.astype(np.float32)[None, :]
    cosine, sine = np.cos(angles), np.sin(angles)
    tables = np.concatenate([cosine, cosine], 1), np.concatenate([-sine, sine], 1)
    return tuple(jnp.asarray(table, F32) for table in tables)


def on_device(
    tensor_count,
    dp_count,
    tokens,
    lengths,
    in_gain,
    w_query,
    w_key,
    w_value,
    query_gain,
    key_gain,
    w_out,
    post_gain,
    w_gate,
    w_up,
    w_down,
    out_grad,
):
    head_width = query_gain.shape[0]
    pairs = w_key.shape[1] // head_width
    group_size = w_query.shape[1] // w_key.shape[1]
    q_block = min(128, tokens.shape[0])
    made = layer_call(
        (tensor_count, dp_count),
        (q_block, head_width, pairs, group_size),
        lengths,
        (in_gain[None], post_gain[None], query_gain[None], key_gain[None]),
        tokens,
        out_grad,
        rope_tables(head_width, tokens.shape[0]),
        (w_query, w_key, w_value, w_out),
        (w_gate, w_up, w_down),
    )
    (
        output,
        in_grad,
        grad_post_gain,
        grad_in_gain,
        grad_query_gain,
        grad_key_gain,
        grad_down,
        grad_gate,
        grad_up,
        grad_query,
        grad_key,
        grad_value,
        grad_out,
    ) = results(dp_count // 2, head_width, w_query.shape[1], w_key.shape[1], made)
    return (
        output,
        in_grad,
        grad_in_gain[0],
        grad_query,
        grad_key,
        grad_value,
        grad_query_gain[0],
        grad_key_gain[0],
        grad_out,
        grad_post_gain[0],
        grad_gate,
        grad_up,
        grad_down,
    )


def solution(mesh):
    tensor_count, dp_count = mesh.shape["tensor"], mesh.shape["dp"]

    def layer(*args):
        return on_device(tensor_count, dp_count, *args)

    return jax.shard_map(
        layer,
        mesh=mesh,
        in_specs=(
            P("dp", None),
            P("dp"),
            P(),
            P(None, "tensor"),
            P(None, "tensor"),
            P(None, "tensor"),
            P(),
            P(),
            P("tensor", None),
            P(),
            P(None, "tensor"),
            P(None, "tensor"),
            P("tensor", None),
            P("dp", None),
        ),
        out_specs=(
            P("dp", None),
            P("dp", None),
            P(),
            P("dp", "tensor"),
            P("dp", "tensor"),
            P("dp", "tensor"),
            P(),
            P(),
            P("tensor", "dp"),
            P(),
            P("dp", "tensor"),
            P("dp", "tensor"),
            P("tensor", "dp"),
        ),
        check_vma=False,
    )
```

```python
import functools

import jax
import jax.numpy as jnp
import numpy as np
from jax import lax
from jax.experimental import pallas as pl
from jax.experimental.pallas import tpu as pltpu
from jax.sharding import PartitionSpec as P

NORM_EPS = 1e-06
ROPE_BASE = 1000000.0
MASK_FILL = -1e30
LOW = jnp.bfloat16
F32 = jnp.float32
MESH = pl.DeviceIdType.MESH
VMEM_BYTES = 65408 * 1024
CHUNK = 256
KEYS = 256
AWAY = 3


def unit_rows(matrix):
    return matrix * lax.rsqrt(jnp.mean(matrix * matrix, axis=-1, keepdims=True) + NORM_EPS)


def dot_nn(left, right):
    return jnp.dot(left, right, preferred_element_type=F32)


def dot_tn(left, right):
    return lax.dot_general(left, right, (((0,), (0,)), ((), ())), preferred_element_type=F32)


def dot_nt(left, right):
    return lax.dot_general(left, right, (((1,), (1,)), ((), ())), preferred_element_type=F32)


class Swap:
    def __init__(self, count, rows, width):
        self.count, self.width = count, width
        self.bits = count.bit_length() - 1
        self.chunk = min(CHUNK, rows)
        self.chunks = rows // self.chunk
        self.block = self.chunk // count
        self.half = width // 2
        self.orders = [list(range(self.bits)), list(range(self.bits))[::-1]]
        self.slots = []
        for order in self.orders:
            slot = {}
            for step in range(self.bits):
                for r in range(count):
                    if not any(r >> b & 1 for b in order[: step + 1]):
                        slot[step, r] = len(slot)
            self.slots.append(slot)

    def landing(self):
        return pltpu.VMEM((2, self.count - 1, self.chunks * self.block, self.half), LOW)

    def semaphores(self):
        n, c = self.count, self.chunks
        return [
            pltpu.SemaphoreType.DMA((2, n, c)),
            pltpu.SemaphoreType.DMA((2, n, c)),
            pltpu.SemaphoreType.DMA((2, n * self.bits, c)),
            pltpu.SemaphoreType.DMA((2, n, c)),
        ]

    def bind(self, part, recv, dest, sems, own=None):
        self.part, self.recv, self.dest, self.sems = part, recv, dest, sems
        self.own = dest if own is None else own
        self.me = lax.axis_index("tensor")
        return self

    def near(self, bit):
        own = (self.me // 2**bit) % 2
        return self.me + (1 - 2 * own) * 2**bit

    def rows(self, r, c):
        owner = self.me
        for bit in range(self.bits):
            if r >> bit & 1:
                owner = owner + (1 - 2 * ((self.me // 2**bit) % 2)) * 2**bit
        return pl.ds(pl.multiple_of(c * self.chunk + owner * self.block, self.block), self.block)

    def local(self, c):
        return pl.ds(c * self.block, self.block)

    def columns(self, half):
        return pl.ds(half * self.half, self.half)

    def signal(self, sem):
        for bit in range(self.bits):
            pl.semaphore_signal(
                sem, inc=1, device_id={"tensor": self.near(bit)}, device_id_type=MESH
            )

    def order(self):
        return sorted(range(1, self.count), key=lambda r: (-bin(r).count("1"), r))

    def first(self, half, r):
        return next(k for k, bit in enumerate(self.orders[half]) if r >> bit & 1)

    def scatter_copy(self, half, r, c):
        step = self.first(half, r)
        bit = self.orders[half][step]
        slot = self.slots[half][step, r ^ (1 << bit)]
        return pltpu.make_async_remote_copy(
            src_ref=self.part.at[self.rows(r, c), self.columns(half)],
            dst_ref=self.recv.at[half, slot, self.local(c)],
            send_sem=self.sems[0].at[half, r, c],
            recv_sem=self.sems[1].at[half, slot, c],
            device_id={"tensor": self.near(bit)},
            device_id_type=MESH,
        )

    def scatter_wait(self, half, step, r, c):
        slot = self.slots[half][step, r]
        ref = self.recv.at[half, slot, self.local(c)]
        pltpu.make_async_copy(ref, ref, self.sems[1].at[half, slot, c]).wait()
        return ref

    def scatter_start(self, c):
        for r in self.order():
            for half in range(2):
                if self.first(half, r) == 0:
                    self.scatter_copy(half, r, c).start()

    def scatter_forward(self, c):
        todo = [
            (self.first(half, r), half, r)
            for half in range(2)
            for r in range(1, self.count)
            if self.first(half, r) > 0
        ]
        for step, half, r in sorted(todo):
            where = self.rows(r, c), self.columns(half)
            total = self.part[where].astype(F32)
            for j in range(step):
                total = total + self.scatter_wait(half, j, r, c)[...].astype(F32)
            self.part[where] = total.astype(LOW)
            self.scatter_copy(half, r, c).start()

    def scatter_result(self, c):
        total = []
        for half in range(2):
            value = self.part[self.rows(0, c), self.columns(half)].astype(F32)
            for j in range(self.bits):
                value = value + self.scatter_wait(half, j, 0, c)[...].astype(F32)
            total.append(value)
        return jnp.concatenate(total, axis=1)

    def scatter_end(self, c):
        for half in range(2):
            for r in range(1, self.count):
                self.scatter_copy(half, r, c).wait_send()

    def last(self, half, r):
        order = self.orders[half][::-1]
        return max([-1] + [j for j, bit in enumerate(order) if r >> bit & 1])

    def gather_copy(self, half, r, step, c):
        bit = self.orders[half][::-1][step]
        where = self.rows(r, c), self.columns(half)
        return pltpu.make_async_remote_copy(
            src_ref=self.dest.at[where] if r else self.own.at[where],
            dst_ref=self.dest.at[where],
            send_sem=self.sems[2].at[half, r * self.bits + step, c],
            recv_sem=self.sems[3].at[half, r ^ (1 << bit), c],
            device_id={"tensor": self.near(bit)},
            device_id_type=MESH,
        )

    def gather_start(self, c):
        for step in range(self.bits):
            for half in range(2):
                self.gather_copy(half, 0, step, c).start()

    def gather_pass(self, c, late):
        todo = [
            (self.last(half, r), bin(r).count("1"), half, r)
            for half in range(2)
            for r in range(1, self.count)
        ]
        for step, _, half, r in sorted(todo):
            if (step == self.bits - 1) != late:
                continue
            ref = self.dest.at[self.rows(r, c), self.columns(half)]
            pltpu.make_async_copy(ref, ref, self.sems[3].at[half, r, c]).wait()
            for later in range(step + 1, self.bits):
                self.gather_copy(half, r, later, c).start()

    def gather_end(self, c):
        for half in range(2):
            for r in range(self.count):
                for step in range(self.last(half, r) + 1, self.bits):
                    self.gather_copy(half, r, step, c).wait_send()


class Line:
    def __init__(self, count, groups, tile, width):
        self.count, self.groups, self.tile, self.width = count, groups, tile, width
        self.places = count // 2

    def outputs(self):
        shape = (self.tile, self.width)
        return [
            jax.ShapeDtypeStruct((self.groups, self.places) + shape, LOW),
            jax.ShapeDtypeStruct((self.groups, self.places) + shape, LOW),
            jax.ShapeDtypeStruct((self.groups, self.places + 1) + shape, LOW),
        ]

    def semaphores(self):
        g, n = self.groups, self.places
        return [
            pltpu.SemaphoreType.DMA((g, n)),
            pltpu.SemaphoreType.DMA((g, n)),
            pltpu.SemaphoreType.DMA((2,)),
            pltpu.SemaphoreType.DMA((2, g, n)),
            pltpu.SemaphoreType.DMA((g, n + 1)),
            pltpu.SemaphoreType.DMA((6,)),
        ]

    def bind(self, core_land, acc, land, sems):
        self.core_land, self.acc, self.land = core_land, acc, land
        (
            self.core_send,
            self.core_recv,
            self.store_sem,
            self.line_send,
            self.line_recv,
            self.local_sem,
        ) = sems
        self.me = lax.axis_index("dp")
        self.place = self.me // 2
        self.core = self.me % 2
        self.other = self.me + 1 - 2 * self.core
        return self

    def signal(self, sem):
        @pl.when(self.place > 0)
        def _():
            pl.semaphore_signal(sem, inc=1, device_id={"dp": self.me - 2}, device_id_type=MESH)

        @pl.when(self.place < self.places - 1)
        def _():
            pl.semaphore_signal(sem, inc=1, device_id={"dp": self.me + 2}, device_id_type=MESH)

    def peers(self):
        ends = (self.places - 1 - self.place) // (self.places - 1) + self.place // (self.places - 1)
        return 2 - ends

    def core_copy(self, group, i, source):
        return pltpu.make_async_remote_copy(
            src_ref=source,
            dst_ref=self.core_land.at[group, i],
            send_sem=self.core_send.at[group, i],
            recv_sem=self.core_recv.at[group, i],
            device_id={"dp": self.other},
            device_id_type=MESH,
        )

    def fill(self, group, tile_of, away, away_slots, home, came, spots):
        n = self.places
        low_side = 1 - self.place // ((n + 1) // 2)

        def which(i):
            return i + low_side * (n - 1 - 2 * i)

        def send(i):
            slot = lax.rem(i, away_slots)

            @pl.when(i >= away_slots)
            def _():
                self.core_copy(group, which(i - away_slots), away(slot)).wait_send()

            for cols, value in tile_of(2 * which(i) + 1 - self.core):
                away(slot)[:, cols] = value.astype(LOW)
            self.core_copy(group, which(i), away(slot)).start()

        def store(i):
            slot = lax.rem(i, 2)
            return pltpu.make_async_copy(
                home(slot), self.acc.at[group, which(i)], self.store_sem.at[slot]
            )

        def fetch(i):
            slot = lax.rem(i, 2)
            return pltpu.make_async_copy(
                self.core_land.at[group, which(i)], came(slot), self.local_sem.at[slot]
            )

        def arrive(i):
            landed = self.core_land.at[group, which(i)]
            pltpu.make_async_copy(landed, landed, self.core_recv.at[group, which(i)]).wait()
            fetch(i).start()

        def done(i):
            store(i).wait()
            j = which(i)
            for way, end in ((0, 0), (1, n - 1)):

                @pl.when(jnp.logical_and(self.place == end, i < spots))
                def _(way=way):
                    self.line_copy(group, way, j, self.acc.at[group, j]).start()

        def keep(i):
            slot = lax.rem(i, 2)
            for spot, (cols, value) in enumerate(tile_of(2 * which(i) + self.core)):
                if spot == 0:
                    fetch(i).wait()
                home(slot)[:, cols] = (value + came(slot)[:, cols].astype(F32)).astype(LOW)

            store(i).start()

        def both(i, carry):
            @pl.when(i < n)
            def _():
                send(i)

            @pl.when(jnp.logical_and(i >= 3, i < n))
            def _():
                done(i - 3)

            @pl.when(jnp.logical_and(i >= 1, i <= n))
            def _():
                arrive(i - 1)

            @pl.when(i >= 2)
            def _():
                keep(i - 2)

            @pl.when(jnp.logical_and(i >= 3, i >= n))
            def _():
                done(i - 3)

            return carry

        lax.fori_loop(0, n + 2, both, 0)
        done(n - 1)
        for i in range(max(0, n - away_slots), n):
            self.core_copy(group, which(i), away(i % away_slots)).wait_send()

    def line_copy(self, group, way, j, source):
        if way == 0:
            slot, to = j, self.me + 2
        else:
            final = 1 - jnp.minimum(self.place - 1 - j, 1)
            slot, to = j + final * (self.places - j), self.me - 2
        return pltpu.make_async_remote_copy(
            src_ref=source,
            dst_ref=self.land.at[group, slot],
            send_sem=self.line_send.at[way, group, j],
            recv_sem=self.line_recv.at[group, slot],
            device_id={"dp": to},
            device_id_type=MESH,
        )

    def ends(self, group, act, spots):
        n = self.places

        @pl.when(self.place == 0)
        def _():
            for spot in spots:
                j = n - 1 - spot
                copy = self.line_copy(group, 0, j, self.acc.at[group, j])
                copy.start() if act == "start" else copy.wait_send()

        @pl.when(self.place == n - 1)
        def _():
            for j in spots:
                copy = self.line_copy(group, 1, j, self.acc.at[group, j])
                copy.start() if act == "start" else copy.wait_send()

    def landed(self, group, slot):
        ref = self.land.at[group, slot]
        pltpu.make_async_copy(ref, ref, self.line_recv.at[group, slot]).wait()
        return ref

    def on_way(self, step, way):
        far = self.place if way == 0 else self.places - 1 - self.place
        index = self.places - 1 - step + self.place if way == 0 else step - far
        return jnp.logical_and(far >= 1, far <= step), index

    def tick(self, group, step, lines):
        ways = [self.on_way(step, way) for way in range(2)]

        def here(way):
            return pltpu.make_async_copy(
                self.acc.at[group, ways[way][1]], lines.at[way, 0], self.local_sem.at[2 * way]
            )

        def there(way):
            return pltpu.make_async_copy(
                self.land.at[group, ways[way][1]], lines.at[way, 1], self.local_sem.at[2 * way + 1]
            )

        def back(way):
            return pltpu.make_async_copy(
                lines.at[way, 0], self.acc.at[group, ways[way][1]], self.local_sem.at[2 * way]
            )

        def come(way):
            here(way).start()
            self.landed(group, ways[way][1])
            there(way).start()

        def add(way):
            here(way).wait()
            there(way).wait()
            lines[way, 0] = (lines[way, 0].astype(F32) + lines[way, 1].astype(F32)).astype(LOW)
            back(way).start()

        def go(way):
            back(way).wait()
            j = ways[way][1]
            self.line_copy(group, way, j, self.acc.at[group, j]).start()

        for act in (come, add, go):
            for way in range(2):
                pl.when(ways[way][0])(functools.partial(act, way))

    def end(self, group):
        for step in range(1, self.places - 1):
            for way in range(2):
                active, j = self.on_way(step, way)

                @pl.when(active)
                def _(way=way, j=j):
                    self.line_copy(group, way, j, self.acc.at[group, j]).wait_send()

        self.ends(group, "wait", range(self.places - 1))

    def arrived(self, group):
        for present, slot in ((self.place > 0, self.place), (self.place < self.places - 1, self.places)):
            pl.when(present)(lambda slot=slot: self.landed(group, slot) and None)


class Spread:
    def __init__(self, counts, length):
        tensor_count, dp_count = counts
        self.length, self.places = length, dp_count // 2
        self.steps = [("tensor", 2**b) for b in range(tensor_count.bit_length() - 1)]
        self.steps.append(("dp", 1))

    def scratch(self):
        n = len(self.steps)
        return [
            pltpu.VMEM((n + 1, 1, self.length), F32),
            pltpu.VMEM((n, 1, self.length), F32),
            pltpu.VMEM((self.places, 1, self.length), F32),
            pltpu.SemaphoreType.DMA((n,)),
            pltpu.SemaphoreType.DMA((n,)),
            pltpu.SemaphoreType.DMA((2, self.places)),
            pltpu.SemaphoreType.DMA((self.places,)),
        ]

    def bind(self, mine, land, far, send, recv, far_send, far_recv):
        self.mine, self.land, self.far = mine, land, far
        self.send, self.recv, self.far_send, self.far_recv = send, recv, far_send, far_recv
        self.me = lax.axis_index("dp")
        self.place = self.me // 2
        return self

    def partner(self, step):
        axis, size = self.steps[step]
        me = lax.axis_index(axis)
        return {axis: me + (1 - 2 * ((me // size) % 2)) * size}

    def signal(self, sem):
        for step in range(len(self.steps)):
            pl.semaphore_signal(
                sem, inc=1, device_id=self.partner(step), device_id_type=MESH
            )

    def copy(self, step):
        return pltpu.make_async_remote_copy(
            src_ref=self.mine.at[step],
            dst_ref=self.land.at[step],
            send_sem=self.send.at[step],
            recv_sem=self.recv.at[step],
            device_id=self.partner(step),
            device_id_type=MESH,
        )

    def next(self, step):
        self.copy(step).wait()
        self.mine[step + 1] = self.mine[step] + self.land[step]
        if step + 1 < len(self.steps):
            self.copy(step + 1).start()

    def far_copy(self, way, place):
        return pltpu.make_async_remote_copy(
            src_ref=self.far.at[place],
            dst_ref=self.far.at[place],
            send_sem=self.far_send.at[way, place],
            recv_sem=self.far_recv.at[place],
            device_id={"dp": self.me + 2 - 4 * way},
            device_id_type=MESH,
        )

    def pass_on(self, hops, act):
        n = self.places
        for way in range(2):
            place = self.place - hops if way == 0 else self.place + hops
            here = place >= 0 if way == 0 else place < n
            onward = self.place < n - 1 if way == 0 else self.place > 0
            if hops and act == "start":

                @pl.when(here)
                def _(place=place):
                    ref = self.far.at[place]
                    pltpu.make_async_copy(ref, ref, self.far_recv.at[place]).wait()

            @pl.when(jnp.logical_and(here, onward))
            def _(place=place, way=way):
                copy = self.far_copy(way, place)
                copy.start() if act == "start" else copy.wait_send()

    def far_start(self):
        self.far[self.place] = self.mine[len(self.steps)]
        self.pass_on(0, "start")

    def result(self):
        total = self.far[0]
        for place in range(1, self.places):
            total = total + self.far[place]
        return total

    def end(self):
        for hops in range(self.places - 1):
            self.pass_on(hops, "end")


def unrolled(total, size, body):
    for start in range(0, total, size):
        body(pl.ds(start, size))


def tiled(total, size, body):
    count = total // size

    def step(i, carry):
        body(pl.ds(pl.multiple_of(i * size, size), size))
        return carry

    lax.fori_loop(0, count, step, 0)


def any_spec():
    return pl.BlockSpec(memory_space=pl.ANY)


def vmem_spec():
    return pl.BlockSpec(memory_space=pltpu.VMEM)


def kernel_params(identity):
    return pltpu.CompilerParams(
        collective_id=identity, has_side_effects=True, vmem_limit_bytes=VMEM_BYTES
    )


def head_forward(raw, cosine, sine, gain):
    width = raw.shape[-1]
    unit = raw * lax.rsqrt(jnp.mean(raw * raw, axis=-1, keepdims=True) + NORM_EPS) * gain
    return (unit * cosine + pltpu.roll(unit, width // 2, 1) * sine).astype(LOW)


def head_back(grad, raw, cosine, sine, gain):
    width = raw.shape[-1]
    turned = grad * cosine - pltpu.roll(grad, width // 2, 1) * sine
    scale = lax.rsqrt(jnp.mean(raw * raw, axis=-1, keepdims=True) + NORM_EPS)
    unit = raw * scale
    gain_sum = jnp.sum(turned * unit, axis=0, keepdims=True)
    inner = turned * gain
    return scale * (inner - unit * jnp.mean(inner * unit, axis=-1, keepdims=True)), gain_sum


def rows_back(d_unit, rows, scale):
    unit = rows * scale
    return scale * (d_unit - unit * jnp.mean(d_unit * unit, axis=-1, keepdims=True))


def inverse_norm(rows):
    return lax.rsqrt(jnp.mean(rows * rows, axis=-1, keepdims=True) + NORM_EPS)


def layer_kernel(plan, *refs):
    swap1, swap3, swap2, swap4, line, spread, sizes = plan
    q_block, head_width, pairs, group_size = sizes
    refs = iter(refs)

    def take(count):
        return [next(refs) for _ in range(count)]

    length_ref, in_gain_ref, post_gain_ref, query_gain_ref, key_gain_ref = take(5)
    tokens_hbm, grad_hbm, cos_hbm, sin_hbm = take(4)
    w_query_hbm, w_key_hbm, w_value_hbm, w_out_hbm = take(4)
    wg_hbm, wu_hbm, wd_hbm = take(3)
    output, in_grad, gains_out = take(3)
    core_land, acc, land, normed_hbm, heads_hbm, q_raw_hbm, k_raw_hbm, resid_hbm = take(8)
    hidden, grad, act, dg, du, part, low, resid, flip, recv = take(10)
    w_query, w_key, w_value, w_out, cosine, sine, lse = take(7)
    in_sems, token_sems, front_sems, own_sems, free_sem = take(5)
    swap1.bind(part, recv, hidden, take(4))
    swap3.bind(part, recv, low, take(4))
    swap2.bind(part, recv, output, take(4), own=part)
    swap4.bind(grad, recv, in_grad, take(4), own=grad)
    line.bind(core_land, acc, land, take(6))
    spread.bind(*take(7))

    rows_all, units = act.shape
    width = swap1.width
    heads_width, keys_width = w_query.shape[1], w_key.shape[1]
    unit_tile = 256
    chunk, chunks = swap1.chunk, swap1.chunks
    score_scale = head_width ** (-0.5)
    lanes = group_size * q_block
    length = length_ref[0]
    post_part = spread.mine.at[0, :, pl.ds(0, width)]
    in_part = spread.mine.at[0, :, pl.ds(width, width)]
    query_part = spread.mine.at[0, :, pl.ds(2 * width, head_width)]
    key_part = spread.mine.at[0, :, pl.ds(2 * width + head_width, head_width)]
    q_at = pl.ds(0, heads_width)
    k_at = pl.ds(heads_width, keys_width)
    v_at = pl.ds(heads_width + keys_width, keys_width)
    o_at = pl.ds(heads_width + 2 * keys_width, heads_width)

    def head_at(base, i):
        return pl.ds(base.start + i * head_width, head_width)

    def load(i, src, dst):
        return pltpu.make_async_copy(src, dst, in_sems.at[i])

    def chunk_rows(c):
        return pl.ds(c * chunk, chunk)

    def valid(rows):
        return rows.start + lax.broadcasted_iota(jnp.int32, (rows.size, 1), 0) < length

    def stacked(ref, rows, base, c):
        return jnp.concatenate(
            [ref[rows, head_at(base, c * group_size + i)] for i in range(group_size)], axis=0
        )

    def allowed_of(block, start, stop):
        k_pos = start + lax.broadcasted_iota(jnp.int32, (stop - start, lanes), 0)
        q_pos = block * q_block + lax.rem(
            lax.broadcasted_iota(jnp.int32, (1, lanes), 1), q_block
        )
        return k_pos < jnp.minimum(q_pos + 1, length)

    def tile_cols(i):
        return pl.ds(pl.multiple_of(i * line.tile, line.tile), line.tile)

    def products(left, right, cuts):
        def tile_of(i):
            flip[...] = left[:, tile_cols(i)].T
            for start in range(*cuts):
                cols = pl.ds(start, cuts[2])
                yield cols, dot_nn(flip[...], right[:, cols])

        return tile_of

    middle_step = line.places // 2

    def tick(group, half, lines):
        for step in (range(1, middle_step), range(middle_step, line.places - 1))[half]:
            line.tick(group, step, lines)

    def add_to(ref, value, first):
        if first:
            ref[...] = value
        else:
            ref[...] += value


    def front(wd, wg, wu, q_raw, k_raw):
        attn_loads = [
            load(0, w_query_hbm, w_query),
            load(1, w_key_hbm, w_key),
            load(2, w_value_hbm, w_value),
            load(3, cos_hbm, cosine),
            load(4, sin_hbm, sine),
            load(5, w_out_hbm, w_out),
        ]
        feed_loads = [
            load(8, grad_hbm, grad),
            load(9, wd_hbm, wd),
            load(6, wg_hbm, wg),
            load(7, wu_hbm, wu),
        ]
        token_loads = [
            pltpu.make_async_copy(
                tokens_hbm.at[chunk_rows(c)], low.at[chunk_rows(c)], token_sems.at[c]
            )
            for c in range(chunks)
        ]
        for item in token_loads[:1] + attn_loads + token_loads[1:] + feed_loads:
            item.start()
        barrier = pltpu.get_barrier_semaphore()
        spread.signal(barrier)
        line.signal(barrier)
        pl.semaphore_wait(barrier, len(spread.steps) + line.peers())

        def front_store(i, src, dst):
            return pltpu.make_async_copy(src, dst, front_sems.at[i])

        raw_stores = []

        def attend(c):
            rows = chunk_rows(c)
            token_loads[c].wait()

            def norm_step(local):
                at = pl.ds(c * chunk + local.start, local.size)
                x = low[at, :].astype(F32)
                hidden[at, :] = (unit_rows(x) * in_gain_ref[...]).astype(LOW)

            tiled(chunk, 32, norm_step)
            store = front_store(0, hidden.at[rows], normed_hbm.at[rows])
            store.start()
            if c == 0:
                for item in attn_loads:
                    item.wait()
            for item in raw_stores:
                item.wait()
            raw_stores.clear()
            q_raw[...] = dot_nn(hidden[rows, :], w_query[...])
            k_raw[...] = dot_nn(hidden[rows, :], w_key[...])
            du[rows, v_at] = dot_nn(hidden[rows, :], w_value[...]).astype(LOW)
            for raw, base, gain in ((q_raw, q_at, query_gain_ref), (k_raw, k_at, key_gain_ref)):
                for i in range(base.size // head_width):
                    du[rows, head_at(base, i)] = head_forward(
                        raw[:, pl.ds(i * head_width, head_width)],
                        cosine[rows, :],
                        sine[rows, :],
                        gain[...],
                    )
            raw_stores.append(front_store(1, q_raw, q_raw_hbm.at[rows]))
            raw_stores.append(front_store(2, k_raw, k_raw_hbm.at[rows]))
            for item in raw_stores:
                item.start()
            for pair in range(pairs):
                for piece in range(chunk // q_block):
                    block = c * (chunk // q_block) + piece
                    q_rows = pl.ds(block * q_block, q_block)
                    end = (block + 1) * q_block
                    queries = stacked(du, q_rows, q_at, pair)
                    peak = total = sums = None
                    for start in range(0, end, KEYS):
                        stop = min(start + KEYS, end)
                        scores = dot_nt(du[start:stop, head_at(k_at, pair)], queries) * score_scale
                        scores = jnp.where(allowed_of(block, start, stop), scores, MASK_FILL)
                        top = jnp.max(scores, axis=0, keepdims=True)
                        new_peak = top if peak is None else jnp.maximum(peak, top)
                        exponent = jnp.exp(scores - new_peak)
                        add = jnp.sum(exponent, axis=0, keepdims=True)
                        more = dot_tn(du[start:stop, head_at(v_at, pair)], exponent.astype(LOW))
                        if peak is None:
                            total, sums = add, more
                        else:
                            shrink = jnp.exp(peak - new_peak)
                            total, sums = total * shrink + add, sums * shrink + more
                        peak = new_peak
                    lse[pair, block] = peak + jnp.log(total)
                    value = (sums * (1.0 / total)).T
                    for i in range(group_size):
                        du[q_rows, head_at(o_at, pair * group_size + i)] = value[
                            i * q_block : (i + 1) * q_block
                        ].astype(LOW)

            def project(cols):
                part[rows, cols] = dot_nn(du[rows, o_at], w_out[:, cols]).astype(LOW)

            unrolled(width, 512, project)
            store.wait()
            swap1.scatter_start(c)

        def settle(c):
            value = low[swap1.rows(0, c), :].astype(F32) + swap1.scatter_result(c)
            resid[swap1.local(c), :] = value
            front_store(4 + c, resid.at[swap1.local(c)], resid_hbm.at[swap1.local(c)]).start()
            hidden[swap1.rows(0, c), :] = (unit_rows(value) * post_gain_ref[...]).astype(LOW)
            swap1.gather_start(c)

        def feed_ahead(c):
            rows = chunk_rows(c)

            def mask_step(local):
                at = pl.ds(c * chunk + local.start, local.size)
                grad[at, :] = jnp.where(valid(at), grad[at, :], jnp.zeros((), LOW))

            tiled(chunk, 32, mask_step)

            def ahead_step(cols):
                dg[rows, cols] = dot_nt(grad[rows, :], wd[cols, :]).astype(LOW)

            unrolled(units, unit_tile * (2 - units // unit_tile % 2), ahead_step)

        def feed_in(c):
            rows = chunk_rows(c)

            def unit_step(cols):
                gate = dot_nn(hidden[rows, :], wg[:, cols])
                up = dot_nn(hidden[rows, :], wu[:, cols])
                d_act = dg[rows, cols].astype(F32)
                sig = jax.nn.sigmoid(gate)
                silu = gate * sig
                act[rows, cols] = (silu * up).astype(LOW)
                dg[rows, cols] = (d_act * up * sig * (1.0 + gate * (1.0 - sig))).astype(LOW)
                du[rows, cols] = (d_act * silu).astype(LOW)

            unrolled(units, unit_tile, unit_step)

        def feed_back(c):
            rows = chunk_rows(c)

            def back_step(cols):
                part[rows, cols] = (
                    dot_nt(dg[rows, :], wg[cols, :]) + dot_nt(du[rows, :], wu[cols, :])
                ).astype(LOW)

            unrolled(width, 512, back_step)

        last = chunks - 1
        for c in range(chunks):
            attend(c)
            if c >= 1:
                swap1.scatter_forward(c - 1)
            if c == min(1, last):
                for item in feed_loads[:2]:
                    item.wait()
                for ahead in range(chunks):
                    feed_ahead(ahead)
            if 1 <= c < last:
                settle(c - 1)
            if 2 <= c < last:
                swap1.gather_pass(c - 2, False)
        heads_store = front_store(3, du, heads_hbm)
        heads_store.start()
        resid_stores = [
            front_store(4 + c, resid.at[swap1.local(c)], resid_hbm.at[swap1.local(c)])
            for c in range(chunks)
        ]
        for item in raw_stores + feed_loads[2:]:
            item.wait()
        if last >= 2:
            swap1.gather_pass(last - 2, False)
        heads_store.wait()
        fed = 0
        if last >= 1:
            swap1.gather_pass(0, True)
            feed_in(0)
            settle(last - 1)
            fed = 1
        swap1.scatter_forward(last)
        if last > 2:
            swap1.gather_pass(1, True)
            feed_in(1)
            fed = 2
        if last >= 1:
            swap1.gather_pass(last - 1, False)
        settle(last)
        swap1.scatter_end(0)
        if fed:
            feed_back(0)
        swap1.gather_pass(last, False)
        for c in range(fed, chunks):
            swap1.gather_pass(c, True)
            feed_in(c)

        def slot_of(ref, first):
            def slot(i):
                start = (first + i) * line.tile
                if not isinstance(i, int):
                    start = pl.multiple_of(start, line.tile)
                return ref.at[pl.ds(start, line.tile), pl.ds(0, units)]

            return slot

        for c in range(1, chunks):
            swap1.scatter_end(c)
        free = chunk // line.tile
        line.fill(
            0,
            products(grad, act, (0, units, unit_tile)),
            slot_of(low, 0),
            2,
            slot_of(part, free),
            slot_of(low, 2),
            line.places - 1,
        )
        for c in range(chunks):
            if c or not fed:
                feed_back(c)
            swap3.scatter_start(c)
            if c:
                swap3.scatter_forward(c - 1)
        for c in range(chunks):
            swap1.gather_end(c)
            resid_stores[c].wait()


    def fill(group, tile_of, lines, stage, spots):
        line.fill(
            group,
            tile_of,
            lambda slot: stage.at[slot],
            AWAY,
            lambda slot: lines.at[0, slot],
            lambda slot: lines.at[1, slot],
            spots,
        )

    def middle(wd, lines, stage):
        def settle3(c):
            d_hidden = swap3.scatter_result(c)
            rows = resid[swap3.local(c), :]
            scale = inverse_norm(rows)
            add_to(post_part, jnp.sum(d_hidden * (rows * scale), axis=0, keepdims=True), c == 0)
            value = grad[swap3.rows(0, c), :].astype(F32) + rows_back(
                d_hidden * post_gain_ref[...], rows, scale
            )
            resid[swap3.local(c), :] = value
            low[swap3.rows(0, c), :] = value.astype(LOW)
            swap3.gather_start(c)

        def mix(c):
            swap3.scatter_end(c)
            rows = chunk_rows(c)

            def mix_step(cols):
                part[rows, cols] = dot_nn(act[rows, :], wd[:, cols]).astype(LOW)

            unrolled(width, 512, mix_step)

        last = chunks - 1
        settle3(0)
        tick(0, 0, lines)
        for c in range(1, last):
            settle3(c)
            if c == 1:
                swap3.scatter_forward(last)
        if last >= 1:
            swap3.gather_pass(0, False)
        fill(1, products(hidden, dg, (0, units, unit_tile)), lines, stage, line.places - 1)
        tick(0, 1, lines)
        if last >= 1:
            settle3(last)
        for c in range(1, last):
            swap3.gather_pass(c, False)
        for c in range(chunks):
            mix(c)
        swap3.gather_pass(last, False)

    def rest(lines, stage, base, q_raw, k_raw, dk, dv):
        raw_loads = [
            load(1, q_raw_hbm, q_raw),
            load(2, k_raw_hbm, k_raw),
            load(3, resid_hbm, base),
        ]
        act_load = load(0, heads_hbm, act)
        for item in raw_loads + [act_load]:
            item.start()
        for c in range(chunks):
            swap3.gather_pass(c, True)
            swap2.scatter_start(c)
            if c == chunks // 2 - 1:
                tick(1, 0, lines)
        fill(2, products(hidden, du, (0, units, unit_tile)), lines, stage, middle_step)
        normed_load = load(4, normed_hbm, hidden)
        normed_load.start()
        tick(1, 1, lines)
        swap2.scatter_forward(0)
        line.arrived(0)
        act_load.wait()

        def d_head_step(rows):
            dg[rows, o_at] = dot_nt(low[rows, :], w_out[...]).astype(LOW)

        unrolled(rows_all, chunk, d_head_step)
        x_loads = [
            pltpu.make_async_copy(
                tokens_hbm.at[swap4.rows(0, c)], w_out.at[swap4.local(c)], token_sems.at[c]
            )
            for c in range(chunks)
        ]
        for item in x_loads:
            item.start()
        for item in raw_loads:
            item.wait()

        def pair_back(pair):
            for block in range(rows_all // q_block):
                rows = pl.ds(block * q_block, q_block)
                end = (block + 1) * q_block
                q2 = stacked(act, rows, q_at, pair)
                do2 = stacked(dg, rows, o_at, pair)
                keys = act[0:end, head_at(k_at, pair)]
                values = act[0:end, head_at(v_at, pair)]
                scores = dot_nt(keys, q2) * score_scale
                probs = jnp.where(
                    allowed_of(block, 0, end), jnp.exp(scores - lse[pair, block]), 0.0
                )
                d_probs = dot_nt(values, do2)
                delta = jnp.sum(probs * d_probs, axis=0, keepdims=True)
                d_scores = (probs * (d_probs - delta)).astype(LOW)
                d_value = dot_nn(probs.astype(LOW), do2)
                d_key = dot_nn(d_scores, q2)
                if block:
                    dv[0 : end - q_block, :] += d_value[: end - q_block]
                    dk[0 : end - q_block, :] += d_key[: end - q_block]
                dv[end - q_block : end, :] = d_value[end - q_block :]
                dk[end - q_block : end, :] = d_key[end - q_block :]
                d_query = (dot_tn(keys, d_scores) * score_scale).T
                for i in range(group_size):
                    head = pair * group_size + i
                    value, gain_sum = head_back(
                        d_query[i * q_block : (i + 1) * q_block],
                        q_raw[rows, pl.ds(head * head_width, head_width)],
                        cosine[rows, :],
                        sine[rows, :],
                        query_gain_ref[...],
                    )
                    dg[rows, head_at(q_at, head)] = value.astype(LOW)
                    add_to(query_part, gain_sum, head == 0 and block == 0)
            value, gain_sum = head_back(
                dk[...] * score_scale,
                k_raw[:, pl.ds(pair * head_width, head_width)],
                cosine[...],
                sine[...],
                key_gain_ref[...],
            )
            dg[:, head_at(k_at, pair)] = value.astype(LOW)
            add_to(key_part, gain_sum, pair == 0)
            dg[:, head_at(v_at, pair)] = dv[...].astype(LOW)

        def own_stores(which, source, target, swap):
            return [
                pltpu.make_async_copy(
                    source.at[swap.rows(0, c), :],
                    target.at[swap.rows(0, c), :],
                    own_sems.at[which, c],
                )
                for c in range(chunks)
            ]

        own2 = own_stores(0, part, output, swap2)
        own4 = own_stores(1, grad, in_grad, swap4)

        def settle2(c):
            rows = swap2.rows(0, c)
            mixed = swap2.scatter_result(c)
            part[rows, :] = jnp.where(valid(rows), base[swap2.local(c), :] + mixed, 0.0).astype(
                LOW
            )
            own2[c].start()

        soon = chunks // 2
        for c in range(1, soon):
            swap2.scatter_forward(c)
        for pair in range(pairs):
            if pair == pairs - 1:
                for c in range(soon, chunks):
                    swap2.scatter_forward(c)
                for c in range(soon):
                    settle2(c)
                    swap2.gather_start(c)
            pair_back(pair)
        for c in range(chunks):
            rows = chunk_rows(c)

            def normed_step(cols):
                grad[rows, cols] = (
                    dot_nt(dg[rows, q_at], w_query[cols, :])
                    + dot_nt(dg[rows, k_at], w_key[cols, :])
                    + dot_nt(dg[rows, v_at], w_value[cols, :])
                ).astype(LOW)

            unrolled(width, 512, normed_step)
        for c in range(soon, chunks):
            settle2(c)
        swap2.signal(free_sem)
        pl.semaphore_wait(free_sem, swap2.bits)
        for c in range(chunks):
            swap4.scatter_start(c)

        tick(2, 0, lines)
        normed_load.wait()
        from_normed = products(hidden, dg, (0, o_at.start, heads_width))
        from_low = products(low, act, (o_at.start, units, heads_width))

        def last_tile(i):
            yield from from_normed(i)
            yield from from_low(i)

        fill(3, last_tile, lines, stage, middle_step)
        line.ends(2, "start", range(middle_step, line.places - 1))
        for c in range(chunks):
            swap4.scatter_forward(c)
            if c == soon - 1:
                tick(2, 1, lines)
                for early in range(soon):
                    swap2.gather_pass(early, False)
        line.arrived(1)
        for item in x_loads:
            item.wait()
        for c in range(chunks):
            local = swap4.local(c)
            d_normed = swap4.scatter_result(c)
            x = w_out[local, :].astype(F32)
            scale = inverse_norm(x)
            add_to(in_part, jnp.sum(d_normed * (x * scale), axis=0, keepdims=True), c == 0)
            value = resid[local, :] + rows_back(d_normed * in_gain_ref[...], x, scale)
            grad[swap4.rows(0, c), :] = value.astype(LOW)
            if c == chunks - 1:
                spread.copy(0).start()
            swap4.gather_start(c)
            own4[c].start()
        steps = len(spread.steps)
        tick(3, 0, lines)
        for c in range(chunks):
            swap4.gather_pass(c, False)
            if c == soon - 1:
                spread.next(0)
            if c == soon:
                swap2.gather_start(c)
        line.ends(3, "start", range(middle_step, line.places - 2))
        tick(3, 1, lines)
        for step in range(1 if soon else 0, steps):
            spread.next(step)
        spread.far_start()
        line.ends(3, "start", range(max(middle_step, line.places - 2), line.places - 1))
        for c in range(soon + 1, chunks):
            swap2.gather_start(c)
        for c in range(soon, chunks):
            swap2.gather_pass(c, False)
        for step in range(1, line.places - 1):
            spread.pass_on(step, "start")
        for swap in (swap4, swap2):
            for c in range(chunks):
                swap.gather_pass(c, True)
        line.arrived(2)
        line.arrived(3)
        spread.pass_on(line.places - 1, "start")
        gains_out[...] = spread.result()
        for item in own2 + own4:
            item.wait()
        for c in range(chunks):
            swap3.gather_end(c)
            for swap in (swap2, swap4):
                swap.scatter_end(c)
                swap.gather_end(c)
        for group in range(line.groups):
            line.end(group)
        spread.end()

    def both(wd):
        pl.run_scoped(
            functools.partial(front, wd),
            pltpu.VMEM((width, units), LOW),
            pltpu.VMEM((width, units), LOW),
            pltpu.VMEM((chunk, heads_width), F32),
            pltpu.VMEM((chunk, keys_width), F32),
        )
        pl.run_scoped(functools.partial(middle, wd), lines, stage)

    lines = pltpu.VMEM((2, 2, line.tile, line.width), LOW)
    stage = pltpu.VMEM((AWAY, line.tile, line.width), LOW)
    pl.run_scoped(both, pltpu.VMEM((units, width), LOW))
    pl.run_scoped(
        rest,
        lines,
        stage,
        pltpu.VMEM(resid.shape, F32),
        pltpu.VMEM((rows_all, heads_width), F32),
        pltpu.VMEM((rows_all, keys_width), F32),
        pltpu.VMEM((rows_all, head_width), F32),
        pltpu.VMEM((rows_all, head_width), F32),
    )


def layer_call(counts, sizes, length, gains, tokens, out_grad, tables, attn_weights, feed_weights):
    tensor_count, dp_count = counts
    q_block, head_width, pairs, group_size = sizes
    rows, width = tokens.shape
    units = feed_weights[0].shape[1]
    heads_width, keys_width = attn_weights[0].shape[1], attn_weights[1].shape[1]
    tile = width // dp_count
    swaps = [Swap(tensor_count, rows, width) for _ in range(4)]
    line = Line(dp_count, 4, tile, units)
    spread = Spread(counts, 2 * width + 2 * head_width)
    chunks = swaps[0].chunks
    wide = jax.ShapeDtypeStruct((rows, width), LOW)
    out_shape = (
        wide,
        wide,
        jax.ShapeDtypeStruct((1, spread.length), F32),
        *line.outputs(),
        wide,
        jax.ShapeDtypeStruct((rows, 2 * heads_width + 2 * keys_width), LOW),
        jax.ShapeDtypeStruct((rows, heads_width), F32),
        jax.ShapeDtypeStruct((rows, keys_width), F32),
        jax.ShapeDtypeStruct((chunks * swaps[0].block, width), F32),
    )
    big = pltpu.VMEM((rows, width), LOW)
    inner = pltpu.VMEM((rows, units), LOW)
    return pl.pallas_call(
        functools.partial(layer_kernel, (*swaps, line, spread, sizes)),
        out_shape=out_shape,
        in_specs=[pl.BlockSpec(memory_space=pltpu.SMEM)] + [vmem_spec()] * 4 + [any_spec()] * 11,
        out_specs=(any_spec(),) * 2 + (vmem_spec(),) + (any_spec(),) * 8,
        scratch_shapes=[
            big,
            big,
            inner,
            inner,
            inner,
            big,
            big,
            pltpu.VMEM((chunks * swaps[0].block, width), F32),
            pltpu.VMEM((tile, rows), LOW),
            swaps[0].landing(),
            pltpu.VMEM((width, heads_width), LOW),
            pltpu.VMEM((width, keys_width), LOW),
            pltpu.VMEM((width, keys_width), LOW),
            pltpu.VMEM((heads_width, width), LOW),
            pltpu.VMEM((rows, head_width), F32),
            pltpu.VMEM((rows, head_width), F32),
            pltpu.VMEM((pairs, rows // q_block, 1, group_size * q_block), F32),
            pltpu.SemaphoreType.DMA((10,)),
            pltpu.SemaphoreType.DMA((chunks,)),
            pltpu.SemaphoreType.DMA((4 + chunks,)),
            pltpu.SemaphoreType.DMA((2, chunks)),
            pltpu.SemaphoreType.REGULAR,
            *[item for swap in swaps for item in swap.semaphores()],
            *line.semaphores(),
            *spread.scratch(),
        ],
        compiler_params=kernel_params(0),
        name="layer",
    )(length, *gains, tokens, out_grad, *tables, *attn_weights, *feed_weights)[:6]


def results_kernel(sizes, *refs):
    places, pieces, cuts, gain_cuts = sizes
    refs = iter(refs)

    def take(count):
        return [next(refs) for _ in range(count)]

    output, in_grad, gains, acc, land = take(5)
    output_out, in_grad_out = take(2)
    gain_outs = take(len(gain_cuts))
    down_out, gate_out, up_out, query_out, key_out, value_out, proj_out = take(7)
    own, sides, total, turned, held, come_sems, go_sems, load_sems, store_sems = take(9)
    place = lax.axis_index("dp") // 2
    groups, rows = own.shape[0], output.shape[0] // pieces

    come, go = [], []
    for which, (src, dst) in enumerate(((output, output_out), (in_grad, in_grad_out))):
        for i in range(pieces):
            at = pl.ds(i * rows, rows)
            spot = held.at[which, at]
            come.append(pltpu.make_async_copy(src.at[at], spot, come_sems.at[which, i]))
            go.append(pltpu.make_async_copy(spot, dst.at[at], go_sems.at[which, i]))

    def load(group, side):
        if side == 0:
            source, target = acc.at[group, place], own.at[group]
        else:
            slot = place if side == 1 else places
            source, target = land.at[group, slot], sides.at[group, side - 1]
        return pltpu.make_async_copy(source, target, load_sems.at[group, side])

    present = (None, place > 0, place < places - 1)
    for group in range(groups):
        load(group, 0).start()
        for side in (1, 2):
            pl.when(present[side])(lambda group=group, side=side: load(group, side).start())
    for item in come:
        item.start()
    start = 0
    for out, size in zip(gain_outs, gain_cuts):
        out[...] = gains[:, pl.ds(start, size)]
        start += size
    stores = []
    q_at, k_at, v_at, o_at = cuts

    def put(src, dst):
        stores.append(pltpu.make_async_copy(src, dst, store_sems.at[len(stores)]))
        stores[-1].start()

    for group in range(groups):
        load(group, 0).wait()
        total[group] = own[group].astype(F32)
        for side in (1, 2):

            @pl.when(present[side])
            def _(group=group, side=side):
                load(group, side).wait()
                total[group] += sides[group, side - 1].astype(F32)

        for i in range(group * len(come) // groups, (group + 1) * len(come) // groups):
            come[i].wait()
            go[i].start()
        if group == 0:
            turned[...] = total[0].T
            put(turned, down_out)
        elif group == 1:
            put(total.at[1], gate_out)
        elif group == 2:
            put(total.at[2], up_out)
        else:
            put(total.at[3, :, q_at], query_out)
            put(total.at[3, :, k_at], key_out)
            put(total.at[3, :, v_at], value_out)
            proj_out[...] = total[3, :, o_at].T
    for item in stores + go:
        item.wait()


def results(places, head_width, heads_width, keys_width, made):
    output, in_grad, gains, _, acc, land = made
    rows, width = output.shape
    tile, units = acc.shape[2:]
    pieces = 4
    cuts = (
        pl.ds(0, heads_width),
        pl.ds(heads_width, keys_width),
        pl.ds(heads_width + keys_width, keys_width),
        pl.ds(heads_width + 2 * keys_width, heads_width),
    )
    gain_cuts = (width, width, head_width, head_width)
    shapes = [(1, size) for size in gain_cuts]
    shapes += [(units, tile), (tile, units), (tile, units), (tile, heads_width)]
    shapes += [(tile, keys_width), (tile, keys_width), (heads_width, tile)]
    return pl.pallas_call(
        functools.partial(results_kernel, (places, pieces, cuts, gain_cuts)),
        out_shape=(
            jax.ShapeDtypeStruct(output.shape, LOW),
            jax.ShapeDtypeStruct(output.shape, LOW),
            *[jax.ShapeDtypeStruct(shape, F32) for shape in shapes],
        ),
        in_specs=[any_spec()] * 2 + [vmem_spec()] + [any_spec()] * 2,
        out_specs=(any_spec(),) * 2 + (vmem_spec(),) * 4 + (any_spec(),) * 6 + (vmem_spec(),),
        scratch_shapes=[
            pltpu.VMEM((4, tile, units), LOW),
            pltpu.VMEM((4, 2, tile, units), LOW),
            pltpu.VMEM((4, tile, units), F32),
            pltpu.VMEM((units, tile), F32),
            pltpu.VMEM((2, rows, width), LOW),
            pltpu.SemaphoreType.DMA((2, pieces)),
            pltpu.SemaphoreType.DMA((2, pieces)),
            pltpu.SemaphoreType.DMA((4, 3)),
            pltpu.SemaphoreType.DMA((6,)),
        ],
        compiler_params=pltpu.CompilerParams(vmem_limit_bytes=VMEM_BYTES),
        name="results",
    )(output, in_grad, gains, acc, land)


def rope_tables(head_width, row_count):
    half_width = head_width // 2
    inv_freq = ROPE_BASE ** (-2.0 * np.arange(half_width, dtype=np.float32) / head_width)
    angles = np.arange(row_count, dtype=np.float32)[:, None] * inv_freq.astype(np.float32)[None, :]
    cosine, sine = np.cos(angles), np.sin(angles)
    tables = np.concatenate([cosine, cosine], 1), np.concatenate([-sine, sine], 1)
    return tuple(jnp.asarray(table, F32) for table in tables)


def on_device(
    tensor_count,
    dp_count,
    tokens,
    lengths,
    in_gain,
    w_query,
    w_key,
    w_value,
    query_gain,
    key_gain,
    w_out,
    post_gain,
    w_gate,
    w_up,
    w_down,
    out_grad,
):
    head_width = query_gain.shape[0]
    pairs = w_key.shape[1] // head_width
    group_size = w_query.shape[1] // w_key.shape[1]
    q_block = min(128, tokens.shape[0])
    made = layer_call(
        (tensor_count, dp_count),
        (q_block, head_width, pairs, group_size),
        lengths,
        (in_gain[None], post_gain[None], query_gain[None], key_gain[None]),
        tokens,
        out_grad,
        rope_tables(head_width, tokens.shape[0]),
        (w_query, w_key, w_value, w_out),
        (w_gate, w_up, w_down),
    )
    (
        output,
        in_grad,
        grad_post_gain,
        grad_in_gain,
        grad_query_gain,
        grad_key_gain,
        grad_down,
        grad_gate,
        grad_up,
        grad_query,
        grad_key,
        grad_value,
        grad_out,
    ) = results(dp_count // 2, head_width, w_query.shape[1], w_key.shape[1], made)
    return (
        output,
        in_grad,
        grad_in_gain[0],
        grad_query,
        grad_key,
        grad_value,
        grad_query_gain[0],
        grad_key_gain[0],
        grad_out,
        grad_post_gain[0],
        grad_gate,
        grad_up,
        grad_down,
    )


def solution(mesh):
    tensor_count, dp_count = mesh.shape["tensor"], mesh.shape["dp"]

    def layer(*args):
        return on_device(tensor_count, dp_count, *args)

    return jax.shard_map(
        layer,
        mesh=mesh,
        in_specs=(
            P("dp", None),
            P("dp"),
            P(),
            P(None, "tensor"),
            P(None, "tensor"),
            P(None, "tensor"),
            P(),
            P(),
            P("tensor", None),
            P(),
            P(None, "tensor"),
            P(None, "tensor"),
            P("tensor", None),
            P("dp", None),
        ),
        out_specs=(
            P("dp", None),
            P("dp", None),
            P(),
            P("dp", "tensor"),
            P("dp", "tensor"),
            P("dp", "tensor"),
            P(),
            P(),
            P("tensor", "dp"),
            P(),
            P("dp", "tensor"),
            P("dp", "tensor"),
            P("tensor", "dp"),
        ),
        check_vma=False,
    )
```
